32 devices in a mesh: rows: 4 (over x, core), cols: 8 (over z, y).
Axes of the slice: x: 2, y: 2, z: 4, core: 2. Of those that a mesh axis runs over, the one named last changes fastest.
Arguments:
- field: bfloat16 [32, 16, 32768], P('cols', 'rows'), may hold values from -6 to 6
- depth_kernel: float32 [7, 7, 32], replicated, may hold values from -0.875 to 0.875
- point_weight: bfloat16 [32, 32], replicated, may hold values from -1 to 1
- point_bias: float32 [32], replicated, may hold values from -3 to 3
- vert_weight: bfloat16 [2, 288, 32], replicated, may hold values from -0.375 to 0.375
- vert_bias: float32 [2, 32], replicated, may hold values from -3 to 3
- exhaust: bfloat16 [16384, 32], P(('rows', 'cols')), may hold values from -6 to 6
- owner: int32 [16384, 1], P(('rows', 'cols')), may hold values from 0 to 7; in each aligned block of 512 rows (0 to 511, 512 to 1023, ...) at most 128 rows name the same one
- cells: int32 [16384], P(('rows', 'cols')), may hold values from 0 to 16383
Outputs:
- advanced: bfloat16 [32, 16, 32768], P(None, 'rows', 'cols')
The draws below stay inside these ranges and needn't reach their ends.
Inputs may be any that keep to these rules, and one draw needn't show every extreme that they name: `owner`: among the 512 rows of one device, no tile is named by more than 128 rows, a bound that some block reaches.
All inputs are finite; a program needn't handle non-finite values.
Results may differ from the reference program's by a relative error of at most 0.0055.
Values may be sent and summed in bfloat16 or wider, within the bound.
No kernel may reach another device: no remote copies, remote signals or barrier semaphores. Data moves between devices by JAX's collectives and lax.ppermute only.
A program may use at most 128 MiB of HBM per device.

```python
import math
import jax
import jax.numpy as jnp
import numpy as np
from jax import lax

C = 32
X = 1024
Z = 32
YB = 4
E_DEV = 512
KH = 7
KV = 9
LAYERS = 2
Y = 16
XT = 128
CAP = 128
EXH = 16384
N_ROWS = 4
N_COLS = 8


def plant(values, own_key, low, top_value):
    place = [jax.random.randint(jax.random.fold_in(own_key, axis), (), 0, length) for axis, length in enumerate(values.shape)]
    widest = values.shape.index(max(values.shape))
    beside = place[:widest] + [(place[widest] + 1) % values.shape[widest]] + place[widest + 1:]
    return values.at[tuple(place)].set(low).at[tuple(beside)].set(top_value)


def block_scale(rng, dims, shards, low, top_value):
    def one(dim, parts):
        heights = jax.random.uniform(jax.random.fold_in(jax.random.fold_in(rng, 6), dim), (parts,), jnp.float32, low / len(shards), top_value / len(shards))
        return jnp.repeat(jnp.exp(heights), dims[dim] // parts).reshape((-1,) + (1,) * (len(dims) - dim - 1))

    gain = one(*shards[0])
    for cut in shards[1:]:
        gain = gain * one(*cut)
    return gain


def routed_block(rng, own, number, rows, amount, top, most, skew):
    ranking = jax.random.permutation(rng, amount)
    packed, ordinary = portions_of(amount, rows * top, most, skew, True), portions_of(amount, rows * top, most, skew, False)
    places = jnp.arange(amount)

    def named(tallies, rotation):
        used = int((tallies > 0).sum())
        fixed = max(1, used // 4)
        moved = fixed + (places - fixed + rotation * (used - fixed)) % max(1, amount - fixed)
        return jnp.zeros((amount,), jnp.int32).at[ranking[jnp.where(places < fixed, places, moved)]].set(jnp.asarray(tallies, jnp.int32))

    tallies = jnp.where(number % 4 == 0, named(packed, number // 4), named(ordinary, number - number // 4 - 1))
    mixed = jax.random.permutation(jax.random.fold_in(own, 3), amount)
    source_of, taker = mixed[0:amount // 2 * 2:2], mixed[1:amount // 2 * 2:2]
    room = jnp.minimum(tallies[source_of] - 1, most - tallies[taker]) // 2
    room = jnp.where((source_of == ranking[0]) | (taker == ranking[0]) | (tallies[taker] == 0), 0, jnp.maximum(room, 0))
    moved = jax.random.randint(jax.random.fold_in(own, 4), (amount // 2,), 0, 1 << 20) % (room + 1)
    tallies = tallies.at[source_of].add(-moved).at[taker].add(moved)
    items = jnp.searchsorted(jnp.cumsum(tallies), jnp.arange(rows * top), side="right").astype(jnp.int32)
    table = items.reshape(top, rows).T
    table = table[jax.random.permutation(jax.random.fold_in(own, 1), rows)]
    rotation = jax.random.randint(jax.random.fold_in(own, 2), (rows, 1), 0, top)
    return jnp.take_along_axis(table, (jnp.arange(top)[None, :] + rotation) % top, axis=1)


def portions_of(amount, total, limit, lean, full):
    weights = [(1 << 20) // math.isqrt(standing ** lean) + 1 for standing in range(1, amount + 1)]
    largest = limit if full else min(limit, max(-(-total // amount), total * weights[0] // sum(weights)))
    least = 1 if total - largest >= amount - 1 else 0
    counts, rest = [largest] + [least] * (amount - 1), total - largest - least * (amount - 1)
    while rest > 0:
        movable = [i for i in range(1, amount) if counts[i] < largest] or [i for i in range(1, amount) if counts[i] < limit]
        pool, remaining = sum([weights[i] for i in movable]), rest
        for i in movable:
            extra = min(limit - counts[i], max(1, remaining * weights[i] // pool), rest)
            counts[i] = counts[i] + extra
            rest = rest - extra
    return np.array(counts)


def centred(rng, dims, scale, limit, shards=(), kind=jnp.bfloat16):
    factor_of = block_scale(rng, dims, shards, -0.22, 0.18) if shards else 1.0
    array = jax.random.normal(rng, dims, jnp.float32) * scale * factor_of
    return jnp.minimum(jnp.maximum(array, -limit), limit).astype(kind)


def setup_inputs(seed: int = 0) -> dict:
    splits = jax.random.split(jax.random.key(seed), 10)
    field = centred(splits[0], (Z, Y, X * C), 1.0, 6.0, ((0, 8), (1, 4)))
    depth_kernel = centred(splits[1], (KH, KH, C), (KH * KH) ** -0.5, 0.875, (), jnp.float32)
    point_weight = centred(splits[2], (C, C), C ** -0.5, 1.0)
    point_bias = centred(splits[3], (C,), 0.5, 3.0, (), jnp.float32)
    vert_weight = centred(splits[4], (LAYERS, KV * C, C), (KV * C) ** -0.5, 0.375)
    vert_bias = centred(splits[5], (LAYERS, C), 0.5, 3.0, (), jnp.float32)
    exhaust = centred(splits[6], (EXH, C), 1.0, 6.0, ((0, 32),))
    owner_keys = jax.random.split(jax.random.fold_in(splits[7], 1), EXH // E_DEV)
    owner_turns = jax.random.permutation(jax.random.fold_in(splits[7], 3), EXH // E_DEV)
    owner = jax.vmap(lambda own, number: routed_block(jax.random.fold_in(splits[7], 2), own, number, E_DEV, N_COLS, 1, CAP, 2))(owner_keys, owner_turns).reshape((EXH, 1))
    cells = plant(jax.random.randint(splits[8], (EXH,), 0, Z * YB * (X // N_COLS)), jax.random.fold_in(splits[8], 1), 0, (Z * YB * (X // N_COLS)) - 1).astype(jnp.int32)
    return {"field": field, "depth_kernel": depth_kernel, "point_weight": point_weight, "point_bias": point_bias, "vert_weight": vert_weight, "vert_bias": vert_bias, "exhaust": exhaust, "owner": owner, "cells": cells}


def horizontal(band, depth_kernel, point_weight, point_bias):
    height = band.shape[1] - 6
    width = band.shape[2] - 6
    total = jnp.zeros((band.shape[0], height, width, C), jnp.float32)
    for i in range(KH):
        for j in range(KH):
            total = total + band[:, i:i + height, j:j + width, :].astype(jnp.float32) * depth_kernel[i, j]
    depth_b = total.astype(jnp.bfloat16)
    proj = jnp.einsum("zyxc,cd->zyxd", depth_b.astype(jnp.float32), point_weight.astype(jnp.float32))
    center = band[:, 3:3 + height, 3:3 + width, :].astype(jnp.float32)
    return (center + jax.nn.gelu(proj + point_bias)).astype(jnp.bfloat16)


def vertical(level_field, vert_weight, vert_bias):
    current = level_field
    result = None
    for layer in range(LAYERS):
        padded = jnp.pad(current, ((4, 4), (0, 0), (0, 0), (0, 0)))
        conv = jnp.zeros(current.shape, jnp.float32) + vert_bias[layer]
        for k in range(KV):
            conv = conv + jnp.einsum("zyxc,cd->zyxd", padded[k:k + Z].astype(jnp.float32),
                                     vert_weight[layer, k * C:(k + 1) * C].astype(jnp.float32))
        result = current.astype(jnp.float32) + jax.nn.gelu(conv)
        if layer < LAYERS - 1:
            current = result.astype(jnp.bfloat16)
    return result


def reference(field, depth_kernel, point_weight, point_bias, vert_weight, vert_bias, exhaust, owner, cells):
    padded = jnp.pad(field, ((0, 0), (3, 3), (0, 0)))
    band_rows = N_COLS * E_DEV

    def one_band(band_index):
        start = (band_index * YB).astype(jnp.int32)
        band = lax.dynamic_slice_in_dim(padded, start, YB + 6, 1).reshape(Z, YB + 6, X, C)
        band = jnp.pad(band, ((0, 0), (0, 0), (3, 3), (0, 0)))
        mixed = horizontal(band, depth_kernel, point_weight, point_bias)
        pre = vertical(mixed, vert_weight, vert_bias)
        first = (band_index * band_rows).astype(jnp.int32)
        emis = lax.dynamic_slice_in_dim(exhaust, first, band_rows, 0).astype(jnp.float32)
        where_to = lax.dynamic_slice_in_dim(owner, first, band_rows, 0)[:, 0]
        which = lax.dynamic_slice_in_dim(cells, first, band_rows, 0)
        level = which // (YB * XT)
        yrow = (which // XT) % YB
        xcol = where_to * XT + which % XT
        source = jnp.zeros((Z, YB, X, C), jnp.float32).at[level, yrow, xcol].add(emis)
        return (pre + source).astype(jnp.bfloat16).reshape(Z, YB, X * C)

    bands = lax.map(one_band, jnp.arange(N_ROWS, dtype=jnp.int32))
    return jnp.transpose(bands, (1, 0, 2, 3)).reshape(Z, Y, X * C)
```

```python
import functools

import jax
import jax.numpy as jnp
from jax import lax
from jax.experimental import pallas as pl
from jax.experimental.pallas import tpu as pltpu
from jax.sharding import PartitionSpec as P

C = 32
KH = 7
KV = 9
SEG = 8
SL = SEG * C
HALF = SL // 2
PACK = 48
VMEM = 56 * 1024 * 1024
NT = (((1,), (1,)), ((), ()))
F32 = jnp.float32
BF16 = jnp.bfloat16


def params():
    return pltpu.CompilerParams(vmem_limit_bytes=VMEM)


def cost(flops, moved):
    return pl.CostEstimate(flops=flops, bytes_accessed=moved, transcendentals=0)


def whole(shape):
    return pl.BlockSpec(shape, lambda *_: (0,) * len(shape))


def gelu(x):
    return 0.5 * x * (1.0 + jnp.tanh(0.7978845608028654 * (x + 0.044715 * (x * x * x))))


def swap_matrix(outer, inner):
    size = outer * inner
    row = lax.broadcasted_iota(jnp.int32, (size, size), 0)
    column = lax.broadcasted_iota(jnp.int32, (size, size), 1)
    return (column == (row % outer) * inner + row // outer).astype(BF16)


def segment_kernel(field_ref, own_ref, first_ref, last_ref):
    levels, height, lanes = field_ref.shape
    rows = levels * height
    group = 256 // rows
    swap = swap_matrix(group, rows)
    stacked = []
    for s in range(group):
        piece = field_ref[:, :, s * SL : (s + 1) * SL]
        stacked.append(piece.reshape(rows, SL))
    mixed_up = jnp.concatenate(stacked, axis=0)
    got = jnp.dot(swap, mixed_up, preferred_element_type=F32).astype(BF16)
    for z in range(levels):
        for y in range(height):
            start = (z * height + y) * group
            piece = got[start : start + group]
            own_ref[y, z] = piece
            if y < 3:
                first_ref[y, z] = piece
            if y >= height - 3:
                last_ref[y - (height - 3), z] = piece


def to_segments(field):
    levels, height, lanes = field.shape
    segments = lanes // SL
    rows = levels * height
    if rows % 16 or 256 % rows:
        own = jnp.transpose(field.reshape(levels, height, segments, SL), (1, 0, 2, 3))
        return own, own[:3], own[height - 3 :]
    group = 256 // rows
    out = lambda n: (
        jax.ShapeDtypeStruct((n, levels, segments, SL), BF16),
        pl.BlockSpec((n, levels, group, SL), lambda g: (0, 0, g, 0)),
    )
    shapes, specs = zip(out(height), out(3), out(3))
    return pl.pallas_call(
        segment_kernel,
        grid=(segments // group,),
        in_specs=[pl.BlockSpec((levels, height, group * SL), lambda g: (0, 0, g))],
        out_specs=list(specs),
        out_shape=list(shapes),
        compiler_params=params(),
        cost_estimate=cost(2 * rows * lanes * 256, 8 * rows * lanes),
    )(field)


def weights_kernel(rows_ref, point_ref, vert_ref, across_ref, up_ref):
    blocks = []
    for i in range(KH):
        parts = []
        for xo in range(4):
            parts.append(point_ref[...] * rows_ref[pl.ds(i * 4 + xo, 1), :])
        blocks.append(jnp.concatenate(parts, axis=0).T.astype(BF16))
    zero = jnp.zeros((3 * HALF, HALF), BF16)
    for yi in range(KH + 1):
        for yo in range(2):
            i = yi - yo
            across_ref[yi * 3 * HALF : (yi + 1) * 3 * HALF, yo * HALF : (yo + 1) * HALF] = (
                blocks[i] if 0 <= i < KH else zero
            )
    row = lax.broadcasted_iota(jnp.int32, (KV * HALF, KV * C), 0)
    column = lax.broadcasted_iota(jnp.int32, (KV * HALF, KV * C), 1)
    spread = ((row // HALF == column // C) & (row % C == column % C)).astype(BF16)
    row = lax.broadcasted_iota(jnp.int32, (C, HALF), 0)
    column = lax.broadcasted_iota(jnp.int32, (C, HALF), 1)
    repeat = (row == column % C).astype(BF16)
    row = lax.broadcasted_iota(jnp.int32, (KV * HALF, HALF), 0)
    column = lax.broadcasted_iota(jnp.int32, (KV * HALF, HALF), 1)
    same = (row % HALF) // C == column // C
    zero = jnp.zeros((HALF, HALF), BF16)
    for layer in range(vert_ref.shape[0]):
        tall = lax.dot_general(spread, vert_ref[layer], NT, preferred_element_type=F32).astype(BF16)
        wide = jnp.dot(tall, repeat, preferred_element_type=F32)
        wide = jnp.where(same, wide, 0.0).astype(BF16)
        for zi in range(KV + 1):
            for zo in range(2):
                k = zi - zo
                up_ref[layer, zi * HALF : (zi + 1) * HALF, zo * HALF : (zo + 1) * HALF] = (
                    wide[k * HALF : (k + 1) * HALF] if 0 <= k < KV else zero
                )


def make_weights(depth_kernel, point_weight, vert_weight):
    flat = depth_kernel.reshape(KH, KH * C)
    wide = 3 * HALF
    rows = jnp.stack(
        [
            jnp.pad(flat, ((0, 0), ((xo + 1) * C, wide - KH * C - (xo + 1) * C)))
            for xo in range(4)
        ],
        axis=1,
    ).reshape(KH * 4, wide)
    point = jnp.tile(point_weight.T.astype(F32), (1, wide // C))
    vert = jnp.transpose(vert_weight, (0, 2, 1))
    layers = vert.shape[0]
    return pl.pallas_call(
        weights_kernel,
        out_shape=[
            jax.ShapeDtypeStruct(((KH + 1) * wide, SL), BF16),
            jax.ShapeDtypeStruct((layers, (KV + 1) * HALF, SL), BF16),
        ],
        compiler_params=params(),
        cost_estimate=cost(10**9, 6 * 10**6),
    )(rows, point, vert)


def horizontal_kernel(own_ref, low_ref, high_ref, weight_ref, bias_ref, out_ref):
    height = own_ref.shape[0]
    segments = own_ref.shape[2]
    row = lax.broadcasted_iota(jnp.int32, (segments, HALF), 0)
    lines = [low_ref[y, 0] for y in range(3)]
    lines += [own_ref[y, 0] for y in range(height)]
    lines += [high_ref[y, 0] for y in range(3)]
    left, right = [], []
    for line in lines:
        a0, a1 = line[:, :HALF], line[:, HALF:]
        before = jnp.where(row == 0, 0.0, pltpu.roll(a1.astype(F32), 1, 0)).astype(BF16)
        after = jnp.where(
            row == segments - 1, 0.0, pltpu.roll(a0.astype(F32), segments - 1, 0)
        ).astype(BF16)
        left.append([before, a0, a1])
        right.append([a0, a1, after])
    stacked = []
    for yp in range(height // 2):
        for side in (left, right):
            stacked.append(
                jnp.concatenate(
                    [tile for y in range(2 * yp, 2 * yp + KH + 1) for tile in side[y]], axis=1
                )
            )
    total = jnp.dot(
        jnp.concatenate(stacked, axis=0), weight_ref[...], preferred_element_type=F32
    )
    tiles, _, _, per, _ = out_ref.shape
    for yp in range(height // 2):
        for h in range(2):
            start = (yp * 2 + h) * segments
            for yo in range(2):
                y = 2 * yp + yo
                part = total[start : start + segments, yo * HALF : (yo + 1) * HALF]
                center = lines[y + 3][:, h * HALF : (h + 1) * HALF].astype(F32)
                value = (center + gelu(part + bias_ref[...])).astype(BF16)
                out_ref[:, 0, y, :, h * HALF : (h + 1) * HALF] = value.reshape(tiles, per, HALF)


def horizontal(own, low, high, weight, bias, tiles):
    height, levels, segments, _ = own.shape
    direct = (segments // tiles) % 16 == 0
    parts = tiles if direct else 1
    per = segments // parts
    line = lambda n: pl.BlockSpec((n, 1, segments, SL), lambda z: (0, z, 0, 0))
    out = pl.pallas_call(
        horizontal_kernel,
        grid=(levels,),
        in_specs=[line(height), line(3), line(3), whole(weight.shape), whole(bias.shape)],
        out_specs=pl.BlockSpec((parts, 1, height, per, SL), lambda z: (0, z, 0, 0, 0)),
        out_shape=jax.ShapeDtypeStruct((parts, levels, height, per, SL), BF16),
        compiler_params=params(),
        cost_estimate=cost(
            2 * levels * height * segments * weight.shape[0] * SL // 2, 4 * 10**6
        ),
    )(own, low, high, weight, bias)
    if not direct:
        out = out.reshape(levels, height, tiles, segments // tiles, SL)
        out = jnp.transpose(out, (2, 0, 1, 3, 4))
    return out


def bucket_kernel(rows_ref, owner_ref, cells_ref, out_ref):
    count = rows_ref.shape[1]
    tiles = out_ref.shape[0]
    cap = 2 * count // tiles
    owner, cells = owner_ref[...], cells_ref[...]
    row = lax.broadcasted_iota(jnp.int32, (count, count), 0)
    column = lax.broadcasted_iota(jnp.int32, (count, count), 1)
    before = (row < column).astype(BF16)
    named = (lax.broadcasted_iota(jnp.int32, (tiles, count), 0) == owner).astype(F32)
    rank = jnp.dot(named.astype(BF16), before, preferred_element_type=F32)
    rank = jnp.sum(rank * named, axis=0, keepdims=True).astype(jnp.int32)
    slot = owner * cap + rank
    chosen = lax.broadcasted_iota(jnp.int32, (tiles * cap, count), 0) == slot
    coarse = (cells // HALF).astype(F32)
    fine = (cells % HALF).astype(F32)
    index = lax.broadcasted_iota(jnp.int32, (PACK - C, count), 0)
    places = jnp.where(index == 0, coarse, jnp.where(index == 1, fine, 0.0)).astype(BF16)
    payload = jnp.concatenate([rows_ref[...], places], axis=0)
    out = lax.dot_general(
        payload, chosen.astype(BF16), NT, preferred_element_type=F32
    ).astype(BF16)
    if cap % HALF == 0:
        for t in range(tiles):
            out_ref[t] = out[:, t * cap : (t + 1) * cap]
    else:
        out_ref[...] = jnp.swapaxes(out.reshape(PACK, tiles, cap), 0, 1)


def bucket(exhaust, owner, cells, tiles):
    count = exhaust.shape[0]
    cap = 2 * count // tiles
    return pl.pallas_call(
        bucket_kernel,
        out_shape=jax.ShapeDtypeStruct((tiles, PACK, cap), BF16),
        compiler_params=params(),
        cost_estimate=cost(10**8, 10**6),
    )(exhaust.T, owner.reshape(1, count), cells.reshape(1, count))


def source_kernel(got_ref, out_ref):
    step = out_ref.shape[0]
    slots = got_ref.shape[1]
    got = got_ref[...]
    cells = (got[C : C + 1].astype(F32) * HALF + got[C + 1 : C + 2].astype(F32)).astype(jnp.int32)
    place, within = cells // SEG, cells % SEG
    rows = got[:C]
    lane = lax.broadcasted_iota(jnp.int32, (SL, slots), 0) // C
    spread = jnp.where(lane == within, jnp.concatenate([rows] * SEG, axis=0).astype(F32), 0.0)
    row = lax.broadcasted_iota(jnp.int32, (step, slots), 0) + pl.program_id(0) * step
    chosen = (row == place).astype(BF16)
    out_ref[...] = lax.dot_general(chosen, spread.astype(BF16), NT, preferred_element_type=F32)


def make_source(got, places):
    slots = got.shape[1]
    step = min(512, places)
    return pl.pallas_call(
        source_kernel,
        grid=(places // step,),
        in_specs=[whole(got.shape)],
        out_specs=pl.BlockSpec((step, SL), lambda g: (g, 0)),
        out_shape=jax.ShapeDtypeStruct((places, SL), F32),
        compiler_params=params(),
        cost_estimate=cost(2 * places * slots * SL, 3 * 10**6),
    )(got)


def vertical_kernel(height, field_ref, source_ref, weight_ref, bias_ref, out_ref, held):
    levels, rows, _ = field_ref.shape
    layers = weight_ref.shape[0]
    step = pl.program_id(0)
    zero = jnp.zeros((rows, HALF), BF16)
    tiles = [[field_ref[z, :, h * HALF : (h + 1) * HALF] for h in range(2)] for z in range(levels)]
    for layer in range(layers):
        taps = []
        for k in range(KV + 1):
            column = []
            for zp in range(levels // 2):
                z = 2 * zp + k - KV // 2
                for h in range(2):
                    column.append(tiles[z][h] if 0 <= z < levels else zero)
            taps.append(jnp.concatenate(column, axis=0))
        total = jnp.dot(
            jnp.concatenate(taps, axis=1), weight_ref[layer], preferred_element_type=F32
        )
        following = []
        for z in range(levels):
            following.append([])
            for h in range(2):
                start = ((z // 2) * 2 + h) * rows
                lane = (z % 2) * HALF
                part = total[start : start + rows, lane : lane + HALF]
                value = tiles[z][h].astype(F32) + gelu(part + bias_ref[pl.ds(layer, 1), :])
                if layer == layers - 1:
                    value = value + source_ref[z, :, h * HALF : (h + 1) * HALF]
                following[z].append(value.astype(BF16))
        tiles = following
    for z in range(levels):
        for h in range(2):
            held[step, z, :, h * HALF : (h + 1) * HALF] = tiles[z][h]

    @pl.when(step == pl.num_programs(0) - 1)
    def _():
        steps = held.shape[0]
        across = steps * rows // height
        group = 256 // (steps * rows)
        swap = swap_matrix(group * height, across)
        for g in range(levels // group):
            pieces = [held[n, g * group + z] for z in range(group) for n in range(steps)]
            turned = jnp.dot(
                swap, jnp.concatenate(pieces, axis=0), preferred_element_type=F32
            ).astype(BF16)
            size = group * height
            for s in range(across):
                out_ref[g * group : (g + 1) * group, :, s * SL : (s + 1) * SL] = turned[
                    s * size : (s + 1) * size
                ].reshape(group, height, SL)


def vertical(field, source, weight, bias, height):
    levels, rows, _ = field.shape
    size = 16
    steps = rows // size
    lanes = rows // height * SL
    return pl.pallas_call(
        functools.partial(vertical_kernel, height),
        grid=(steps,),
        in_specs=[
            pl.BlockSpec((levels, size, SL), lambda g: (0, g, 0)),
            pl.BlockSpec((levels, size, SL), lambda g: (0, g, 0)),
            whole(weight.shape),
            whole(bias.shape),
        ],
        out_specs=whole((levels, height, lanes)),
        out_shape=jax.ShapeDtypeStruct((levels, height, lanes), BF16),
        scratch_shapes=[pltpu.VMEM((steps, levels, size, SL), BF16)],
        compiler_params=params(),
        cost_estimate=cost(4 * levels * rows * weight.shape[1] * SL, 6 * 10**6),
    )(field, source, weight, bias)


def body(
    field, depth_kernel, point_weight, point_bias, vert_weight, vert_bias, exhaust, owner, cells
):
    columns, bands = lax.axis_size("cols"), lax.axis_size("rows")
    forward = [(i, i + 1) for i in range(bands - 1)]
    backward = [(target, source) for source, target in forward]
    height = field.shape[1]
    own, first, last = to_segments(field)
    low = lax.ppermute(last, "rows", forward)
    high = lax.ppermute(first, "rows", backward)
    sent = bucket(exhaust, owner, cells, columns)
    got = lax.all_to_all(sent, "cols", split_axis=0, concat_axis=0, tiled=True)
    got = jnp.transpose(got, (1, 0, 2)).reshape(PACK, -1)
    across, up = make_weights(depth_kernel, point_weight, vert_weight)
    mixed = horizontal(
        own, low, high, across, jnp.tile(point_bias, 4).reshape(1, HALF), columns
    )
    tiles, levels, _, per, _ = mixed.shape
    mixed = mixed.reshape(tiles, levels, height * per, SL)
    taken = lax.all_to_all(mixed, "cols", split_axis=0, concat_axis=0, tiled=True)
    taken = taken.reshape(tiles * levels, height * per, SL)
    source = make_source(got, taken.shape[0] * taken.shape[1]).reshape(taken.shape)
    return vertical(taken, source, up, jnp.tile(vert_bias, (1, 4)), height)


def solution(mesh):
    placed = (
        P("cols", "rows", None),
        P(),
        P(),
        P(),
        P(),
        P(),
        P(("rows", "cols"), None),
        P(("rows", "cols"), None),
        P(("rows", "cols")),
    )
    return jax.shard_map(
        body, mesh=mesh, in_specs=placed, out_specs=P(None, "rows", "cols"), check_vma=False
    )
```

```python
import functools

import jax
import jax.numpy as jnp
from jax import lax
from jax.experimental import pallas as pl
from jax.experimental.pallas import tpu as pltpu
from jax.sharding import PartitionSpec as P

C = 32
KH = 7
KV = 9
SEG = 8
SL = SEG * C
HALF = SL // 2
PACK = 48
VMEM = 24 * 1024 * 1024
NT = (((1,), (1,)), ((), ()))
F32 = jnp.float32
BF16 = jnp.bfloat16


def params():
    return pltpu.CompilerParams(vmem_limit_bytes=VMEM)


def cost(flops, moved):
    return pl.CostEstimate(flops=flops, bytes_accessed=moved, transcendentals=0)


def whole(shape):
    return pl.BlockSpec(shape, lambda *_: (0,) * len(shape))


def gelu(x):
    return 0.5 * x * (1.0 + jnp.tanh(0.7978845608028654 * (x + 0.044715 * (x * x * x))))


def swap_matrix(outer, inner):
    size = outer * inner
    row = lax.broadcasted_iota(jnp.int32, (size, size), 0)
    column = lax.broadcasted_iota(jnp.int32, (size, size), 1)
    return (column == (row % outer) * inner + row // outer).astype(BF16)


def segment_kernel(field_ref, own_ref, first_ref, last_ref):
    levels, height, lanes = field_ref.shape
    rows = levels * height
    group = 256 // rows
    swap = swap_matrix(group, rows)
    for g in range(lanes // (group * SL)):
        at = [(g * group + s) * SL for s in range(group)]
        pieces = [field_ref[:, :, n : n + SL].reshape(rows, SL) for n in at]
        got = jnp.dot(
            swap, jnp.concatenate(pieces, axis=0), preferred_element_type=F32
        ).astype(BF16)
        for z in range(levels):
            for y in range(height):
                start = (z * height + y) * group
                piece = got[start : start + group]
                place = slice(g * group, (g + 1) * group)
                own_ref[y, z, place] = piece
                if y < 3:
                    first_ref[y, z, place] = piece
                if y >= height - 3:
                    last_ref[y - (height - 3), z, place] = piece


def to_segments(field):
    levels, height, lanes = field.shape
    segments = lanes // SL
    rows = levels * height
    if rows % 16 or 256 % rows:
        own = jnp.transpose(field.reshape(levels, height, segments, SL), (1, 0, 2, 3))
        return own, own[:3], own[height - 3 :]
    steps = 2
    part = segments // steps
    out = lambda n: (
        jax.ShapeDtypeStruct((n, levels, segments, SL), BF16),
        pl.BlockSpec((n, levels, part, SL), lambda g: (0, 0, g, 0)),
    )
    shapes, specs = zip(out(height), out(3), out(3))
    return pl.pallas_call(
        segment_kernel,
        grid=(steps,),
        in_specs=[pl.BlockSpec((levels, height, part * SL), lambda g: (0, 0, g))],
        out_specs=list(specs),
        out_shape=list(shapes),
        compiler_params=params(),
        cost_estimate=cost(2 * rows * lanes * 256, 8 * rows * lanes),
    )(field)


def across_kernel(depth_ref, point_ref, out_ref):
    point = jnp.concatenate([point_ref[...].astype(F32)] * (HALF // C), axis=1)
    lane = lax.broadcasted_iota(jnp.int32, (C, HALF), 1) // C
    wide = 3 * HALF
    out_ref[...] = jnp.zeros_like(out_ref)
    for i in range(KH):
        columns = jnp.transpose(depth_ref[i])
        scaled = [point * columns[:, j : j + 1] for j in range(KH)]
        for xt in range(wide // C):
            block = jnp.zeros((C, HALF), F32)
            for xo in range(HALF // C):
                j = xt - 1 - xo
                if 0 <= j < KH:
                    block = jnp.where(lane == xo, scaled[j], block)
            block = block.astype(BF16)
            for yo in range(2):
                row = (i + yo) * wide + xt * C
                out_ref[row : row + C, yo * HALF : (yo + 1) * HALF] = block


def across_weights(depth_kernel, point_weight):
    return pl.pallas_call(
        across_kernel,
        out_shape=jax.ShapeDtypeStruct(((KH + 1) * 3 * HALF, SL), BF16),
        compiler_params=params(),
        cost_estimate=cost(1000, 1000),
    )(depth_kernel, point_weight)


def up_kernel(vert_ref, out_ref):
    row = lax.broadcasted_iota(jnp.int32, (KV * HALF, KV * C), 0)
    column = lax.broadcasted_iota(jnp.int32, (KV * HALF, KV * C), 1)
    spread = ((row // HALF == column // C) & (row % C == column % C)).astype(BF16)
    row = lax.broadcasted_iota(jnp.int32, (C, HALF), 0)
    column = lax.broadcasted_iota(jnp.int32, (C, HALF), 1)
    repeat = (row == column % C).astype(BF16)
    row = lax.broadcasted_iota(jnp.int32, (KV * HALF, HALF), 0)
    column = lax.broadcasted_iota(jnp.int32, (KV * HALF, HALF), 1)
    same = (row % HALF) // C == column // C
    zero = jnp.zeros((HALF, HALF), BF16)
    for layer in range(vert_ref.shape[0]):
        tall = lax.dot_general(spread, vert_ref[layer], NT, preferred_element_type=F32).astype(BF16)
        wide = jnp.dot(tall, repeat, preferred_element_type=F32)
        wide = jnp.where(same, wide, 0.0).astype(BF16)
        for zi in range(KV + 1):
            for zo in range(2):
                k = zi - zo
                out_ref[layer, zi * HALF : (zi + 1) * HALF, zo * HALF : (zo + 1) * HALF] = (
                    wide[k * HALF : (k + 1) * HALF] if 0 <= k < KV else zero
                )


def up_weights(vert_weight):
    vert = jnp.transpose(vert_weight, (0, 2, 1))
    return pl.pallas_call(
        up_kernel,
        out_shape=jax.ShapeDtypeStruct((vert.shape[0], (KV + 1) * HALF, SL), BF16),
        compiler_params=params(),
        cost_estimate=cost(1000, 1000),
    )(vert)


def bias_row(row):
    return jnp.concatenate([row] * (HALF // C), axis=1)


def horizontal_kernel(own_ref, low_ref, high_ref, weight_ref, bias_ref, out_ref):
    height = own_ref.shape[0]
    segments = own_ref.shape[2]
    row = lax.broadcasted_iota(jnp.int32, (segments, HALF), 0)
    lines = [low_ref[y, 0] for y in range(3)]
    lines += [own_ref[y, 0] for y in range(height)]
    lines += [high_ref[y, 0] for y in range(3)]
    left, right = [], []
    for line in lines:
        a0, a1 = line[:, :HALF], line[:, HALF:]
        before = jnp.where(row == 0, 0.0, pltpu.roll(a1.astype(F32), 1, 0)).astype(BF16)
        after = jnp.where(
            row == segments - 1, 0.0, pltpu.roll(a0.astype(F32), segments - 1, 0)
        ).astype(BF16)
        left.append([before, a0, a1])
        right.append([a0, a1, after])
    stacked = []
    for yp in range(height // 2):
        for side in (left, right):
            stacked.append(
                jnp.concatenate(
                    [tile for y in range(2 * yp, 2 * yp + KH + 1) for tile in side[y]], axis=1
                )
            )
    total = jnp.dot(
        jnp.concatenate(stacked, axis=0), weight_ref[...], preferred_element_type=F32
    )
    bias = bias_row(bias_ref[...])
    tiles, _, _, per, _ = out_ref.shape
    for yp in range(height // 2):
        for h in range(2):
            start = (yp * 2 + h) * segments
            for yo in range(2):
                y = 2 * yp + yo
                part = total[start : start + segments, yo * HALF : (yo + 1) * HALF]
                center = lines[y + 3][:, h * HALF : (h + 1) * HALF].astype(F32)
                value = (center + gelu(part + bias)).astype(BF16)
                out_ref[:, 0, y, :, h * HALF : (h + 1) * HALF] = value.reshape(tiles, per, HALF)


def horizontal(own, low, high, weight, bias, tiles):
    height, levels, segments, _ = own.shape
    direct = (segments // tiles) % 16 == 0
    parts = tiles if direct else 1
    per = segments // parts
    line = lambda n: pl.BlockSpec((n, 1, segments, SL), lambda z: (0, z, 0, 0))
    out = pl.pallas_call(
        horizontal_kernel,
        grid=(levels,),
        in_specs=[line(height), line(3), line(3), whole(weight.shape), whole(bias.shape)],
        out_specs=pl.BlockSpec((parts, 1, height, per, SL), lambda z: (0, z, 0, 0, 0)),
        out_shape=jax.ShapeDtypeStruct((parts, levels, height, per, SL), BF16),
        compiler_params=params(),
        cost_estimate=cost(
            2 * levels * height * segments * weight.shape[0] * SL // 2, 4 * 10**6
        ),
    )(own, low, high, weight, bias)
    if not direct:
        out = out.reshape(levels, height, tiles, segments // tiles, SL)
        out = jnp.transpose(out, (2, 0, 1, 3, 4))
    return out


def half_kernel(tiles, place_ref, own_ref, low_ref, high_ref, weight_ref, bias_ref, *rest):
    extra_refs, out_refs, done = rest[: -tiles - 1], rest[-tiles - 1 : -1], rest[-1]
    height, levels, segments, _ = own_ref.shape
    size = segments // 2
    start = pl.multiple_of(place_ref[0], size)
    per = size // tiles
    ahead = pl.multiple_of(jnp.maximum(start - 16, 0), 16)
    behind = pl.multiple_of(jnp.minimum(start + size, segments - 16), 16)
    has_ahead = jnp.where(start > 0, 1.0, 0.0)
    has_behind = jnp.where(start + size < segments, 1.0, 0.0)
    bias = bias_row(bias_ref[...])
    refs = [(low_ref, y) for y in range(3)]
    refs += [(own_ref, y) for y in range(height)]
    refs += [(high_ref, y) for y in range(3)]
    stacked, centers = [], []
    for z in range(levels):
        left, right = [], []
        centers.append([])
        for ref, y in refs:
            line = ref[y, z, pl.ds(start, size)]
            a0, a1 = line[:, :HALF], line[:, HALF:]
            edge = ref[y, z, pl.ds(ahead, 16), HALF:].astype(F32) * has_ahead
            before = jnp.concatenate([edge, a1.astype(F32)], axis=0)
            before = pltpu.roll(before, 1, 0)[16:].astype(BF16)
            edge = ref[y, z, pl.ds(behind, 16), :HALF].astype(F32) * has_behind
            after = jnp.concatenate([a0.astype(F32), edge], axis=0)
            after = pltpu.roll(after, size + 15, 0)[:size].astype(BF16)
            left.append([before, a0, a1])
            right.append([a0, a1, after])
            centers[z].append(line)
        for yp in range(height // 2):
            for side in (left, right):
                stacked.append(
                    jnp.concatenate(
                        [tile for y in range(2 * yp, 2 * yp + KH + 1) for tile in side[y]], axis=1
                    )
                )
    total = jnp.dot(jnp.concatenate(stacked, axis=0), weight_ref[...], preferred_element_type=F32)
    for z in range(levels):
        for y in range(height):
            for h in range(2):
                row = ((z * (height // 2) + y // 2) * 2 + h) * size
                lane = (y % 2) * HALF
                part = total[row : row + size, lane : lane + HALF]
                center = centers[z][y + 3][:, h * HALF : (h + 1) * HALF].astype(F32)
                value = (center + gelu(part + bias)).astype(BF16)
                at = (z * height + y) * per
                done[:, at : at + per, h * HALF : (h + 1) * HALF] = value.reshape(tiles, per, HALF)
    rows = levels * height * per
    for slot, out_ref in enumerate(out_refs):
        tile = place_ref[1] ^ slot
        out_ref[:rows] = done[tile]
        for n, extra_ref in enumerate(extra_refs):
            out_ref[rows:, n * HALF : (n + 1) * HALF] = extra_ref[tile]


def half_horizontal(place, own, low, high, weight, bias, tiles, extra=()):
    height, levels, segments, _ = own.shape
    per = segments // (2 * tiles)
    rows = levels * height * per
    full = pl.BlockSpec(memory_space=pltpu.VMEM)
    shape = (rows + (PACK if extra else 0), SL)
    return pl.pallas_call(
        functools.partial(half_kernel, tiles),
        in_specs=[pl.BlockSpec(memory_space=pltpu.SMEM)] + [full] * (5 + len(extra)),
        out_specs=[full] * tiles,
        out_shape=[jax.ShapeDtypeStruct(shape, BF16)] * tiles,
        scratch_shapes=[pltpu.VMEM((tiles, rows, SL), BF16)],
        compiler_params=params(),
        cost_estimate=cost(1000, 1000),
    )(place, own, low, high, weight, bias, *extra)


def bucket_kernel(near_ref, rows_ref, owner_ref, cells_ref, *rest):
    out_refs, held = rest[:-1], rest[-1]
    count = rows_ref.shape[1]
    tiles, _, cap = held.shape
    owner, cells = owner_ref[...], cells_ref[...]
    row = lax.broadcasted_iota(jnp.int32, (count, count), 0)
    column = lax.broadcasted_iota(jnp.int32, (count, count), 1)
    before = (row < column).astype(BF16)
    named = (lax.broadcasted_iota(jnp.int32, (tiles, count), 0) == owner).astype(F32)
    rank = jnp.dot(named.astype(BF16), before, preferred_element_type=F32)
    rank = jnp.sum(rank * named, axis=0, keepdims=True).astype(jnp.int32)
    slot = owner * cap + rank
    chosen = lax.broadcasted_iota(jnp.int32, (tiles * cap, count), 0) == slot
    coarse = (cells // HALF).astype(F32)
    fine = (cells % HALF).astype(F32)
    index = lax.broadcasted_iota(jnp.int32, (PACK - C, count), 0)
    places = jnp.where(index == 0, coarse, jnp.where(index == 1, fine, 0.0)).astype(BF16)
    payload = jnp.concatenate([rows_ref[...], places], axis=0)
    out = lax.dot_general(
        payload, chosen.astype(BF16), NT, preferred_element_type=F32
    ).astype(BF16)
    if cap % HALF == 0:
        for t in range(tiles):
            held[t] = out[:, t * cap : (t + 1) * cap]
    else:
        held[...] = jnp.swapaxes(out.reshape(PACK, tiles, cap), 0, 1)
    size = tiles // len(out_refs)
    for n, out_ref in enumerate(out_refs):
        out_ref[...] = held[pl.ds((near_ref[0] ^ n) * size, size)]


def bucket(near, exhaust, owner, cells, tiles, parts):
    count = exhaust.shape[0]
    cap = 2 * count // tiles
    full = pl.BlockSpec(memory_space=pltpu.VMEM)
    return pl.pallas_call(
        bucket_kernel,
        in_specs=[pl.BlockSpec(memory_space=pltpu.SMEM)] + [full] * 3,
        out_specs=[full] * parts,
        out_shape=[jax.ShapeDtypeStruct((tiles // parts, PACK, cap), BF16)] * parts,
        scratch_shapes=[pltpu.VMEM((tiles, PACK, cap), BF16)],
        compiler_params=params(),
        cost_estimate=cost(1000, 1000),
    )(near, exhaust.T, owner.reshape(1, count), cells.reshape(1, count))


def source_kernel(*refs):
    got_refs, out_ref = refs[:-1], refs[-1]
    places = out_ref.shape[0]
    got = jnp.concatenate([ref[ref.shape[0] - PACK :] for ref in got_refs], axis=1)
    slots = got.shape[1]
    cells = (got[C : C + 1].astype(F32) * HALF + got[C + 1 : C + 2].astype(F32)).astype(jnp.int32)
    place, within = cells // SEG, cells % SEG
    lane = lax.broadcasted_iota(jnp.int32, (SL, slots), 0) // C
    spread = jnp.where(lane == within, jnp.concatenate([got[:C]] * SEG, axis=0).astype(F32), 0.0)
    row = lax.broadcasted_iota(jnp.int32, (places, slots), 0)
    chosen = (row == place).astype(BF16)
    out_ref[...] = lax.dot_general(chosen, spread.astype(BF16), NT, preferred_element_type=F32)


def make_source(got, places):
    full = pl.BlockSpec(memory_space=pltpu.VMEM)
    return pl.pallas_call(
        source_kernel,
        in_specs=[full] * len(got),
        out_specs=full,
        out_shape=jax.ShapeDtypeStruct((places, SL), F32),
        compiler_params=params(),
        cost_estimate=cost(1000, 1000),
    )(*got)


def vertical_kernel(height, me_ref, *refs):
    count = len(refs) - 5
    piece_refs = refs[:count]
    source_ref, weight_ref, bias_ref, out_ref, held = refs[count:]
    levels, rows, _ = held.shape
    per = levels // count
    for d, piece_ref in enumerate(piece_refs):
        for z in range(per):
            held[(me_ref[0] ^ d) * per + z] = piece_ref[z * rows : (z + 1) * rows]
    bias = bias_row(bias_ref[...])
    layers = weight_ref.shape[0]
    zero = jnp.zeros((rows, HALF), BF16)
    tiles = [[held[z, :, h * HALF : (h + 1) * HALF] for h in range(2)] for z in range(levels)]
    for layer in range(layers):
        taps = []
        for k in range(KV + 1):
            column = []
            for zp in range(levels // 2):
                z = 2 * zp + k - KV // 2
                for h in range(2):
                    column.append(tiles[z][h] if 0 <= z < levels else zero)
            taps.append(jnp.concatenate(column, axis=0))
        total = jnp.dot(
            jnp.concatenate(taps, axis=1), weight_ref[layer], preferred_element_type=F32
        )
        following = []
        for z in range(levels):
            following.append([])
            for h in range(2):
                start = ((z // 2) * 2 + h) * rows
                lane = (z % 2) * HALF
                part = total[start : start + rows, lane : lane + HALF]
                value = tiles[z][h].astype(F32) + gelu(part + bias[layer : layer + 1])
                if layer == layers - 1:
                    value = value + source_ref[z, :, h * HALF : (h + 1) * HALF]
                following[z].append(value.astype(BF16))
        tiles = following
    across = rows // height
    group = 256 // rows
    swap = swap_matrix(group * height, across)
    size = group * height
    for g in range(levels // group):
        pieces = [jnp.concatenate(tiles[g * group + z], axis=1) for z in range(group)]
        turned = jnp.dot(
            swap, jnp.concatenate(pieces, axis=0), preferred_element_type=F32
        ).astype(BF16)
        for s in range(across):
            out_ref[g * group : (g + 1) * group, :, s * SL : (s + 1) * SL] = turned[
                s * size : (s + 1) * size
            ].reshape(group, height, SL)


def vertical(me, pieces, source, weight, bias, height):
    levels, rows, _ = source.shape
    lanes = rows // height * SL
    full = pl.BlockSpec(memory_space=pltpu.VMEM)
    return pl.pallas_call(
        functools.partial(vertical_kernel, height),
        in_specs=[pl.BlockSpec(memory_space=pltpu.SMEM)] + [full] * (len(pieces) + 3),
        out_specs=full,
        out_shape=jax.ShapeDtypeStruct((levels, height, lanes), BF16),
        scratch_shapes=[pltpu.VMEM((levels, rows, SL), BF16)],
        compiler_params=params(),
        cost_estimate=cost(4 * levels * rows * weight.shape[1] * SL, 6 * 10**6),
    )(me, *pieces, source, weight, bias)


def exchange(block, distance):
    count = lax.axis_size("cols")
    return lax.ppermute(block, "cols", [(i, i ^ distance) for i in range(count)])


def body(
    field, depth_kernel, point_weight, point_bias, vert_weight, vert_bias, exhaust, owner, cells
):
    columns, bands = lax.axis_size("cols"), lax.axis_size("rows")
    forward = [(i, i + 1) for i in range(bands - 1)]
    backward = [(target, source) for source, target in forward]
    levels, height, lanes = field.shape
    segments = lanes // SL
    per = segments // columns
    me = lax.axis_index("cols")
    own, first, last = to_segments(field)
    low = lax.ppermute(last, "rows", forward)
    high = lax.ppermute(first, "rows", backward)
    across = across_weights(depth_kernel, point_weight)
    bias = point_bias.reshape(1, C)
    if per % 16 == 0 and columns % 2 == 0:
        tiles = columns // 2
        spot, near = me % tiles, me // tiles
        place = lambda half: jnp.stack([half * (segments // 2), spot]).astype(jnp.int32)
        close_rows, far_rows = bucket(
            near.reshape(1).astype(jnp.int32), exhaust, owner, cells, columns, 2
        )
        relayed = exchange(far_rows, tiles)
        far = half_horizontal(place(1 - near), own, low, high, across, bias, tiles)
        pieces = [exchange(block, tiles + slot) for slot, block in enumerate(far)]
        spot_near, _ = lax.optimization_barrier((place(near), far[0]))
        close = half_horizontal(
            spot_near, own, low, high, across, bias, tiles, (close_rows, relayed)
        )
        close = [exchange(block, slot) if slot else block for slot, block in enumerate(close)]
        pieces += close
        got = close
        at = me ^ tiles
    else:
        (sent,) = bucket(jnp.zeros((1,), jnp.int32), exhaust, owner, cells, columns, 1)
        got = lax.all_to_all(sent, "cols", split_axis=0, concat_axis=0, tiled=True)
        got = [jnp.transpose(got, (1, 0, 2)).reshape(PACK, -1)]
        mixed = horizontal(own, low, high, across, bias, columns)
        mixed = mixed.reshape(columns, levels, -1, SL)
        taken = lax.all_to_all(mixed, "cols", split_axis=0, concat_axis=0, tiled=True)
        pieces = [taken.reshape(-1, SL)]
        at = me * 0
    depth = columns * levels
    source = make_source(got, depth * height * per).reshape(depth, height * per, SL)
    up = up_weights(vert_weight)
    return vertical(at.reshape(1).astype(jnp.int32), pieces, source, up, vert_bias, height)


def solution(mesh):
    placed = (
        P("cols", "rows", None),
        P(),
        P(),
        P(),
        P(),
        P(),
        P(("rows", "cols"), None),
        P(("rows", "cols"), None),
        P(("rows", "cols")),
    )
    return jax.shard_map(
        body, mesh=mesh, in_specs=placed, out_specs=P(None, "rows", "cols"), check_vma=False
    )
```

```python
import functools

import jax
import jax.numpy as jnp
from jax import lax
from jax.experimental import pallas as pl
from jax.experimental.pallas import tpu as pltpu
from jax.sharding import PartitionSpec as P

C = 32
KH = 7
KV = 9
SEG = 8
SL = SEG * C
PAD = 2
TAPS = (KV + 1) // 2
HALF = SL // 2
PACK = 48
VMEM = 20 * 1024 * 1024
NT = (((1,), (1,)), ((), ()))
F32 = jnp.float32
BF16 = jnp.bfloat16


def params():
    return pltpu.CompilerParams(vmem_limit_bytes=VMEM)


def cost(flops, moved):
    return pl.CostEstimate(flops=flops, bytes_accessed=moved, transcendentals=0)


def whole(shape):
    return pl.BlockSpec(shape, lambda *_: (0,) * len(shape))


def gelu(x):
    return 0.5 * x * (1.0 + jnp.tanh(0.7978845608028654 * (x + 0.044715 * (x * x * x))))


def swap_matrix(outer, inner):
    size = outer * inner
    row = lax.broadcasted_iota(jnp.int32, (size, size), 0)
    column = lax.broadcasted_iota(jnp.int32, (size, size), 1)
    return (column == (row % outer) * inner + row // outer).astype(BF16)


def segment_kernel(ids_ref, field_ref, own_ref, cross_ref, pair_ref):
    levels, height, lanes = field_ref.shape
    rows = levels * height
    group = 256 // rows
    swap = swap_matrix(group, rows)
    for g in range(lanes // (group * SL)):
        at = [(g * group + s) * SL for s in range(group)]
        pieces = [field_ref[:, :, n : n + SL].reshape(rows, SL) for n in at]
        got = jnp.dot(
            swap, jnp.concatenate(pieces, axis=0), preferred_element_type=F32
        ).astype(BF16)
        for z in range(levels):
            for y in range(height):
                start = (z * height + y) * group
                own_ref[y, z, g * group : (g + 1) * group] = got[start : start + group]
    odd = ids_ref[1] % 2
    for y in range(3):
        cross_ref[y] = own_ref[odd * (height - 3) + y]
        pair_ref[y] = own_ref[(1 - odd) * (height - 3) + y]


def to_segments(ids, field):
    levels, height, lanes = field.shape
    full = pl.BlockSpec(memory_space=pltpu.VMEM)
    out = lambda n: jax.ShapeDtypeStruct((n, levels, lanes // SL, SL), BF16)
    return pl.pallas_call(
        segment_kernel,
        in_specs=[pl.BlockSpec(memory_space=pltpu.SMEM), full],
        out_specs=[full] * 3,
        out_shape=[out(height), out(3), out(3)],
        compiler_params=params(),
        cost_estimate=cost(1000, 1000),
    )(ids, field)


def across_kernel(depth_ref, point_ref, out_ref):
    point = jnp.concatenate([point_ref[...].astype(F32)] * (HALF // C), axis=1)
    lane = lax.broadcasted_iota(jnp.int32, (C, HALF), 1) // C
    wide = 3 * HALF
    out_ref[...] = jnp.zeros_like(out_ref)
    for i in range(KH):
        columns = jnp.transpose(depth_ref[i])
        scaled = [point * columns[:, j : j + 1] for j in range(KH)]
        for xt in range(wide // C):
            block = jnp.zeros((C, HALF), F32)
            for xo in range(HALF // C):
                j = xt - 1 - xo
                if 0 <= j < KH:
                    block = jnp.where(lane == xo, scaled[j], block)
            block = block.astype(BF16)
            for yo in range(2):
                row = (i + yo + PAD) * wide + xt * C
                out_ref[row : row + C, yo * HALF : (yo + 1) * HALF] = block


def across_weights(depth_kernel, point_weight):
    return pl.pallas_call(
        across_kernel,
        out_shape=jax.ShapeDtypeStruct(((KH + 1 + 2 * PAD) * 3 * HALF, SL), BF16),
        compiler_params=params(),
        cost_estimate=cost(1000, 1000),
    )(depth_kernel, point_weight)


def up_kernel(tiles, ids_ref, vert_ref, out_ref):
    row = lax.broadcasted_iota(jnp.int32, (KV * HALF, KV * C), 0)
    column = lax.broadcasted_iota(jnp.int32, (KV * HALF, KV * C), 1)
    spread = ((row // HALF == column // C) & (row % C == column % C)).astype(BF16)
    row = lax.broadcasted_iota(jnp.int32, (C, HALF), 0)
    column = lax.broadcasted_iota(jnp.int32, (C, HALF), 1)
    repeat = (row == column % C).astype(BF16)
    row = lax.broadcasted_iota(jnp.int32, (KV * HALF, HALF), 0)
    column = lax.broadcasted_iota(jnp.int32, (KV * HALF, HALF), 1)
    same = (row % HALF) // C == column // C
    zero = jnp.zeros((HALF, HALF), BF16)
    for layer in range(vert_ref.shape[0]):
        tall = lax.dot_general(spread, vert_ref[layer], NT, preferred_element_type=F32).astype(BF16)
        wide = jnp.dot(tall, repeat, preferred_element_type=F32)
        wide = jnp.where(same, wide, 0.0).astype(BF16)
        for block in range(TAPS):
            at = pl.multiple_of(turned_index(ids_ref, tiles, block, TAPS) * SL, SL)
            for zi in range(2):
                parts = []
                for zo in range(2):
                    k = 2 * block + zi - zo
                    parts.append(wide[k * HALF : (k + 1) * HALF] if 0 <= k < KV else zero)
                out_ref[layer, pl.ds(at + zi * HALF, HALF)] = jnp.concatenate(parts, axis=1)


def turned_index(ids_ref, tiles, index, count):
    if not tiles:
        return index
    return jnp.where(ids_ref[0] // tiles == 0, index, count - 1 - index)


def up_weights(ids, vert_weight, tiles):
    vert = jnp.transpose(vert_weight, (0, 2, 1))
    full = pl.BlockSpec(memory_space=pltpu.VMEM)
    return pl.pallas_call(
        functools.partial(up_kernel, tiles),
        in_specs=[pl.BlockSpec(memory_space=pltpu.SMEM), full],
        out_specs=full,
        out_shape=jax.ShapeDtypeStruct((vert.shape[0], TAPS * SL, SL), BF16),
        compiler_params=params(),
        cost_estimate=cost(1000, 1000),
    )(ids, vert)


def bias_row(row):
    return jnp.concatenate([row] * (HALF // C), axis=1)


def horizontal_kernel(own_ref, low_ref, high_ref, weight_ref, bias_ref, out_ref):
    height = own_ref.shape[0]
    segments = own_ref.shape[2]
    row = lax.broadcasted_iota(jnp.int32, (segments, HALF), 0)
    lines = [low_ref[y, 0] for y in range(3)]
    lines += [own_ref[y, 0] for y in range(height)]
    lines += [high_ref[y, 0] for y in range(3)]
    left, right = [], []
    for line in lines:
        a0, a1 = line[:, :HALF], line[:, HALF:]
        before = jnp.where(row == 0, 0.0, pltpu.roll(a1.astype(F32), 1, 0)).astype(BF16)
        after = jnp.where(
            row == segments - 1, 0.0, pltpu.roll(a0.astype(F32), segments - 1, 0)
        ).astype(BF16)
        left.append([before, a0, a1])
        right.append([a0, a1, after])
    stacked = []
    for yp in range(height // 2):
        for side in (left, right):
            stacked.append(
                jnp.concatenate(
                    [tile for y in range(2 * yp, 2 * yp + KH + 1) for tile in side[y]], axis=1
                )
            )
    wide = 3 * HALF
    total = jnp.dot(
        jnp.concatenate(stacked, axis=0),
        weight_ref[PAD * wide : (PAD + KH + 1) * wide],
        preferred_element_type=F32,
    )
    bias = bias_row(bias_ref[...])
    tiles, _, _, per, _ = out_ref.shape
    for yp in range(height // 2):
        for h in range(2):
            start = (yp * 2 + h) * segments
            for yo in range(2):
                y = 2 * yp + yo
                part = total[start : start + segments, yo * HALF : (yo + 1) * HALF]
                center = lines[y + 3][:, h * HALF : (h + 1) * HALF].astype(F32)
                value = (center + gelu(part + bias)).astype(BF16)
                out_ref[:, 0, y, :, h * HALF : (h + 1) * HALF] = value.reshape(tiles, per, HALF)


def horizontal(own, low, high, weight, bias, tiles):
    height, levels, segments, _ = own.shape
    direct = (segments // tiles) % 16 == 0
    parts = tiles if direct else 1
    per = segments // parts
    line = lambda n: pl.BlockSpec((n, 1, segments, SL), lambda z: (0, z, 0, 0))
    out = pl.pallas_call(
        horizontal_kernel,
        grid=(levels,),
        in_specs=[line(height), line(3), line(3), whole(weight.shape), whole(bias.shape)],
        out_specs=pl.BlockSpec((parts, 1, height, per, SL), lambda z: (0, z, 0, 0, 0)),
        out_shape=jax.ShapeDtypeStruct((parts, levels, height, per, SL), BF16),
        compiler_params=params(),
        cost_estimate=cost(
            2 * levels * height * segments * weight.shape[0] * SL // 2, 4 * 10**6
        ),
    )(own, low, high, weight, bias)
    if not direct:
        out = out.reshape(levels, height, tiles, segments // tiles, SL)
        out = jnp.transpose(out, (2, 0, 1, 3, 4))
    return out


def line_sides(line, ahead, behind):
    count = line.shape[0]
    a0, a1 = line[:, :HALF], line[:, HALF:]
    before = jnp.concatenate([ahead, a1.astype(F32)], axis=0)
    before = pltpu.roll(before, 1, 0)[16:].astype(BF16)
    after = jnp.concatenate([a0.astype(F32), behind], axis=0)
    after = pltpu.roll(after, count + 15, 0)[:count].astype(BF16)
    return [before, a0, a1], [a0, a1, after]


def halo_weight(weight_ref, first, yp):
    wide = 3 * HALF
    at = pl.multiple_of((first - 2 * yp + PAD) * wide, wide)
    return weight_ref[pl.ds(at, 3 * wide)]


def early_kernel(ids_ref, own_ref, pair_ref, weight_ref, out_ref):
    height, levels, segments, _ = own_ref.shape
    wide = 3 * HALF
    zero = jnp.zeros((16, HALF), F32)
    own, pair = [], []
    for z in range(levels):
        for rows, ref in ((own, own_ref), (pair, pair_ref)):
            sides = [line_sides(ref[y, z], zero, zero) for y in range(ref.shape[0])]
            for h in range(2):
                rows.append(jnp.concatenate([tile for side in sides for tile in side[h]], axis=1))
    own = jnp.concatenate(own, axis=0)
    pair = jnp.concatenate(pair, axis=0)
    first = (1 - ids_ref[1] % 2) * (height + 3)
    for yp in range(height // 2):
        at = (3 - 2 * yp + PAD) * wide
        total = jnp.dot(own, weight_ref[at : at + height * wide], preferred_element_type=F32)
        total += jnp.dot(pair, halo_weight(weight_ref, first, yp), preferred_element_type=F32)
        out_ref[yp] = total.reshape(levels, 2, segments, SL)


def early_horizontal(ids, own, pair, weight):
    height, levels, segments, _ = own.shape
    full = pl.BlockSpec(memory_space=pltpu.VMEM)
    return pl.pallas_call(
        early_kernel,
        in_specs=[pl.BlockSpec(memory_space=pltpu.SMEM)] + [full] * 3,
        out_specs=full,
        out_shape=jax.ShapeDtypeStruct((height // 2, levels, 2, segments, SL), F32),
        compiler_params=params(),
        cost_estimate=cost(1000, 1000),
    )(ids, own, pair, weight)


def half_kernel(tiles, is_near, ids_ref, own_ref, cross_ref, early_ref, *rest):
    weight_ref, bias_ref = rest[:2]
    rest, done = rest[2:-1], rest[-1]
    extra_refs, out_refs = rest[:-tiles], rest[-tiles:]
    height, levels, segments, _ = own_ref.shape
    size = segments // 2
    near = ids_ref[0] // tiles
    start = pl.multiple_of((near if is_near else 1 - near) * size, size)
    per = size // tiles
    ahead = pl.multiple_of(jnp.maximum(start - 16, 0), 16)
    behind = pl.multiple_of(jnp.minimum(start + size, segments - 16), 16)
    has_ahead = jnp.where(start > 0, 1.0, 0.0)
    has_behind = jnp.where(start + size < segments, 1.0, 0.0)
    bias = bias_row(bias_ref[...])
    cross = []
    for z in range(levels):
        sides = []
        for y in range(3):
            sides.append(
                line_sides(
                    cross_ref[y, z, pl.ds(start, size)],
                    cross_ref[y, z, pl.ds(ahead, 16), HALF:].astype(F32) * has_ahead,
                    cross_ref[y, z, pl.ds(behind, 16), :HALF].astype(F32) * has_behind,
                )
            )
        for h in range(2):
            cross.append(jnp.concatenate([tile for side in sides for tile in side[h]], axis=1))
    cross = jnp.concatenate(cross, axis=0)
    first = ids_ref[1] % 2 * (height + 3)
    for yp in range(height // 2):
        total = jnp.dot(cross, halo_weight(weight_ref, first, yp), preferred_element_type=F32)
        for z in range(levels):
            for h in range(2):
                row = (z * 2 + h) * size
                part = total[row : row + size] + early_ref[yp, z, h, pl.ds(start, size)]
                for yo in range(2):
                    y = 2 * yp + yo
                    center = own_ref[y, z, pl.ds(start, size), h * HALF : (h + 1) * HALF]
                    value = gelu(part[:, yo * HALF : (yo + 1) * HALF] + bias)
                    value = (center.astype(F32) + value).astype(BF16)
                    at = ((z // 2 * 2 + h) * height + y) * per
                    lane = z % 2 * HALF
                    done[:, at : at + per, lane : lane + HALF] = value.reshape(tiles, per, HALF)
    rows = levels * height * per
    for slot, out_ref in enumerate(out_refs):
        tile = ids_ref[0] % tiles ^ slot
        out_ref[:rows] = done[tile]
        for n, extra_ref in enumerate(extra_refs):
            out_ref[rows:, n * HALF : (n + 1) * HALF] = extra_ref[tile]


def half_horizontal(ids, own, cross, early, weight, bias, tiles, is_near, extra=()):
    height, levels, segments, _ = own.shape
    per = segments // (2 * tiles)
    rows = levels * height * per
    full = pl.BlockSpec(memory_space=pltpu.VMEM)
    shape = (rows + (PACK if extra else 0), SL)
    return pl.pallas_call(
        functools.partial(half_kernel, tiles, is_near),
        in_specs=[pl.BlockSpec(memory_space=pltpu.SMEM)] + [full] * (5 + len(extra)),
        out_specs=[full] * tiles,
        out_shape=[jax.ShapeDtypeStruct(shape, BF16)] * tiles,
        scratch_shapes=[pltpu.VMEM((tiles, rows, SL), BF16)],
        compiler_params=params(),
        cost_estimate=cost(1000, 1000),
    )(ids, own, cross, early, weight, bias, *extra)


def bucket_kernel(ids_ref, rows_ref, owner_ref, cells_ref, *rest):
    out_refs, held = rest[:-1], rest[-1]
    count = rows_ref.shape[1]
    tiles, _, cap = held.shape
    owner, cells = owner_ref[...], cells_ref[...]
    row = lax.broadcasted_iota(jnp.int32, (count, count), 0)
    column = lax.broadcasted_iota(jnp.int32, (count, count), 1)
    before = (row < column).astype(BF16)
    named = (lax.broadcasted_iota(jnp.int32, (tiles, count), 0) == owner).astype(F32)
    rank = jnp.dot(named.astype(BF16), before, preferred_element_type=F32)
    rank = jnp.sum(rank * named, axis=0, keepdims=True).astype(jnp.int32)
    slot = owner * cap + rank
    chosen = lax.broadcasted_iota(jnp.int32, (tiles * cap, count), 0) == slot
    coarse = (cells // HALF).astype(F32)
    fine = (cells % HALF).astype(F32)
    index = lax.broadcasted_iota(jnp.int32, (PACK - C, count), 0)
    places = jnp.where(index == 0, coarse, jnp.where(index == 1, fine, 0.0)).astype(BF16)
    payload = jnp.concatenate([rows_ref[...], places], axis=0)
    out = lax.dot_general(
        payload, chosen.astype(BF16), NT, preferred_element_type=F32
    ).astype(BF16)
    if cap % HALF == 0:
        for t in range(tiles):
            held[t] = out[:, t * cap : (t + 1) * cap]
    else:
        held[...] = jnp.swapaxes(out.reshape(PACK, tiles, cap), 0, 1)
    size = tiles // len(out_refs)
    for n, out_ref in enumerate(out_refs):
        out_ref[...] = held[pl.ds((ids_ref[0] // size ^ n) * size, size)]


def bucket(ids, exhaust, owner, cells, tiles):
    count = exhaust.shape[0]
    cap = 2 * count // tiles
    full = pl.BlockSpec(memory_space=pltpu.VMEM)
    return pl.pallas_call(
        bucket_kernel,
        in_specs=[pl.BlockSpec(memory_space=pltpu.SMEM)] + [full] * 3,
        out_specs=[full],
        out_shape=[jax.ShapeDtypeStruct((tiles, PACK, cap), BF16)],
        scratch_shapes=[pltpu.VMEM((tiles, PACK, cap), BF16)],
        compiler_params=params(),
        cost_estimate=cost(1000, 1000),
    )(ids, exhaust.T, owner.reshape(1, count), cells.reshape(1, count))


def source_kernel(tiles, rows, ids_ref, *refs):
    got_refs, out_ref = refs[:-1], refs[-1]
    places = out_ref.shape[0]
    pairs = places // (2 * rows)
    got = jnp.concatenate([ref[ref.shape[0] - PACK :] for ref in got_refs], axis=1)
    slots = got.shape[1]
    cells = (got[C : C + 1].astype(F32) * HALF + got[C + 1 : C + 2].astype(F32)).astype(jnp.int32)
    x, row, level = cells % SEG, cells // SEG % rows, cells // (SEG * rows)
    pair = turned_index(ids_ref, tiles, level // 2, pairs)
    place = (pair * 2 + x // (SEG // 2)) * rows + row
    within = level % 2 * (SEG // 2) + x % (SEG // 2)
    lane = lax.broadcasted_iota(jnp.int32, (SL, slots), 0) // C
    spread = jnp.where(lane == within, jnp.concatenate([got[:C]] * SEG, axis=0).astype(F32), 0.0)
    index = lax.broadcasted_iota(jnp.int32, (places, slots), 0)
    chosen = (index == place).astype(BF16)
    out_ref[...] = lax.dot_general(chosen, spread.astype(BF16), NT, preferred_element_type=F32)


def make_source(ids, got, places, rows, tiles):
    full = pl.BlockSpec(memory_space=pltpu.VMEM)
    return pl.pallas_call(
        functools.partial(source_kernel, tiles, rows),
        in_specs=[pl.BlockSpec(memory_space=pltpu.SMEM)] + [full] * len(got),
        out_specs=full,
        out_shape=jax.ShapeDtypeStruct((places, SL), F32),
        compiler_params=params(),
        cost_estimate=cost(1000, 1000),
    )(ids, *got)


def prepare_kernel(ids_ref, depth_ref, point_ref, rows_ref, owner_ref, cells_ref, *rest):
    across_ref, close_ref, far_ref, held = rest
    bucket_kernel(ids_ref, rows_ref, owner_ref, cells_ref, close_ref, far_ref, held)
    across_kernel(depth_ref, point_ref, across_ref)


def prepare(ids, depth_kernel, point_weight, exhaust, owner, cells, tiles):
    count = exhaust.shape[0]
    cap = 2 * count // tiles
    full = pl.BlockSpec(memory_space=pltpu.VMEM)
    block = jax.ShapeDtypeStruct((tiles // 2, PACK, cap), BF16)
    return pl.pallas_call(
        prepare_kernel,
        in_specs=[pl.BlockSpec(memory_space=pltpu.SMEM)] + [full] * 5,
        out_specs=[full] * 3,
        out_shape=[jax.ShapeDtypeStruct(((KH + 1 + 2 * PAD) * 3 * HALF, SL), BF16), block, block],
        scratch_shapes=[pltpu.VMEM((tiles, PACK, cap), BF16)],
        compiler_params=params(),
        cost_estimate=cost(1000, 1000),
    )(
        ids,
        depth_kernel,
        point_weight,
        exhaust.T,
        owner.reshape(1, count),
        cells.reshape(1, count),
    )


def chunks(first, last, size):
    return [(n, min(n + size, last)) for n in range(first, last, size)]


def layer_step(held, base, first, last, block, weight, bias):
    taps = [held[(first - base + k) * block : (last - base + k) * block] for k in range(TAPS)]
    total = jnp.dot(jnp.concatenate(taps, axis=1), weight, preferred_element_type=F32)
    center = held[(first - base + 2) * block : (last - base + 2) * block].astype(F32)
    return center + gelu(total + bias)


def put_group(out_ref, value, height, block, at_of):
    rows = block // 2
    count = 256 // block
    across = rows // height
    swap = swap_matrix(2 * count * height, across)
    for g in range(value.shape[0] // (count * block)):
        pieces = []
        for n in range(count):
            start = (g * count + n) * block
            for j in range(2):
                lane = slice(j * HALF, (j + 1) * HALF)
                pieces.append(
                    jnp.concatenate(
                        [value[start : start + rows, lane], value[start + rows : start + block, lane]],
                        axis=1,
                    )
                )
        turned = jnp.dot(
            swap, jnp.concatenate(pieces, axis=0), preferred_element_type=F32
        ).astype(BF16)
        size = 2 * height
        for n in range(count):
            at = at_of(g * count + n) * 2
            for s in range(across):
                start = (s * count + n) * size
                out_ref[pl.ds(at, 2), :, s * SL : (s + 1) * SL] = turned[
                    start : start + size
                ].reshape(2, height, SL)


def near_kernel(tiles, height, ids_ref, *refs):
    piece_refs = refs[:tiles]
    source_ref, weight_ref, bias_ref, out_ref, kept_ref, later_ref, held, step = refs[tiles:]
    pairs = out_ref.shape[0] // 2 + 4
    block = kept_ref.shape[0] // 4
    bias = [bias_row(bias_ref[n : n + 1]) for n in range(2)]
    bias = [jnp.concatenate([row, row], axis=1) for row in bias]
    held[: 2 * block] = jnp.zeros((2 * block, SL), BF16)
    step[: 2 * block] = jnp.zeros((2 * block, SL), BF16)
    per = pairs // tiles
    for d, piece_ref in enumerate(piece_refs):
        for n in range(per):
            number = (ids_ref[0] % tiles ^ d) * per + n
            at = turned_index(ids_ref, tiles, number, pairs) + 2
            held[pl.ds(pl.multiple_of(at * block, block), block)] = piece_ref[
                n * block : (n + 1) * block
            ]
    kept_ref[...] = held[(pairs - 2) * block : (pairs + 2) * block]
    for first, last in chunks(0, pairs - 2, 4):
        value = layer_step(held, 0, first, last, block, weight_ref[0], bias[0])
        step[(first + 2) * block : (last + 2) * block] = value.astype(BF16)
    later_ref[...] = step[(pairs - 4) * block : pairs * block]
    for first, last in chunks(0, pairs - 4, 4):
        value = layer_step(step, 0, first, last, block, weight_ref[1], bias[1])
        value = (value + source_ref[first * block : last * block]).astype(BF16)
        put_group(
            out_ref,
            value,
            height,
            block,
            lambda n: turned_index(ids_ref, tiles, first + n, pairs - 4),
        )


def far_kernel(tiles, height, ids_ref, *refs):
    piece_refs = refs[:tiles]
    early_ref, kept_ref, later_ref, source_ref, weight_ref, bias_ref, out_ref, held, step = refs[tiles:]
    pairs = out_ref.shape[0] // 2
    half = pairs // 2
    block = kept_ref.shape[0] // 4
    bias = [bias_row(bias_ref[n : n + 1]) for n in range(2)]
    bias = [jnp.concatenate([row, row], axis=1) for row in bias]
    held[: 4 * block] = kept_ref[...]
    held[(half + 4) * block :] = jnp.zeros((2 * block, SL), BF16)
    step[: 4 * block] = later_ref[...]
    step[(half + 6) * block :] = jnp.zeros((2 * block, SL), BF16)
    per = half // tiles
    for d, piece_ref in enumerate(piece_refs):
        for n in range(per):
            number = (ids_ref[0] % tiles ^ d) * per + n
            at = turned_index(ids_ref, tiles, number, half) + 4
            held[pl.ds(pl.multiple_of(at * block, block), block)] = piece_ref[
                n * block : (n + 1) * block
            ]
    for first, last in chunks(half - 2, pairs, 5):
        value = layer_step(held, half - 2, first, last, block, weight_ref[0], bias[0])
        step[(first - half + 6) * block : (last - half + 6) * block] = value.astype(BF16)
    early = early_ref.shape[0]
    out_ref[pl.ds(turned_index(ids_ref, tiles, 0, 2 * pairs // early) * early, early)] = early_ref[...]
    for first, last in chunks(half - 4, pairs, 4):
        value = layer_step(step, half - 4, first, last, block, weight_ref[1], bias[1])
        value = (value + source_ref[first * block : last * block]).astype(BF16)
        put_group(
            out_ref, value, height, block, lambda n: turned_index(ids_ref, tiles, first + n, pairs)
        )


def whole_kernel(height, ids_ref, piece_ref, source_ref, weight_ref, bias_ref, out_ref, held, step):
    levels = out_ref.shape[0]
    pairs = levels // 2
    rows = piece_ref.shape[0] // levels
    block = 2 * rows
    bias = [bias_row(bias_ref[n : n + 1]) for n in range(2)]
    bias = [jnp.concatenate([row, row], axis=1) for row in bias]
    for buffer in (held, step):
        buffer[: 2 * block] = jnp.zeros((2 * block, SL), BF16)
        buffer[(pairs + 2) * block :] = jnp.zeros((2 * block, SL), BF16)
    for z in range(levels):
        for h in range(2):
            start = (z // 2 + 2) * block + h * rows
            held[start : start + rows, z % 2 * HALF : (z % 2 + 1) * HALF] = piece_ref[
                z * rows : (z + 1) * rows, h * HALF : (h + 1) * HALF
            ]
    value = layer_step(held, 0, 0, pairs, block, weight_ref[0], bias[0])
    step[2 * block : (pairs + 2) * block] = value.astype(BF16)
    value = layer_step(step, 0, 0, pairs, block, weight_ref[1], bias[1])
    value = (value + source_ref[...]).astype(BF16)
    put_group(out_ref, value, height, block, lambda n: n)


def vertical(ids, close, far, source, weight, bias, levels, height, tiles):
    full = pl.BlockSpec(memory_space=pltpu.VMEM)
    smem = pl.BlockSpec(memory_space=pltpu.SMEM)
    rows = source.shape[0] // levels
    block = 2 * rows
    pairs = levels // 2
    lanes = rows // height * SL
    buffer = lambda count: pltpu.VMEM((count * block, SL), BF16)
    array = lambda count: jax.ShapeDtypeStruct((count * block, SL), BF16)
    result = lambda count: jax.ShapeDtypeStruct((count, height, lanes), BF16)
    if not far:
        return pl.pallas_call(
            functools.partial(whole_kernel, height),
            in_specs=[smem] + [full] * 4,
            out_specs=full,
            out_shape=result(levels),
            scratch_shapes=[buffer(pairs + 4)] * 2,
            compiler_params=params(),
            cost_estimate=cost(1000, 1000),
        )(ids, *close, source, weight, bias)
    half = pairs // 2
    early, kept, later = pl.pallas_call(
        functools.partial(near_kernel, tiles, height),
        in_specs=[smem] + [full] * (len(close) + 3),
        out_specs=[full] * 3,
        out_shape=[result(2 * (half - 4)), array(4), array(4)],
        scratch_shapes=[buffer(half + 2), buffer(half)],
        compiler_params=params(),
        cost_estimate=cost(1000, 1000),
    )(ids, *close, source, weight, bias)
    return pl.pallas_call(
        functools.partial(far_kernel, tiles, height),
        in_specs=[smem] + [full] * (len(far) + 6),
        out_specs=full,
        out_shape=result(levels),
        scratch_shapes=[buffer(half + 6), buffer(half + 8)],
        compiler_params=params(),
        cost_estimate=cost(1000, 1000),
    )(ids, *far, early, kept, later, source, weight, bias)


def exchange(block, distance):
    count = lax.axis_size("cols")
    return lax.ppermute(block, "cols", [(i, i ^ distance) for i in range(count)])


def body(
    field, depth_kernel, point_weight, point_bias, vert_weight, vert_bias, exhaust, owner, cells
):
    columns, bands = lax.axis_size("cols"), lax.axis_size("rows")
    forward = [(i, i + 1) for i in range(bands - 1)]
    backward = [(target, source) for source, target in forward]
    levels, height, lanes = field.shape
    segments = lanes // SL
    per = segments // columns
    ids = jnp.stack([lax.axis_index("cols"), lax.axis_index("rows")]).astype(jnp.int32)
    bias = point_bias.reshape(1, C)
    if per % 16 == 0 and columns % 2 == 0 and bands % 2 == 0 and 256 % (levels * height) == 0:
        tiles = columns // 2
        own, cross, pair = to_segments(ids, field)
        inside = [(i, i ^ 1) for i in range(bands)]
        beyond = [(i, i + 1 if i % 2 else i - 1) for i in range(1, bands - 1)]
        cross = lax.ppermute(cross, "rows", beyond)
        pair = lax.ppermute(pair, "rows", inside)
        across, close_rows, far_rows = prepare(
            ids, depth_kernel, point_weight, exhaust, owner, cells, columns
        )
        relayed = exchange(far_rows, tiles)
        early = early_horizontal(ids, own, pair, across)
        far = half_horizontal(ids, own, cross, early, across, bias, tiles, False)
        ids_near, _ = lax.optimization_barrier((ids, far[0]))
        far = [exchange(block, tiles + slot) for slot, block in enumerate(far)]
        close = half_horizontal(
            ids_near, own, cross, early, across, bias, tiles, True, (close_rows, relayed)
        )
        close = [exchange(block, slot) if slot else block for slot, block in enumerate(close)]
        got = close
    else:
        tiles, far = 0, []
        (sent,) = bucket(ids, exhaust, owner, cells, columns)
        got = lax.all_to_all(sent, "cols", split_axis=0, concat_axis=0, tiled=True)
        got = [jnp.transpose(got, (1, 0, 2)).reshape(PACK, -1)]
        own = jnp.transpose(field.reshape(levels, height, segments, SL), (1, 0, 2, 3))
        low = lax.ppermute(own[height - 3 :], "rows", forward)
        high = lax.ppermute(own[:3], "rows", backward)
        across = across_weights(depth_kernel, point_weight)
        mixed = horizontal(own, low, high, across, bias, columns)
        mixed = mixed.reshape(columns, levels, -1, SL)
        taken = lax.all_to_all(mixed, "cols", split_axis=0, concat_axis=0, tiled=True)
        close = [taken.reshape(-1, SL)]
    depth = columns * levels
    source = make_source(ids, got, depth * height * per, height * per, tiles)
    up = up_weights(ids, vert_weight, tiles)
    return vertical(ids, close, far, source, up, vert_bias, depth, height, tiles)


def solution(mesh):
    placed = (
        P("cols", "rows", None),
        P(),
        P(),
        P(),
        P(),
        P(),
        P(("rows", "cols"), None),
        P(("rows", "cols"), None),
        P(("rows", "cols")),
    )
    return jax.shard_map(
        body, mesh=mesh, in_specs=placed, out_specs=P(None, "rows", "cols"), check_vma=False
    )
```

```python
import functools

import jax
import jax.numpy as jnp
from jax import lax
from jax.experimental import pallas as pl
from jax.experimental.pallas import tpu as pltpu
from jax.sharding import PartitionSpec as P

C = 32
KH = 7
KV = 9
SEG = 8
SL = SEG * C
PAD = 2
QUAD = 4
TAPS = 3
HALF = SL // 2
PACK = 48
VMEM = 20 * 1024 * 1024
NT = (((1,), (1,)), ((), ()))
F32 = jnp.float32
BF16 = jnp.bfloat16


def params():
    return pltpu.CompilerParams(vmem_limit_bytes=VMEM)


def cost(flops, moved):
    return pl.CostEstimate(flops=flops, bytes_accessed=moved, transcendentals=0)


def whole(shape):
    return pl.BlockSpec(shape, lambda *_: (0,) * len(shape))


def gelu(x):
    return 0.5 * x * (1.0 + jnp.tanh(0.7978845608028654 * (x + 0.044715 * (x * x * x))))


def swap_matrix(outer, inner):
    size = outer * inner
    row = lax.broadcasted_iota(jnp.int32, (size, size), 0)
    column = lax.broadcasted_iota(jnp.int32, (size, size), 1)
    return (column == (row % outer) * inner + row // outer).astype(BF16)


def segment_kernel(ids_ref, field_ref, own_ref, cross_ref, pair_ref):
    levels, height, lanes = field_ref.shape
    rows = levels * height
    group = 256 // rows
    swap = swap_matrix(group, rows)
    for g in range(lanes // (group * SL)):
        at = [(g * group + s) * SL for s in range(group)]
        pieces = [field_ref[:, :, n : n + SL].reshape(rows, SL) for n in at]
        got = jnp.dot(
            swap, jnp.concatenate(pieces, axis=0), preferred_element_type=F32
        ).astype(BF16)
        for z in range(levels):
            for y in range(height):
                start = (z * height + y) * group
                own_ref[y, z, g * group : (g + 1) * group] = got[start : start + group]
    odd = ids_ref[1] % 2
    for y in range(3):
        cross_ref[y] = own_ref[odd * (height - 3) + y]
        pair_ref[y] = own_ref[(1 - odd) * (height - 3) + y]


def to_segments(ids, field):
    levels, height, lanes = field.shape
    full = pl.BlockSpec(memory_space=pltpu.VMEM)
    out = lambda n: jax.ShapeDtypeStruct((n, levels, lanes // SL, SL), BF16)
    return pl.pallas_call(
        segment_kernel,
        in_specs=[pl.BlockSpec(memory_space=pltpu.SMEM), full],
        out_specs=[full] * 3,
        out_shape=[out(height), out(3), out(3)],
        compiler_params=params(),
        cost_estimate=cost(2 * levels * height * lanes * 256, 8 * levels * height * lanes),
    )(ids, field)


def across_kernel(depth_ref, point_ref, out_ref):
    point = jnp.concatenate([point_ref[...].astype(F32)] * (HALF // C), axis=1)
    lane = lax.broadcasted_iota(jnp.int32, (C, HALF), 1) // C
    wide = 3 * HALF
    out_ref[...] = jnp.zeros_like(out_ref)
    for i in range(KH):
        columns = jnp.transpose(depth_ref[i])
        scaled = [point * columns[:, j : j + 1] for j in range(KH)]
        for xt in range(wide // C):
            block = jnp.zeros((C, HALF), F32)
            for xo in range(HALF // C):
                j = xt - 1 - xo
                if 0 <= j < KH:
                    block = jnp.where(lane == xo, scaled[j], block)
            block = block.astype(BF16)
            for yo in range(2):
                row = (i + yo + PAD) * wide + xt * C
                out_ref[row : row + C, yo * HALF : (yo + 1) * HALF] = block


def across_weights(depth_kernel, point_weight):
    return pl.pallas_call(
        across_kernel,
        out_shape=jax.ShapeDtypeStruct(((KH + 1 + 2 * PAD) * 3 * HALF, SL), BF16),
        compiler_params=params(),
        cost_estimate=cost(1000, 1000),
    )(depth_kernel, point_weight)


def up_kernel(tiles, ids_ref, vert_ref, out_ref):
    two = 2 * C
    row = lax.broadcasted_iota(jnp.int32, (KV * two, KV * C), 0)
    column = lax.broadcasted_iota(jnp.int32, (KV * two, KV * C), 1)
    spread = ((row // two == column // C) & (row % C == column % C)).astype(BF16)
    row = lax.broadcasted_iota(jnp.int32, (C, HALF), 0)
    column = lax.broadcasted_iota(jnp.int32, (C, HALF), 1)
    repeat = (row == column % C).astype(BF16)
    row = lax.broadcasted_iota(jnp.int32, (KV * two, HALF), 0)
    column = lax.broadcasted_iota(jnp.int32, (KV * two, HALF), 1)
    same = (row % two) // C == (column % two) // C
    low = lax.broadcasted_iota(jnp.int32, (two, HALF), 1) < two
    for layer in range(vert_ref.shape[0]):
        tall = lax.dot_general(spread, vert_ref[layer], NT, preferred_element_type=F32).astype(BF16)
        wide = jnp.dot(tall, repeat, preferred_element_type=F32)
        wide = jnp.where(same, wide, 0.0)
        tap = lambda k: wide[k * two : (k + 1) * two] if 0 <= k < KV else jnp.zeros((two, HALF), F32)
        for block in range(TAPS):
            at = pl.multiple_of(turned_index(ids_ref, tiles, block, TAPS) * SL, SL)
            rows = []
            for n in range(QUAD):
                zi = QUAD * block + n
                parts = [jnp.where(low, tap(zi - zo), tap(zi - zo - 1)) for zo in (0, 2)]
                rows.append(jnp.concatenate(parts, axis=1))
            out_ref[layer, pl.ds(at, SL)] = jnp.concatenate(rows, axis=0).astype(BF16)


def turned_index(ids_ref, tiles, index, count):
    if not tiles:
        return index
    return jnp.where(ids_ref[0] // tiles == 0, index, count - 1 - index)


def up_weights(ids, vert_weight, tiles):
    vert = jnp.transpose(vert_weight, (0, 2, 1))
    full = pl.BlockSpec(memory_space=pltpu.VMEM)
    return pl.pallas_call(
        functools.partial(up_kernel, tiles),
        in_specs=[pl.BlockSpec(memory_space=pltpu.SMEM), full],
        out_specs=full,
        out_shape=jax.ShapeDtypeStruct((vert.shape[0], TAPS * SL, SL), BF16),
        compiler_params=params(),
        cost_estimate=cost(1000, 1000),
    )(ids, vert)


def bias_row(row):
    return jnp.concatenate([row] * (HALF // C), axis=1)


def horizontal_kernel(own_ref, low_ref, high_ref, weight_ref, bias_ref, out_ref):
    height = own_ref.shape[0]
    segments = own_ref.shape[2]
    row = lax.broadcasted_iota(jnp.int32, (segments, HALF), 0)
    lines = [low_ref[y, 0] for y in range(3)]
    lines += [own_ref[y, 0] for y in range(height)]
    lines += [high_ref[y, 0] for y in range(3)]
    left, right = [], []
    for line in lines:
        a0, a1 = line[:, :HALF], line[:, HALF:]
        before = jnp.where(row == 0, 0.0, pltpu.roll(a1.astype(F32), 1, 0)).astype(BF16)
        after = jnp.where(
            row == segments - 1, 0.0, pltpu.roll(a0.astype(F32), segments - 1, 0)
        ).astype(BF16)
        left.append([before, a0, a1])
        right.append([a0, a1, after])
    stacked = []
    for yp in range(height // 2):
        for side in (left, right):
            stacked.append(
                jnp.concatenate(
                    [tile for y in range(2 * yp, 2 * yp + KH + 1) for tile in side[y]], axis=1
                )
            )
    wide = 3 * HALF
    total = jnp.dot(
        jnp.concatenate(stacked, axis=0),
        weight_ref[PAD * wide : (PAD + KH + 1) * wide],
        preferred_element_type=F32,
    )
    bias = bias_row(bias_ref[...])
    tiles, _, _, per, _ = out_ref.shape
    for yp in range(height // 2):
        for h in range(2):
            start = (yp * 2 + h) * segments
            for yo in range(2):
                y = 2 * yp + yo
                part = total[start : start + segments, yo * HALF : (yo + 1) * HALF]
                center = lines[y + 3][:, h * HALF : (h + 1) * HALF].astype(F32)
                value = (center + gelu(part + bias)).astype(BF16)
                out_ref[:, 0, y, :, h * HALF : (h + 1) * HALF] = value.reshape(tiles, per, HALF)


def horizontal(own, low, high, weight, bias, tiles):
    height, levels, segments, _ = own.shape
    direct = (segments // tiles) % 16 == 0
    parts = tiles if direct else 1
    per = segments // parts
    line = lambda n: pl.BlockSpec((n, 1, segments, SL), lambda z: (0, z, 0, 0))
    out = pl.pallas_call(
        horizontal_kernel,
        grid=(levels,),
        in_specs=[line(height), line(3), line(3), whole(weight.shape), whole(bias.shape)],
        out_specs=pl.BlockSpec((parts, 1, height, per, SL), lambda z: (0, z, 0, 0, 0)),
        out_shape=jax.ShapeDtypeStruct((parts, levels, height, per, SL), BF16),
        compiler_params=params(),
        cost_estimate=cost(
            2 * levels * height * segments * weight.shape[0] * SL // 2, 4 * 10**6
        ),
    )(own, low, high, weight, bias)
    if not direct:
        out = out.reshape(levels, height, tiles, segments // tiles, SL)
        out = jnp.transpose(out, (2, 0, 1, 3, 4))
    return out


def line_sides(line):
    count = line.shape[0]
    row = lax.broadcasted_iota(jnp.int32, (count, HALF), 0)
    a0, a1 = line[:, :HALF], line[:, HALF:]
    before = pltpu.roll(a1.astype(F32), 1, 0)
    before = jnp.where(row == 0, 0.0, before).astype(BF16)
    after = pltpu.roll(a0.astype(F32), count - 1, 0)
    after = jnp.where(row == count - 1, 0.0, after).astype(BF16)
    first, second = [before, a0, a1], [a0, a1, after]
    return jnp.concatenate(first, axis=1), jnp.concatenate(second, axis=1)


def halo_sums(lines, weight_ref, beyond, height):
    wide = 3 * HALF
    first = beyond * (height + 3)
    full = beyond * (height // 2 - 1)
    at = pl.multiple_of((first - 2 * full + PAD) * wide, wide)
    stacked = jnp.concatenate([jnp.concatenate(line, axis=1) for line in lines], axis=0)
    total = jnp.dot(stacked, weight_ref[pl.ds(at, 3 * wide)], preferred_element_type=F32)
    nearest = [jnp.where(beyond == 1, line[0], line[2]) for line in lines]
    thin = height // 2 - 1 - full
    at = pl.multiple_of((first + 2 * (1 - beyond) - 2 * thin + PAD) * wide, wide)
    less = jnp.dot(
        jnp.concatenate(nearest, axis=0), weight_ref[pl.ds(at, wide)], preferred_element_type=F32
    )
    return total, less


def early_kernel(ids_ref, own_ref, pair_ref, weight_ref, out_ref):
    height, levels, segments, _ = own_ref.shape
    wide = 3 * HALF
    own, pair = [], []
    for z in range(levels):
        sides = [line_sides(own_ref[y, z]) for y in range(height)]
        for h in range(2):
            own.append(jnp.concatenate([side[h] for side in sides], axis=1))
        sides = [line_sides(pair_ref[y, z]) for y in range(3)]
        pair += [[side[h] for side in sides] for h in range(2)]
    own = jnp.concatenate(own, axis=0)
    beyond = 1 - ids_ref[1] % 2
    sums = halo_sums(pair, weight_ref, beyond, height)
    for n, total in enumerate(sums):
        yp = beyond if n == 0 else 1 - beyond
        at = pl.multiple_of((3 - 2 * yp + PAD) * wide, wide)
        weight = weight_ref[pl.ds(at, height * wide)]
        total = total + jnp.dot(own, weight, preferred_element_type=F32)
        out_ref[yp] = total.reshape(levels, 2, segments, SL)


def early_horizontal(ids, own, pair, weight):
    height, levels, segments, _ = own.shape
    full = pl.BlockSpec(memory_space=pltpu.VMEM)
    return pl.pallas_call(
        early_kernel,
        in_specs=[pl.BlockSpec(memory_space=pltpu.SMEM)] + [full] * 3,
        out_specs=full,
        out_shape=jax.ShapeDtypeStruct((height // 2, levels, 2, segments, SL), F32),
        compiler_params=params(),
        cost_estimate=cost(1000, 1000),
    )(ids, own, pair, weight)


def swap_halves(first, second):
    low = lax.broadcasted_iota(jnp.int32, first.shape, 1) < HALF // 2
    lower = jnp.where(low, first, pltpu.roll(second, HALF // 2, 1))
    upper = jnp.where(low, pltpu.roll(first, HALF // 2, 1), second)
    return lower, upper


def level_lanes(values):
    sides = [swap_halves(values[n], values[n + 1]) for n in (0, 2)]
    return [jnp.concatenate([side[n] for side in sides], axis=1) for n in range(2)]


def finish_kernel(ids_ref, own_ref, cross_ref, early_ref, weight_ref, bias_ref, *rest):
    extra_refs, out_refs, done = rest[:2], rest[2:-1], rest[-1]
    height, levels, segments, _ = own_ref.shape
    tiles = len(out_refs)
    per = segments // tiles
    bias = bias_row(bias_ref[...])
    cross = []
    for z in range(levels):
        sides = [line_sides(cross_ref[y, z]) for y in range(3)]
        cross += [[side[h] for side in sides] for h in range(2)]
    beyond = ids_ref[1] % 2
    sums = halo_sums(cross, weight_ref, beyond, height)
    for yn, total in enumerate(sums):
        yp = beyond if yn == 0 else 1 - beyond
        for h in range(2):
            for yo in range(2):
                y = 2 * yp + yo
                lane = slice(yo * HALF, (yo + 1) * HALF)
                values = []
                for z in range(levels):
                    row = (z * 2 + h) * segments
                    part = total[row : row + segments, lane] + early_ref[yp, z, h, :, lane]
                    center = own_ref[y, z, :, h * HALF : (h + 1) * HALF]
                    values.append(center.astype(F32) + gelu(part + bias))
                for n, lanes in enumerate(level_lanes(values)):
                    at = pl.multiple_of(((2 * h + n) * height + y) * per, per)
                    done[:, pl.ds(at, per)] = lanes.astype(BF16).reshape(tiles, per, SL)
    rows = levels * height * per
    for slot, out_ref in enumerate(out_refs):
        tile = ids_ref[0] ^ slot
        out_ref[:rows] = done[tile]
        if slot < tiles // 2:
            for n, extra_ref in enumerate(extra_refs):
                out_ref[rows:, n * HALF : (n + 1) * HALF] = extra_ref[tile % (tiles // 2)]


def finish_horizontal(ids, own, cross, early, weight, bias, extra, tiles):
    height, levels, segments, _ = own.shape
    rows = levels * height * segments // tiles
    full = pl.BlockSpec(memory_space=pltpu.VMEM)
    shape = lambda more: jax.ShapeDtypeStruct((rows + more, SL), BF16)
    return pl.pallas_call(
        finish_kernel,
        in_specs=[pl.BlockSpec(memory_space=pltpu.SMEM)] + [full] * 7,
        out_specs=[full] * tiles,
        out_shape=[shape(PACK)] * (tiles // 2) + [shape(0)] * (tiles // 2),
        scratch_shapes=[pltpu.VMEM((tiles, rows, SL), BF16)],
        compiler_params=params(),
        cost_estimate=cost(1000, 1000),
    )(ids, own, cross, early, weight, bias, *extra)


def bucket_kernel(ids_ref, rows_ref, owner_ref, cells_ref, *rest):
    out_refs, held = rest[:-1], rest[-1]
    count = rows_ref.shape[1]
    tiles, _, cap = held.shape
    owner, cells = owner_ref[...], cells_ref[...]
    row = lax.broadcasted_iota(jnp.int32, (count, count), 0)
    column = lax.broadcasted_iota(jnp.int32, (count, count), 1)
    before = (row < column).astype(BF16)
    named = (lax.broadcasted_iota(jnp.int32, (tiles, count), 0) == owner).astype(F32)
    rank = jnp.dot(named.astype(BF16), before, preferred_element_type=F32)
    rank = jnp.sum(rank * named, axis=0, keepdims=True).astype(jnp.int32)
    slot = owner * cap + rank
    chosen = lax.broadcasted_iota(jnp.int32, (tiles * cap, count), 0) == slot
    coarse = (cells // HALF).astype(F32)
    fine = (cells % HALF).astype(F32)
    index = lax.broadcasted_iota(jnp.int32, (PACK - C, count), 0)
    places = jnp.where(index == 0, coarse, jnp.where(index == 1, fine, 0.0)).astype(BF16)
    payload = jnp.concatenate([rows_ref[...], places], axis=0)
    out = lax.dot_general(
        payload, chosen.astype(BF16), NT, preferred_element_type=F32
    ).astype(BF16)
    if cap % HALF == 0:
        for t in range(tiles):
            held[t] = out[:, t * cap : (t + 1) * cap]
    else:
        held[...] = jnp.swapaxes(out.reshape(PACK, tiles, cap), 0, 1)
    size = tiles // len(out_refs)
    for n, out_ref in enumerate(out_refs):
        out_ref[...] = held[pl.ds((ids_ref[0] // size ^ n) * size, size)]


def bucket(ids, exhaust, owner, cells, tiles):
    count = exhaust.shape[0]
    cap = 2 * count // tiles
    full = pl.BlockSpec(memory_space=pltpu.VMEM)
    return pl.pallas_call(
        bucket_kernel,
        in_specs=[pl.BlockSpec(memory_space=pltpu.SMEM)] + [full] * 3,
        out_specs=[full],
        out_shape=[jax.ShapeDtypeStruct((tiles, PACK, cap), BF16)],
        scratch_shapes=[pltpu.VMEM((tiles, PACK, cap), BF16)],
        compiler_params=params(),
        cost_estimate=cost(1000, 1000),
    )(ids, exhaust.T, owner.reshape(1, count), cells.reshape(1, count))


def source_kernel(tiles, rows, ids_ref, *refs):
    got_refs, out_ref = refs[:-1], refs[-1]
    places = out_ref.shape[0]
    groups = places // (QUAD * rows)
    got = jnp.concatenate([ref[ref.shape[0] - PACK :] for ref in got_refs], axis=1)
    slots = got.shape[1]
    cells = (got[C : C + 1].astype(F32) * HALF + got[C + 1 : C + 2].astype(F32)).astype(jnp.int32)
    x, row, level = cells % SEG, cells // SEG % rows, cells // (SEG * rows)
    group = turned_index(ids_ref, tiles, level // QUAD, groups)
    place = (group * QUAD + x // 2) * rows + row
    within = level % QUAD * 2 + x % 2
    lane = lax.broadcasted_iota(jnp.int32, (SL, slots), 0) // C
    spread = jnp.where(lane == within, jnp.concatenate([got[:C]] * SEG, axis=0).astype(F32), 0.0)
    index = lax.broadcasted_iota(jnp.int32, (places, slots), 0)
    chosen = (index == place).astype(BF16)
    out_ref[...] = lax.dot_general(chosen, spread.astype(BF16), NT, preferred_element_type=F32)


def make_source(ids, got, places, rows, tiles):
    full = pl.BlockSpec(memory_space=pltpu.VMEM)
    return pl.pallas_call(
        functools.partial(source_kernel, tiles, rows),
        in_specs=[pl.BlockSpec(memory_space=pltpu.SMEM)] + [full] * len(got),
        out_specs=full,
        out_shape=jax.ShapeDtypeStruct((places, SL), F32),
        compiler_params=params(),
        cost_estimate=cost(1000, 1000),
    )(ids, *got)


def prepare_kernel(ids_ref, depth_ref, point_ref, rows_ref, owner_ref, cells_ref, *rest):
    across_ref, close_ref, far_ref, held = rest
    bucket_kernel(ids_ref, rows_ref, owner_ref, cells_ref, close_ref, far_ref, held)
    across_kernel(depth_ref, point_ref, across_ref)


def prepare(ids, depth_kernel, point_weight, exhaust, owner, cells, tiles):
    count = exhaust.shape[0]
    cap = 2 * count // tiles
    full = pl.BlockSpec(memory_space=pltpu.VMEM)
    block = jax.ShapeDtypeStruct((tiles // 2, PACK, cap), BF16)
    return pl.pallas_call(
        prepare_kernel,
        in_specs=[pl.BlockSpec(memory_space=pltpu.SMEM)] + [full] * 5,
        out_specs=[full] * 3,
        out_shape=[jax.ShapeDtypeStruct(((KH + 1 + 2 * PAD) * 3 * HALF, SL), BF16), block, block],
        scratch_shapes=[pltpu.VMEM((tiles, PACK, cap), BF16)],
        compiler_params=params(),
        cost_estimate=cost(1000, 1000),
    )(
        ids,
        depth_kernel,
        point_weight,
        exhaust.T,
        owner.reshape(1, count),
        cells.reshape(1, count),
    )


def chunks(first, last, size):
    return [(n, min(n + size, last)) for n in range(first, last, size)]


def layer_step(held, base, first, last, block, weight, bias):
    taps = [held[(first - base + k) * block : (last - base + k) * block] for k in range(TAPS)]
    total = jnp.dot(jnp.concatenate(taps, axis=1), weight, preferred_element_type=F32)
    center = held[(first - base + 1) * block : (last - base + 1) * block].astype(F32)
    return center + gelu(total + bias)


def put_groups(out_ref, value, height, block, place_of):
    rows = block // QUAD
    across = rows // height
    count = max(1, 256 // block)
    size = QUAD * height
    swap = swap_matrix(count * size, across)
    for g in range(0, value.shape[0] // block, count):
        pieces = []
        for n in range(g, g + count):
            tile = lambda q, t: value[
                n * block + q * rows : n * block + (q + 1) * rows, t * HALF : (t + 1) * HALF
            ]
            for t in range(2):
                sides = [swap_halves(tile(2 * h, t), tile(2 * h + 1, t)) for h in range(2)]
                for level in range(2):
                    pieces.append(jnp.concatenate([side[level] for side in sides], axis=1))
        turned = jnp.dot(
            swap, jnp.concatenate(pieces, axis=0).astype(BF16), preferred_element_type=F32
        ).astype(BF16)
        for n in range(count):
            at = place_of(g + n) * QUAD
            for s in range(across):
                start = (s * count + n) * size
                out_ref[pl.ds(at, QUAD), :, s * SL : (s + 1) * SL] = turned[
                    start : start + size
                ].reshape(QUAD, height, SL)


def lane_biases(bias_ref):
    rows = [bias_row(bias_ref[n : n + 1]) for n in range(2)]
    return [jnp.concatenate([row, row], axis=1) for row in rows]


def place_pieces(tiles, ids_ref, piece_refs, held, first, block):
    for d, piece_ref in enumerate(piece_refs):
        at = turned_index(ids_ref, tiles, ids_ref[0] % tiles ^ d, tiles) + first
        held[pl.ds(pl.multiple_of(at * block, block), block)] = piece_ref[:block]


def near_kernel(tiles, height, ids_ref, *refs):
    piece_refs = refs[:tiles]
    source_ref, weight_ref, bias_ref, out_ref, kept_ref, later_ref, held, step = refs[tiles:]
    groups = out_ref.shape[0] // QUAD + 2
    block = kept_ref.shape[0] // 2
    bias = lane_biases(bias_ref)
    held[:block] = jnp.zeros((block, SL), BF16)
    step[:block] = jnp.zeros((block, SL), BF16)
    place_pieces(tiles, ids_ref, piece_refs, held, 1, block)
    kept_ref[...] = held[(groups - 1) * block : (groups + 1) * block]
    for first, last in chunks(0, groups - 1, 2):
        value = layer_step(held, 0, first, last, block, weight_ref[0], bias[0])
        step[(first + 1) * block : (last + 1) * block] = value.astype(BF16)
    later_ref[...] = step[(groups - 2) * block : groups * block]
    for first, last in chunks(0, groups - 2, 2):
        value = layer_step(step, 0, first, last, block, weight_ref[1], bias[1])
        value = value + source_ref[first * block : last * block]
        put_groups(
            out_ref,
            value,
            height,
            block,
            lambda n: turned_index(ids_ref, tiles, first + n, groups - 2),
        )


def far_kernel(tiles, height, ids_ref, *refs):
    piece_refs = refs[:tiles]
    early_ref, kept_ref, later_ref, source_ref, weight_ref, bias_ref = refs[tiles : tiles + 6]
    out_ref, held, step, result, sems = refs[tiles + 6 :]
    groups = out_ref.shape[0] // QUAD
    half = groups // 2
    block = kept_ref.shape[0] // 2
    early = early_ref.shape[0]
    at = turned_index(ids_ref, tiles, 0, groups * QUAD // early) * early
    copies = [pltpu.make_async_copy(early_ref, out_ref.at[pl.ds(at, early)], sems.at[groups])]
    copies[0].start()
    bias = lane_biases(bias_ref)
    held[: 2 * block] = kept_ref[...]
    held[(half + 2) * block :] = jnp.zeros((block, SL), BF16)
    step[: 2 * block] = later_ref[...]
    step[(half + 3) * block :] = jnp.zeros((block, SL), BF16)
    place_pieces(tiles, ids_ref, piece_refs, held, 2, block)
    for first, last in chunks(half - 1, groups, 3):
        value = layer_step(held, half - 1, first, last, block, weight_ref[0], bias[0])
        step[(first - half + 3) * block : (last - half + 3) * block] = value.astype(BF16)
    for first, last in chunks(half - 2, groups, 2):
        value = layer_step(step, half - 2, first, last, block, weight_ref[1], bias[1])
        value = value + source_ref[first * block : last * block]
        place_of = lambda n: turned_index(ids_ref, tiles, first + n, groups)
        put_groups(result, value, height, block, place_of)
        for n in range(last - first):
            span = pl.ds(place_of(n) * QUAD, QUAD)
            copies.append(
                pltpu.make_async_copy(result.at[span], out_ref.at[span], sems.at[first + n])
            )
            copies[-1].start()
    for copy in copies:
        copy.wait()


def whole_kernel(height, ids_ref, piece_ref, source_ref, weight_ref, bias_ref, out_ref, held, step):
    levels = out_ref.shape[0]
    groups = levels // QUAD
    rows = piece_ref.shape[0] // levels
    block = QUAD * rows
    bias = lane_biases(bias_ref)
    for buffer in (held, step):
        buffer[:block] = jnp.zeros((block, SL), BF16)
        buffer[(groups + 1) * block :] = jnp.zeros((block, SL), BF16)
    for group in range(groups):
        for h in range(2):
            values = []
            for z in range(group * QUAD, (group + 1) * QUAD):
                tile = piece_ref[z * rows : (z + 1) * rows, h * HALF : (h + 1) * HALF]
                values.append(tile.astype(F32))
            for n, lanes in enumerate(level_lanes(values)):
                at = (group + 1) * block + (2 * h + n) * rows
                held[at : at + rows] = lanes.astype(BF16)
    value = layer_step(held, 0, 0, groups, block, weight_ref[0], bias[0])
    step[block : (groups + 1) * block] = value.astype(BF16)
    value = layer_step(step, 0, 0, groups, block, weight_ref[1], bias[1])
    put_groups(out_ref, value + source_ref[...], height, block, lambda n: n)


def vertical(ids, close, far, source, weight, bias, levels, height, tiles):
    full = pl.BlockSpec(memory_space=pltpu.VMEM)
    smem = pl.BlockSpec(memory_space=pltpu.SMEM)
    rows = source.shape[0] // levels
    block = QUAD * rows
    groups = levels // QUAD
    lanes = rows // height * SL
    buffer = lambda count: pltpu.VMEM((count * block, SL), BF16)
    array = lambda count: jax.ShapeDtypeStruct((count * block, SL), BF16)
    result = lambda count: jax.ShapeDtypeStruct((count, height, lanes), BF16)
    if not far:
        return pl.pallas_call(
            functools.partial(whole_kernel, height),
            in_specs=[smem] + [full] * 4,
            out_specs=full,
            out_shape=result(levels),
            scratch_shapes=[buffer(groups + 2)] * 2,
            compiler_params=params(),
            cost_estimate=cost(1000, 1000),
        )(ids, *close, source, weight, bias)
    half = groups // 2
    early, kept, later = pl.pallas_call(
        functools.partial(near_kernel, tiles, height),
        in_specs=[smem] + [full] * (len(close) + 3),
        out_specs=[full] * 3,
        out_shape=[result(QUAD * (half - 2)), array(2), array(2)],
        scratch_shapes=[buffer(half + 1), buffer(half)],
        compiler_params=params(),
        cost_estimate=cost(1000, 1000),
    )(ids, *close, source, weight, bias)
    return pl.pallas_call(
        functools.partial(far_kernel, tiles, height),
        in_specs=[smem] + [full] * (len(far) + 6),
        out_specs=pl.BlockSpec(memory_space=pl.ANY),
        out_shape=result(levels),
        scratch_shapes=[
            buffer(half + 3),
            buffer(half + 4),
            pltpu.VMEM((levels, height, lanes), BF16),
            pltpu.SemaphoreType.DMA((groups + 1,)),
        ],
        compiler_params=params(),
        cost_estimate=cost(1000, 1000),
    )(ids, *far, early, kept, later, source, weight, bias)


def exchange(block, distance):
    count = lax.axis_size("cols")
    return lax.ppermute(block, "cols", [(i, i ^ distance) for i in range(count)])


def body(
    field, depth_kernel, point_weight, point_bias, vert_weight, vert_bias, exhaust, owner, cells
):
    columns, bands = lax.axis_size("cols"), lax.axis_size("rows")
    forward = [(i, i + 1) for i in range(bands - 1)]
    backward = [(target, source) for source, target in forward]
    levels, height, lanes = field.shape
    segments = lanes // SL
    per = segments // columns
    ids = jnp.stack([lax.axis_index("cols"), lax.axis_index("rows")]).astype(jnp.int32)
    bias = point_bias.reshape(1, C)
    if per % 16 == 0 and columns % 2 == 0 and bands % 2 == 0 and levels == QUAD and 256 % (levels * height) == 0:
        tiles = columns // 2
        own, cross, pair = to_segments(ids, field)
        inside = [(i, i ^ 1) for i in range(bands)]
        beyond = [(i, i + 1 if i % 2 else i - 1) for i in range(1, bands - 1)]
        cross = lax.ppermute(cross, "rows", beyond)
        pair = lax.ppermute(pair, "rows", inside)
        across, close_rows, far_rows = prepare(
            ids, depth_kernel, point_weight, exhaust, owner, cells, columns
        )
        relayed = exchange(far_rows, tiles)
        early = early_horizontal(ids, own, pair, across)
        pieces = finish_horizontal(
            ids, own, cross, early, across, bias, (close_rows, relayed), columns
        )
        pieces = [exchange(block, slot) if slot else block for slot, block in enumerate(pieces)]
        close, far = pieces[:tiles], pieces[tiles:]
        got = close
    else:
        tiles, far = 0, []
        (sent,) = bucket(ids, exhaust, owner, cells, columns)
        got = lax.all_to_all(sent, "cols", split_axis=0, concat_axis=0, tiled=True)
        got = [jnp.transpose(got, (1, 0, 2)).reshape(PACK, -1)]
        own = jnp.transpose(field.reshape(levels, height, segments, SL), (1, 0, 2, 3))
        low = lax.ppermute(own[height - 3 :], "rows", forward)
        high = lax.ppermute(own[:3], "rows", backward)
        across = across_weights(depth_kernel, point_weight)
        mixed = horizontal(own, low, high, across, bias, columns)
        mixed = mixed.reshape(columns, levels, -1, SL)
        taken = lax.all_to_all(mixed, "cols", split_axis=0, concat_axis=0, tiled=True)
        close = [taken.reshape(-1, SL)]
    depth = columns * levels
    source = make_source(ids, got, depth * height * per, height * per, tiles)
    up = up_weights(ids, vert_weight, tiles)
    return vertical(ids, close, far, source, up, vert_bias, depth, height, tiles)


def solution(mesh):
    placed = (
        P("cols", "rows", None),
        P(),
        P(),
        P(),
        P(),
        P(),
        P(("rows", "cols"), None),
        P(("rows", "cols"), None),
        P(("rows", "cols")),
    )
    return jax.shard_map(
        body, mesh=mesh, in_specs=placed, out_specs=P(None, "rows", "cols"), check_vma=False
    )
```

```python
import functools

import jax
import jax.numpy as jnp
from jax import lax
from jax.experimental import pallas as pl
from jax.experimental.pallas import tpu as pltpu
from jax.sharding import PartitionSpec as P

C = 32
KH = 7
KV = 9
SEG = 8
SL = SEG * C
PAD = 2
QUAD = 4
TAPS = 3
HALF = SL // 2
PACK = 48
VMEM = 20 * 1024 * 1024
NT = (((1,), (1,)), ((), ()))
F32 = jnp.float32
BF16 = jnp.bfloat16


def params():
    return pltpu.CompilerParams(vmem_limit_bytes=VMEM)


def cost(flops, moved):
    return pl.CostEstimate(flops=flops, bytes_accessed=moved, transcendentals=0)


def whole(shape):
    return pl.BlockSpec(shape, lambda *_: (0,) * len(shape))


def gelu(x):
    half = 0.5 * x
    return half + half * jnp.tanh(x * (0.7978845608028654 + 0.035677408136300125 * (x * x)))


def swap_matrix(outer, inner):
    size = outer * inner
    row = lax.broadcasted_iota(jnp.int32, (size, size), 0)
    column = lax.broadcasted_iota(jnp.int32, (size, size), 1)
    return (column == (row % outer) * inner + row // outer).astype(BF16)


def segment_kernel(ids_ref, field_ref, own_ref, cross_ref, pair_ref):
    levels, height, lanes = field_ref.shape
    rows = levels * height
    group = 256 // rows
    swap = swap_matrix(group, rows)
    for g in range(lanes // (group * SL)):
        at = [(g * group + s) * SL for s in range(group)]
        pieces = [field_ref[:, :, n : n + SL].reshape(rows, SL) for n in at]
        got = jnp.dot(
            swap, jnp.concatenate(pieces, axis=0), preferred_element_type=F32
        ).astype(BF16)
        for z in range(levels):
            for y in range(height):
                start = (z * height + y) * group
                own_ref[y, z, g * group : (g + 1) * group] = got[start : start + group]
    odd = ids_ref[1] % 2
    for y in range(3):
        cross_ref[y] = own_ref[odd * (height - 3) + y]
        pair_ref[y] = own_ref[(1 - odd) * (height - 3) + y]


def to_segments(ids, field):
    levels, height, lanes = field.shape
    full = pl.BlockSpec(memory_space=pltpu.VMEM)
    out = lambda n: jax.ShapeDtypeStruct((n, levels, lanes // SL, SL), BF16)
    return pl.pallas_call(
        segment_kernel,
        in_specs=[pl.BlockSpec(memory_space=pltpu.SMEM), full],
        out_specs=[full] * 3,
        out_shape=[out(height), out(3), out(3)],
        compiler_params=params(),
        cost_estimate=cost(2 * levels * height * lanes * 256, 8 * levels * height * lanes),
    )(ids, field)


def across_kernel(depth_ref, point_ref, out_ref):
    point = jnp.concatenate([point_ref[...].astype(F32)] * (HALF // C), axis=1)
    lane = lax.broadcasted_iota(jnp.int32, (C, HALF), 1) // C
    wide = 3 * HALF
    out_ref[...] = jnp.zeros_like(out_ref)
    for i in range(KH):
        columns = jnp.transpose(depth_ref[i])
        scaled = [point * columns[:, j : j + 1] for j in range(KH)]
        for xt in range(wide // C):
            block = jnp.zeros((C, HALF), F32)
            for xo in range(HALF // C):
                j = xt - 1 - xo
                if 0 <= j < KH:
                    block = jnp.where(lane == xo, scaled[j], block)
            block = block.astype(BF16)
            for yo in range(2):
                row = (i + yo + PAD) * wide + xt * C
                out_ref[row : row + C, yo * HALF : (yo + 1) * HALF] = block


def across_weights(depth_kernel, point_weight):
    return pl.pallas_call(
        across_kernel,
        out_shape=jax.ShapeDtypeStruct(((KH + 1 + 2 * PAD) * 3 * HALF, SL), BF16),
        compiler_params=params(),
        cost_estimate=cost(1000, 1000),
    )(depth_kernel, point_weight)


def up_kernel(tiles, ids_ref, vert_ref, out_ref):
    two = 2 * C
    row = lax.broadcasted_iota(jnp.int32, (KV * two, KV * C), 0)
    column = lax.broadcasted_iota(jnp.int32, (KV * two, KV * C), 1)
    spread = ((row // two == column // C) & (row % C == column % C)).astype(BF16)
    row = lax.broadcasted_iota(jnp.int32, (C, HALF), 0)
    column = lax.broadcasted_iota(jnp.int32, (C, HALF), 1)
    repeat = (row == column % C).astype(BF16)
    row = lax.broadcasted_iota(jnp.int32, (KV * two, HALF), 0)
    column = lax.broadcasted_iota(jnp.int32, (KV * two, HALF), 1)
    same = (row % two) // C == (column % two) // C
    low = lax.broadcasted_iota(jnp.int32, (two, HALF), 1) < two
    for layer in range(vert_ref.shape[0]):
        tall = lax.dot_general(spread, vert_ref[layer], NT, preferred_element_type=F32).astype(BF16)
        wide = jnp.dot(tall, repeat, preferred_element_type=F32)
        wide = jnp.where(same, wide, 0.0)
        tap = lambda k: wide[k * two : (k + 1) * two] if 0 <= k < KV else jnp.zeros((two, HALF), F32)
        for block in range(TAPS):
            at = pl.multiple_of(turned_index(ids_ref, tiles, block, TAPS) * SL, SL)
            rows = []
            for n in range(QUAD):
                zi = QUAD * block + n
                parts = [jnp.where(low, tap(zi - zo), tap(zi - zo - 1)) for zo in (0, 2)]
                rows.append(jnp.concatenate(parts, axis=1))
            out_ref[layer, pl.ds(at, SL)] = jnp.concatenate(rows, axis=0).astype(BF16)


def turned_index(ids_ref, tiles, index, count):
    if not tiles:
        return index
    return jnp.where(ids_ref[0] // tiles == 0, index, count - 1 - index)


def up_weights(ids, vert_weight, tiles):
    vert = jnp.transpose(vert_weight, (0, 2, 1))
    full = pl.BlockSpec(memory_space=pltpu.VMEM)
    return pl.pallas_call(
        functools.partial(up_kernel, tiles),
        in_specs=[pl.BlockSpec(memory_space=pltpu.SMEM), full],
        out_specs=full,
        out_shape=jax.ShapeDtypeStruct((vert.shape[0], TAPS * SL, SL), BF16),
        compiler_params=params(),
        cost_estimate=cost(1000, 1000),
    )(ids, vert)


def bias_row(row):
    return jnp.concatenate([row] * (HALF // C), axis=1)


def horizontal_kernel(own_ref, low_ref, high_ref, weight_ref, bias_ref, out_ref):
    height = own_ref.shape[0]
    segments = own_ref.shape[2]
    row = lax.broadcasted_iota(jnp.int32, (segments, HALF), 0)
    lines = [low_ref[y, 0] for y in range(3)]
    lines += [own_ref[y, 0] for y in range(height)]
    lines += [high_ref[y, 0] for y in range(3)]
    left, right = [], []
    for line in lines:
        a0, a1 = line[:, :HALF], line[:, HALF:]
        before = jnp.where(row == 0, 0.0, pltpu.roll(a1.astype(F32), 1, 0)).astype(BF16)
        after = jnp.where(
            row == segments - 1, 0.0, pltpu.roll(a0.astype(F32), segments - 1, 0)
        ).astype(BF16)
        left.append([before, a0, a1])
        right.append([a0, a1, after])
    stacked = []
    for yp in range(height // 2):
        for side in (left, right):
            stacked.append(
                jnp.concatenate(
                    [tile for y in range(2 * yp, 2 * yp + KH + 1) for tile in side[y]], axis=1
                )
            )
    wide = 3 * HALF
    total = jnp.dot(
        jnp.concatenate(stacked, axis=0),
        weight_ref[PAD * wide : (PAD + KH + 1) * wide],
        preferred_element_type=F32,
    )
    bias = bias_row(bias_ref[...])
    tiles, _, _, per, _ = out_ref.shape
    for yp in range(height // 2):
        for h in range(2):
            start = (yp * 2 + h) * segments
            for yo in range(2):
                y = 2 * yp + yo
                part = total[start : start + segments, yo * HALF : (yo + 1) * HALF]
                center = lines[y + 3][:, h * HALF : (h + 1) * HALF].astype(F32)
                value = (center + gelu(part + bias)).astype(BF16)
                out_ref[:, 0, y, :, h * HALF : (h + 1) * HALF] = value.reshape(tiles, per, HALF)


def horizontal(own, low, high, weight, bias, tiles):
    height, levels, segments, _ = own.shape
    direct = (segments // tiles) % 16 == 0
    parts = tiles if direct else 1
    per = segments // parts
    line = lambda n: pl.BlockSpec((n, 1, segments, SL), lambda z: (0, z, 0, 0))
    out = pl.pallas_call(
        horizontal_kernel,
        grid=(levels,),
        in_specs=[line(height), line(3), line(3), whole(weight.shape), whole(bias.shape)],
        out_specs=pl.BlockSpec((parts, 1, height, per, SL), lambda z: (0, z, 0, 0, 0)),
        out_shape=jax.ShapeDtypeStruct((parts, levels, height, per, SL), BF16),
        compiler_params=params(),
        cost_estimate=cost(
            2 * levels * height * segments * weight.shape[0] * SL // 2, 4 * 10**6
        ),
    )(own, low, high, weight, bias)
    if not direct:
        out = out.reshape(levels, height, tiles, segments // tiles, SL)
        out = jnp.transpose(out, (2, 0, 1, 3, 4))
    return out


def line_sides(line):
    count = line.shape[0]
    row = lax.broadcasted_iota(jnp.int32, (count, HALF), 0)
    a0, a1 = line[:, :HALF], line[:, HALF:]
    before = pltpu.roll(a1.astype(F32), 1, 0)
    before = jnp.where(row == 0, 0.0, before).astype(BF16)
    after = pltpu.roll(a0.astype(F32), count - 1, 0)
    after = jnp.where(row == count - 1, 0.0, after).astype(BF16)
    first, second = [before, a0, a1], [a0, a1, after]
    return jnp.concatenate(first, axis=1), jnp.concatenate(second, axis=1)


def halo_sums(lines, weight_ref, beyond, height):
    wide = 3 * HALF
    first = beyond * (height + 3)
    full = beyond * (height // 2 - 1)
    at = pl.multiple_of((first - 2 * full + PAD) * wide, wide)
    stacked = jnp.concatenate([jnp.concatenate(line, axis=1) for line in lines], axis=0)
    total = jnp.dot(stacked, weight_ref[pl.ds(at, 3 * wide)], preferred_element_type=F32)
    nearest = [jnp.where(beyond == 1, line[0], line[2]) for line in lines]
    thin = height // 2 - 1 - full
    at = pl.multiple_of((first + 2 * (1 - beyond) - 2 * thin + PAD) * wide, wide)
    less = jnp.dot(
        jnp.concatenate(nearest, axis=0), weight_ref[pl.ds(at, wide)], preferred_element_type=F32
    )
    return total, less


def early_kernel(ids_ref, own_ref, pair_ref, weight_ref, out_ref):
    height, levels, segments, _ = own_ref.shape
    wide = 3 * HALF
    own, pair = [], []
    for z in range(levels):
        sides = [line_sides(own_ref[y, z]) for y in range(height)]
        for h in range(2):
            own.append(jnp.concatenate([side[h] for side in sides], axis=1))
        sides = [line_sides(pair_ref[y, z]) for y in range(3)]
        pair += [[side[h] for side in sides] for h in range(2)]
    own = jnp.concatenate(own, axis=0)
    beyond = 1 - ids_ref[1] % 2
    sums = halo_sums(pair, weight_ref, beyond, height)
    for n, total in enumerate(sums):
        yp = beyond if n == 0 else 1 - beyond
        at = pl.multiple_of((3 - 2 * yp + PAD) * wide, wide)
        weight = weight_ref[pl.ds(at, height * wide)]
        total = total + jnp.dot(own, weight, preferred_element_type=F32)
        out_ref[yp] = total.reshape(levels, 2, segments, SL)


def early_horizontal(ids, own, pair, weight):
    height, levels, segments, _ = own.shape
    full = pl.BlockSpec(memory_space=pltpu.VMEM)
    return pl.pallas_call(
        early_kernel,
        in_specs=[pl.BlockSpec(memory_space=pltpu.SMEM)] + [full] * 3,
        out_specs=full,
        out_shape=jax.ShapeDtypeStruct((height // 2, levels, 2, segments, SL), F32),
        compiler_params=params(),
        cost_estimate=cost(1000, 1000),
    )(ids, own, pair, weight)


def swap_halves(first, second):
    low = lax.broadcasted_iota(jnp.int32, first.shape, 1) < HALF // 2
    lower = jnp.where(low, first, pltpu.roll(second, HALF // 2, 1))
    upper = jnp.where(low, pltpu.roll(first, HALF // 2, 1), second)
    return lower, upper


def level_lanes(values):
    sides = [swap_halves(values[n], values[n + 1]) for n in (0, 2)]
    return [jnp.concatenate([side[n] for side in sides], axis=1) for n in range(2)]


def finish_kernel(ids_ref, own_ref, cross_ref, early_ref, weight_ref, bias_ref, *rest):
    extra_refs, out_refs, done = rest[:2], rest[2:-1], rest[-1]
    height, levels, segments, _ = own_ref.shape
    tiles = len(out_refs)
    per = segments // tiles
    bias = bias_row(bias_ref[...])
    cross = []
    for z in range(levels):
        sides = [line_sides(cross_ref[y, z]) for y in range(3)]
        cross += [[side[h] for side in sides] for h in range(2)]
    beyond = ids_ref[1] % 2
    sums = halo_sums(cross, weight_ref, beyond, height)
    for yn, total in enumerate(sums):
        yp = beyond if yn == 0 else 1 - beyond
        for h in range(2):
            for yo in range(2):
                y = 2 * yp + yo
                lane = slice(yo * HALF, (yo + 1) * HALF)
                values = []
                for z in range(levels):
                    row = (z * 2 + h) * segments
                    part = total[row : row + segments, lane] + early_ref[yp, z, h, :, lane]
                    center = own_ref[y, z, :, h * HALF : (h + 1) * HALF]
                    values.append(center.astype(F32) + gelu(part + bias))
                for n, lanes in enumerate(level_lanes(values)):
                    at = pl.multiple_of(((2 * h + n) * height + y) * per, per)
                    done[:, pl.ds(at, per)] = lanes.astype(BF16).reshape(tiles, per, SL)
    rows = levels * height * per
    for slot, out_ref in enumerate(out_refs):
        tile = ids_ref[0] ^ slot
        out_ref[:rows] = done[tile]
        if slot < tiles // 2:
            for n, extra_ref in enumerate(extra_refs):
                out_ref[rows:, n * HALF : (n + 1) * HALF] = extra_ref[tile % (tiles // 2)]


def finish_horizontal(ids, own, cross, early, weight, bias, extra, tiles):
    height, levels, segments, _ = own.shape
    rows = levels * height * segments // tiles
    full = pl.BlockSpec(memory_space=pltpu.VMEM)
    shape = lambda more: jax.ShapeDtypeStruct((rows + more, SL), BF16)
    return pl.pallas_call(
        finish_kernel,
        in_specs=[pl.BlockSpec(memory_space=pltpu.SMEM)] + [full] * 7,
        out_specs=[full] * tiles,
        out_shape=[shape(PACK)] * (tiles // 2) + [shape(0)] * (tiles // 2),
        scratch_shapes=[pltpu.VMEM((tiles, rows, SL), BF16)],
        compiler_params=params(),
        cost_estimate=cost(1000, 1000),
    )(ids, own, cross, early, weight, bias, *extra)


def bucket_kernel(ids_ref, rows_ref, owner_ref, cells_ref, *rest):
    out_refs, held = rest[:-1], rest[-1]
    count = rows_ref.shape[1]
    tiles, _, cap = held.shape
    owner, cells = owner_ref[...], cells_ref[...]
    row = lax.broadcasted_iota(jnp.int32, (count, count), 0)
    column = lax.broadcasted_iota(jnp.int32, (count, count), 1)
    before = (row < column).astype(BF16)
    named = (lax.broadcasted_iota(jnp.int32, (tiles, count), 0) == owner).astype(F32)
    rank = jnp.dot(named.astype(BF16), before, preferred_element_type=F32)
    rank = jnp.sum(rank * named, axis=0, keepdims=True).astype(jnp.int32)
    slot = owner * cap + rank
    chosen = lax.broadcasted_iota(jnp.int32, (tiles * cap, count), 0) == slot
    coarse = (cells // HALF).astype(F32)
    fine = (cells % HALF).astype(F32)
    index = lax.broadcasted_iota(jnp.int32, (PACK - C, count), 0)
    places = jnp.where(index == 0, coarse, jnp.where(index == 1, fine, 0.0)).astype(BF16)
    payload = jnp.concatenate([rows_ref[...], places], axis=0)
    out = lax.dot_general(
        payload, chosen.astype(BF16), NT, preferred_element_type=F32
    ).astype(BF16)
    if cap % HALF == 0:
        for t in range(tiles):
            held[t] = out[:, t * cap : (t + 1) * cap]
    else:
        held[...] = jnp.swapaxes(out.reshape(PACK, tiles, cap), 0, 1)
    size = tiles // len(out_refs)
    for n, out_ref in enumerate(out_refs):
        out_ref[...] = held[pl.ds((ids_ref[0] // size ^ n) * size, size)]


def bucket(ids, exhaust, owner, cells, tiles):
    count = exhaust.shape[0]
    cap = 2 * count // tiles
    full = pl.BlockSpec(memory_space=pltpu.VMEM)
    return pl.pallas_call(
        bucket_kernel,
        in_specs=[pl.BlockSpec(memory_space=pltpu.SMEM)] + [full] * 3,
        out_specs=[full],
        out_shape=[jax.ShapeDtypeStruct((tiles, PACK, cap), BF16)],
        scratch_shapes=[pltpu.VMEM((tiles, PACK, cap), BF16)],
        compiler_params=params(),
        cost_estimate=cost(1000, 1000),
    )(ids, exhaust.T, owner.reshape(1, count), cells.reshape(1, count))


def source_kernel(tiles, rows, ids_ref, *refs):
    got_refs, out_ref = refs[:-1], refs[-1]
    places = out_ref.shape[0]
    groups = places // (QUAD * rows)
    got = jnp.concatenate([ref[ref.shape[0] - PACK :] for ref in got_refs], axis=1)
    slots = got.shape[1]
    cells = (got[C : C + 1].astype(F32) * HALF + got[C + 1 : C + 2].astype(F32)).astype(jnp.int32)
    x, row, level = cells % SEG, cells // SEG % rows, cells // (SEG * rows)
    group = turned_index(ids_ref, tiles, level // QUAD, groups)
    place = (group * QUAD + x // 2) * rows + row
    within = level % QUAD * 2 + x % 2
    lane = lax.broadcasted_iota(jnp.int32, (SL, slots), 0) // C
    spread = jnp.where(lane == within, jnp.concatenate([got[:C]] * SEG, axis=0).astype(F32), 0.0)
    index = lax.broadcasted_iota(jnp.int32, (places, slots), 0)
    chosen = (index == place).astype(BF16)
    out_ref[...] = lax.dot_general(chosen, spread.astype(BF16), NT, preferred_element_type=F32)


def make_source(ids, got, places, rows, tiles):
    full = pl.BlockSpec(memory_space=pltpu.VMEM)
    return pl.pallas_call(
        functools.partial(source_kernel, tiles, rows),
        in_specs=[pl.BlockSpec(memory_space=pltpu.SMEM)] + [full] * len(got),
        out_specs=full,
        out_shape=jax.ShapeDtypeStruct((places, SL), F32),
        compiler_params=params(),
        cost_estimate=cost(1000, 1000),
    )(ids, *got)


def prepare_kernel(ids_ref, depth_ref, point_ref, rows_ref, owner_ref, cells_ref, *rest):
    across_ref, close_ref, far_ref, held = rest
    bucket_kernel(ids_ref, rows_ref, owner_ref, cells_ref, close_ref, far_ref, held)
    across_kernel(depth_ref, point_ref, across_ref)


def prepare(ids, depth_kernel, point_weight, exhaust, owner, cells, tiles):
    count = exhaust.shape[0]
    cap = 2 * count // tiles
    full = pl.BlockSpec(memory_space=pltpu.VMEM)
    block = jax.ShapeDtypeStruct((tiles // 2, PACK, cap), BF16)
    return pl.pallas_call(
        prepare_kernel,
        in_specs=[pl.BlockSpec(memory_space=pltpu.SMEM)] + [full] * 5,
        out_specs=[full] * 3,
        out_shape=[jax.ShapeDtypeStruct(((KH + 1 + 2 * PAD) * 3 * HALF, SL), BF16), block, block],
        scratch_shapes=[pltpu.VMEM((tiles, PACK, cap), BF16)],
        compiler_params=params(),
        cost_estimate=cost(1000, 1000),
    )(
        ids,
        depth_kernel,
        point_weight,
        exhaust.T,
        owner.reshape(1, count),
        cells.reshape(1, count),
    )


def chunks(first, last, size):
    return [(n, min(n + size, last)) for n in range(first, last, size)]


def layer_step(held, base, first, last, block, weight, bias):
    taps = [held[(first - base + k) * block : (last - base + k) * block] for k in range(TAPS)]
    total = jnp.dot(jnp.concatenate(taps, axis=1), weight, preferred_element_type=F32)
    rows = block // QUAD
    start = (first - base + 1) * block
    for n in range(0, (last - first) * block, rows):
        center = held[start + n : start + n + rows].astype(F32)
        yield n, center + gelu(total[n : n + rows] + bias)


def layer_store(out, at, values):
    for n, value in values:
        out[at + n : at + n + value.shape[0]] = value.astype(BF16)


def tile_matrix(height, across):
    size = 2 * height * across
    row = lax.broadcasted_iota(jnp.int32, (size, size), 0)
    column = lax.broadcasted_iota(jnp.int32, (size, size), 1)
    tile = row // height % 4
    segment = row // (4 * height) * 2 + tile // 2
    wanted = (tile % 2 * height + row % height) * across + segment
    return (column == wanted).astype(BF16)


def put_groups(out_ref, values, source_ref, first, height, block, place_of):
    rows = block // QUAD
    turn = tile_matrix(height, rows // height)
    parts, halves = [], [[], []]
    for n, value in values:
        value = value + source_ref[first * block + n : first * block + n + rows]
        parts.append([value[:, :HALF], value[:, HALF:]])
        if len(parts) == QUAD:
            for h in range(2):
                for t in range(2):
                    pair = swap_halves(parts[2 * h][t], parts[2 * h + 1][t])
                    halves[h] += [one.astype(BF16) for one in pair]
            parts = []
    stacked = jnp.concatenate([jnp.concatenate(half, axis=1) for half in halves], axis=0)
    turned = jnp.dot(turn, stacked, preferred_element_type=F32).astype(BF16)
    for n in range(len(halves[0]) // QUAD):
        at = place_of(n) * QUAD
        for z in range(QUAD):
            lane = (n * QUAD + z) * HALF
            out_ref[at + z] = turned[:, lane : lane + HALF].reshape(out_ref.shape[1:])


def lane_biases(bias_ref):
    rows = [bias_row(bias_ref[n : n + 1]) for n in range(2)]
    return [jnp.concatenate([row, row], axis=1) for row in rows]


def place_pieces(tiles, ids_ref, piece_refs, held, first, block):
    for d, piece_ref in enumerate(piece_refs):
        at = turned_index(ids_ref, tiles, ids_ref[0] % tiles ^ d, tiles) + first
        held[pl.ds(pl.multiple_of(at * block, block), block)] = piece_ref[:block]


def near_kernel(tiles, height, ids_ref, *refs):
    piece_refs = refs[:tiles]
    source_ref, weight_ref, bias_ref, out_ref, kept_ref, later_ref, held, step = refs[tiles:]
    groups = out_ref.shape[0] // QUAD + 2
    block = kept_ref.shape[0] // 2
    bias = lane_biases(bias_ref)
    held[:block] = jnp.zeros((block, SL), BF16)
    step[:block] = jnp.zeros((block, SL), BF16)
    place_pieces(tiles, ids_ref, piece_refs, held, 1, block)
    kept_ref[...] = held[(groups - 1) * block : (groups + 1) * block]
    for first, last in chunks(0, groups - 1, 2):
        values = layer_step(held, 0, first, last, block, weight_ref[0], bias[0])
        layer_store(step, (first + 1) * block, values)
    later_ref[...] = step[(groups - 2) * block : groups * block]
    for first, last in chunks(0, groups - 2, 2):
        values = layer_step(step, 0, first, last, block, weight_ref[1], bias[1])
        place_of = lambda n: turned_index(ids_ref, tiles, first + n, groups - 2)
        put_groups(out_ref, values, source_ref, first, height, block, place_of)


def far_kernel(tiles, height, ids_ref, *refs):
    piece_refs = refs[:tiles]
    early_ref, kept_ref, later_ref, source_ref, weight_ref, bias_ref = refs[tiles : tiles + 6]
    out_ref, held, step, result, sems = refs[tiles + 6 :]
    groups = out_ref.shape[0] // QUAD
    half = groups // 2
    block = kept_ref.shape[0] // 2
    early = early_ref.shape[0]
    at = turned_index(ids_ref, tiles, 0, groups * QUAD // early) * early
    copies = [pltpu.make_async_copy(early_ref, out_ref.at[pl.ds(at, early)], sems.at[groups])]
    copies[0].start()
    bias = lane_biases(bias_ref)
    held[: 2 * block] = kept_ref[...]
    held[(half + 2) * block :] = jnp.zeros((block, SL), BF16)
    step[: 2 * block] = later_ref[...]
    step[(half + 3) * block :] = jnp.zeros((block, SL), BF16)
    place_pieces(tiles, ids_ref, piece_refs, held, 2, block)
    for first, last in chunks(half - 1, groups, 3):
        values = layer_step(held, half - 1, first, last, block, weight_ref[0], bias[0])
        layer_store(step, (first - half + 3) * block, values)
    for first, last in chunks(half - 2, groups, 2):
        values = layer_step(step, half - 2, first, last, block, weight_ref[1], bias[1])
        place_of = lambda n: turned_index(ids_ref, tiles, first + n, groups)
        put_groups(result, values, source_ref, first, height, block, place_of)
        for n in range(last - first):
            span = pl.ds(place_of(n) * QUAD, QUAD)
            copies.append(
                pltpu.make_async_copy(result.at[span], out_ref.at[span], sems.at[first + n])
            )
            copies[-1].start()
    for copy in copies:
        copy.wait()


def whole_kernel(height, ids_ref, piece_ref, source_ref, weight_ref, bias_ref, out_ref, held, step):
    levels = out_ref.shape[0]
    groups = levels // QUAD
    rows = piece_ref.shape[0] // levels
    block = QUAD * rows
    bias = lane_biases(bias_ref)
    for buffer in (held, step):
        buffer[:block] = jnp.zeros((block, SL), BF16)
        buffer[(groups + 1) * block :] = jnp.zeros((block, SL), BF16)
    for group in range(groups):
        for h in range(2):
            values = []
            for z in range(group * QUAD, (group + 1) * QUAD):
                tile = piece_ref[z * rows : (z + 1) * rows, h * HALF : (h + 1) * HALF]
                values.append(tile.astype(F32))
            for n, lanes in enumerate(level_lanes(values)):
                at = (group + 1) * block + (2 * h + n) * rows
                held[at : at + rows] = lanes.astype(BF16)
    layer_store(step, block, layer_step(held, 0, 0, groups, block, weight_ref[0], bias[0]))
    values = layer_step(step, 0, 0, groups, block, weight_ref[1], bias[1])
    put_groups(out_ref, values, source_ref, 0, height, block, lambda n: n)


def in_order(out, height):
    levels, blocks, rows, lanes = out.shape
    out = out.reshape(levels, blocks, rows // height, height, lanes)
    return jnp.transpose(out, (0, 3, 1, 2, 4)).reshape(levels, height, -1)


def vertical(ids, close, far, source, weight, bias, levels, height, tiles):
    full = pl.BlockSpec(memory_space=pltpu.VMEM)
    smem = pl.BlockSpec(memory_space=pltpu.SMEM)
    rows = source.shape[0] // levels
    block = QUAD * rows
    groups = levels // QUAD
    lanes = rows // height * SL
    buffer = lambda count: pltpu.VMEM((count * block, SL), BF16)
    array = lambda count: jax.ShapeDtypeStruct((count * block, SL), BF16)
    kind = (lanes // (4 * HALF), 4 * height, HALF)
    result = lambda count: jax.ShapeDtypeStruct((count, *kind), BF16)
    if not far:
        out = pl.pallas_call(
            functools.partial(whole_kernel, height),
            in_specs=[smem] + [full] * 4,
            out_specs=full,
            out_shape=result(levels),
            scratch_shapes=[buffer(groups + 2)] * 2,
            compiler_params=params(),
            cost_estimate=cost(1000, 1000),
        )(ids, *close, source, weight, bias)
        return in_order(out, height)
    half = groups // 2
    early, kept, later = pl.pallas_call(
        functools.partial(near_kernel, tiles, height),
        in_specs=[smem] + [full] * (len(close) + 3),
        out_specs=[full] * 3,
        out_shape=[result(QUAD * (half - 2)), array(2), array(2)],
        scratch_shapes=[buffer(half + 1), buffer(half)],
        compiler_params=params(),
        cost_estimate=cost(1000, 1000),
    )(ids, *close, source, weight, bias)
    out = pl.pallas_call(
        functools.partial(far_kernel, tiles, height),
        in_specs=[smem] + [full] * (len(far) + 6),
        out_specs=pl.BlockSpec(memory_space=pl.ANY),
        out_shape=result(levels),
        scratch_shapes=[
            buffer(half + 3),
            buffer(half + 4),
            pltpu.VMEM((levels, *kind), BF16),
            pltpu.SemaphoreType.DMA((groups + 1,)),
        ],
        compiler_params=params(),
        cost_estimate=cost(1000, 1000),
    )(ids, *far, early, kept, later, source, weight, bias)
    return in_order(out, height)


def exchange(block, distance):
    count = lax.axis_size("cols")
    return lax.ppermute(block, "cols", [(i, i ^ distance) for i in range(count)])


def body(
    field, depth_kernel, point_weight, point_bias, vert_weight, vert_bias, exhaust, owner, cells
):
    columns, bands = lax.axis_size("cols"), lax.axis_size("rows")
    forward = [(i, i + 1) for i in range(bands - 1)]
    backward = [(target, source) for source, target in forward]
    levels, height, lanes = field.shape
    segments = lanes // SL
    per = segments // columns
    ids = jnp.stack([lax.axis_index("cols"), lax.axis_index("rows")]).astype(jnp.int32)
    bias = point_bias.reshape(1, C)
    if per % 16 == 0 and columns % 2 == 0 and bands % 2 == 0 and levels == QUAD and 256 % (levels * height) == 0:
        tiles = columns // 2
        own, cross, pair = to_segments(ids, field)
        inside = [(i, i ^ 1) for i in range(bands)]
        beyond = [(i, i + 1 if i % 2 else i - 1) for i in range(1, bands - 1)]
        cross = lax.ppermute(cross, "rows", beyond)
        pair = lax.ppermute(pair, "rows", inside)
        across, close_rows, far_rows = prepare(
            ids, depth_kernel, point_weight, exhaust, owner, cells, columns
        )
        relayed = exchange(far_rows, tiles)
        early = early_horizontal(ids, own, pair, across)
        pieces = finish_horizontal(
            ids, own, cross, early, across, bias, (close_rows, relayed), columns
        )
        pieces = [exchange(block, slot) if slot else block for slot, block in enumerate(pieces)]
        close, far = pieces[:tiles], pieces[tiles:]
        got = close
    else:
        tiles, far = 0, []
        (sent,) = bucket(ids, exhaust, owner, cells, columns)
        got = lax.all_to_all(sent, "cols", split_axis=0, concat_axis=0, tiled=True)
        got = [jnp.transpose(got, (1, 0, 2)).reshape(PACK, -1)]
        own = jnp.transpose(field.reshape(levels, height, segments, SL), (1, 0, 2, 3))
        low = lax.ppermute(own[height - 3 :], "rows", forward)
        high = lax.ppermute(own[:3], "rows", backward)
        across = across_weights(depth_kernel, point_weight)
        mixed = horizontal(own, low, high, across, bias, columns)
        mixed = mixed.reshape(columns, levels, -1, SL)
        taken = lax.all_to_all(mixed, "cols", split_axis=0, concat_axis=0, tiled=True)
        close = [taken.reshape(-1, SL)]
    depth = columns * levels
    source = make_source(ids, got, depth * height * per, height * per, tiles)
    up = up_weights(ids, vert_weight, tiles)
    return vertical(ids, close, far, source, up, vert_bias, depth, height, tiles)


def solution(mesh):
    placed = (
        P("cols", "rows", None),
        P(),
        P(),
        P(),
        P(),
        P(),
        P(("rows", "cols"), None),
        P(("rows", "cols"), None),
        P(("rows", "cols")),
    )
    return jax.shard_map(
        body, mesh=mesh, in_specs=placed, out_specs=P(None, "rows", "cols"), check_vma=False
    )
```

```python
import functools

import jax
import jax.numpy as jnp
from jax import lax
from jax.experimental import pallas as pl
from jax.experimental.pallas import tpu as pltpu
from jax.sharding import PartitionSpec as P

C = 32
KH = 7
KV = 9
SEG = 8
SL = SEG * C
PAD = 2
QUAD = 4
TAPS = 3
HALF = SL // 2
PACK = 48
VMEM = 20 * 1024 * 1024
NT = (((1,), (1,)), ((), ()))
F32 = jnp.float32
BF16 = jnp.bfloat16


def params():
    return pltpu.CompilerParams(vmem_limit_bytes=VMEM)


def cost(flops, moved):
    return pl.CostEstimate(flops=flops, bytes_accessed=moved, transcendentals=0)


def whole(shape):
    return pl.BlockSpec(shape, lambda *_: (0,) * len(shape))


def gelu(x):
    half = 0.5 * x
    return half + half * jnp.tanh(x * (0.7978845608028654 + 0.035677408136300125 * (x * x)))


def swap_matrix(outer, inner):
    size = outer * inner
    row = lax.broadcasted_iota(jnp.int32, (size, size), 0)
    column = lax.broadcasted_iota(jnp.int32, (size, size), 1)
    return (column == (row % outer) * inner + row // outer).astype(BF16)


def segment_kernel(only_cross, ids_ref, field_ref, own_ref, halo_ref):
    if only_cross:
        own_ref, halo_ref = halo_ref, own_ref
    levels, height, lanes = field_ref.shape
    rows = levels * height
    group = 256 // rows
    swap = swap_matrix(group, rows)
    for g in range(lanes // (group * SL)):
        at = [(g * group + s) * SL for s in range(group)]
        pieces = [field_ref[:, :, n : n + SL].reshape(rows, SL) for n in at]
        got = jnp.dot(
            swap, jnp.concatenate(pieces, axis=0), preferred_element_type=F32
        ).astype(BF16)
        for z in range(levels):
            for y in range(height):
                start = (z * height + y) * group
                own_ref[y, z, g * group : (g + 1) * group] = got[start : start + group]
    odd = ids_ref[1] % 2
    first = odd if only_cross else 1 - odd
    for y in range(3):
        halo_ref[y] = own_ref[first * (height - 3) + y]


def to_segments(ids, field, only_cross):
    levels, height, lanes = field.shape
    full = pl.BlockSpec(memory_space=pltpu.VMEM)
    shape = lambda n: (n, levels, lanes // SL, SL)
    out = lambda n: jax.ShapeDtypeStruct(shape(n), BF16)
    return pl.pallas_call(
        functools.partial(segment_kernel, only_cross),
        in_specs=[pl.BlockSpec(memory_space=pltpu.SMEM), full],
        out_specs=[full] if only_cross else [full] * 2,
        out_shape=[out(3)] if only_cross else [out(height), out(3)],
        scratch_shapes=[pltpu.VMEM(shape(height), BF16)] if only_cross else [],
        compiler_params=params(),
        cost_estimate=cost(1000, 1000),
    )(ids, field)


def across_kernel(depth_ref, point_ref, out_ref):
    point = jnp.concatenate([point_ref[...].astype(F32)] * (HALF // C), axis=1)
    lane = lax.broadcasted_iota(jnp.int32, (C, HALF), 1) // C
    wide = 3 * HALF
    out_ref[...] = jnp.zeros_like(out_ref)
    for i in range(KH):
        columns = jnp.transpose(depth_ref[i])
        scaled = [point * columns[:, j : j + 1] for j in range(KH)]
        for xt in range(wide // C):
            block = jnp.zeros((C, HALF), F32)
            for xo in range(HALF // C):
                j = xt - 1 - xo
                if 0 <= j < KH:
                    block = jnp.where(lane == xo, scaled[j], block)
            block = block.astype(BF16)
            for yo in range(2):
                row = (i + yo + PAD) * wide + xt * C
                out_ref[row : row + C, yo * HALF : (yo + 1) * HALF] = block


def across_weights(depth_kernel, point_weight):
    return pl.pallas_call(
        across_kernel,
        out_shape=jax.ShapeDtypeStruct(((KH + 1 + 2 * PAD) * 3 * HALF, SL), BF16),
        compiler_params=params(),
        cost_estimate=cost(1000, 1000),
    )(depth_kernel, point_weight)


def up_kernel(tiles, ids_ref, vert_ref, out_ref):
    two = 2 * C
    row = lax.broadcasted_iota(jnp.int32, (KV * two, KV * C), 0)
    column = lax.broadcasted_iota(jnp.int32, (KV * two, KV * C), 1)
    spread = ((row // two == column // C) & (row % C == column % C)).astype(BF16)
    row = lax.broadcasted_iota(jnp.int32, (C, HALF), 0)
    column = lax.broadcasted_iota(jnp.int32, (C, HALF), 1)
    repeat = (row == column % C).astype(BF16)
    row = lax.broadcasted_iota(jnp.int32, (KV * two, HALF), 0)
    column = lax.broadcasted_iota(jnp.int32, (KV * two, HALF), 1)
    same = (row % two) // C == (column % two) // C
    low = lax.broadcasted_iota(jnp.int32, (two, HALF), 1) < two
    for layer in range(vert_ref.shape[0]):
        tall = lax.dot_general(spread, vert_ref[layer], NT, preferred_element_type=F32).astype(BF16)
        wide = jnp.dot(tall, repeat, preferred_element_type=F32)
        wide = jnp.where(same, wide, 0.0)
        tap = lambda k: wide[k * two : (k + 1) * two] if 0 <= k < KV else jnp.zeros((two, HALF), F32)
        for block in range(TAPS):
            at = pl.multiple_of(turned_index(ids_ref, tiles, block, TAPS) * SL, SL)
            rows = []
            for n in range(QUAD):
                zi = QUAD * block + n
                parts = [jnp.where(low, tap(zi - zo), tap(zi - zo - 1)) for zo in (0, 2)]
                rows.append(jnp.concatenate(parts, axis=1))
            out_ref[layer, pl.ds(at, SL)] = jnp.concatenate(rows, axis=0).astype(BF16)


def turned_index(ids_ref, tiles, index, count):
    if not tiles:
        return index
    return jnp.where(ids_ref[0] // tiles == 0, index, count - 1 - index)


def up_weights(ids, vert_weight, tiles):
    vert = jnp.transpose(vert_weight, (0, 2, 1))
    full = pl.BlockSpec(memory_space=pltpu.VMEM)
    return pl.pallas_call(
        functools.partial(up_kernel, tiles),
        in_specs=[pl.BlockSpec(memory_space=pltpu.SMEM), full],
        out_specs=full,
        out_shape=jax.ShapeDtypeStruct((vert.shape[0], TAPS * SL, SL), BF16),
        compiler_params=params(),
        cost_estimate=cost(1000, 1000),
    )(ids, vert)


def bias_row(row):
    return jnp.concatenate([row] * (HALF // C), axis=1)


def horizontal_kernel(own_ref, low_ref, high_ref, weight_ref, bias_ref, out_ref):
    height = own_ref.shape[0]
    segments = own_ref.shape[2]
    row = lax.broadcasted_iota(jnp.int32, (segments, HALF), 0)
    lines = [low_ref[y, 0] for y in range(3)]
    lines += [own_ref[y, 0] for y in range(height)]
    lines += [high_ref[y, 0] for y in range(3)]
    left, right = [], []
    for line in lines:
        a0, a1 = line[:, :HALF], line[:, HALF:]
        before = jnp.where(row == 0, 0.0, pltpu.roll(a1.astype(F32), 1, 0)).astype(BF16)
        after = jnp.where(
            row == segments - 1, 0.0, pltpu.roll(a0.astype(F32), segments - 1, 0)
        ).astype(BF16)
        left.append([before, a0, a1])
        right.append([a0, a1, after])
    stacked = []
    for yp in range(height // 2):
        for side in (left, right):
            stacked.append(
                jnp.concatenate(
                    [tile for y in range(2 * yp, 2 * yp + KH + 1) for tile in side[y]], axis=1
                )
            )
    wide = 3 * HALF
    total = jnp.dot(
        jnp.concatenate(stacked, axis=0),
        weight_ref[PAD * wide : (PAD + KH + 1) * wide],
        preferred_element_type=F32,
    )
    bias = bias_row(bias_ref[...])
    tiles, _, _, per, _ = out_ref.shape
    for yp in range(height // 2):
        for h in range(2):
            start = (yp * 2 + h) * segments
            for yo in range(2):
                y = 2 * yp + yo
                part = total[start : start + segments, yo * HALF : (yo + 1) * HALF]
                center = lines[y + 3][:, h * HALF : (h + 1) * HALF].astype(F32)
                value = (center + gelu(part + bias)).astype(BF16)
                out_ref[:, 0, y, :, h * HALF : (h + 1) * HALF] = value.reshape(tiles, per, HALF)


def horizontal(own, low, high, weight, bias, tiles):
    height, levels, segments, _ = own.shape
    direct = (segments // tiles) % 16 == 0
    parts = tiles if direct else 1
    per = segments // parts
    line = lambda n: pl.BlockSpec((n, 1, segments, SL), lambda z: (0, z, 0, 0))
    out = pl.pallas_call(
        horizontal_kernel,
        grid=(levels,),
        in_specs=[line(height), line(3), line(3), whole(weight.shape), whole(bias.shape)],
        out_specs=pl.BlockSpec((parts, 1, height, per, SL), lambda z: (0, z, 0, 0, 0)),
        out_shape=jax.ShapeDtypeStruct((parts, levels, height, per, SL), BF16),
        compiler_params=params(),
        cost_estimate=cost(
            2 * levels * height * segments * weight.shape[0] * SL // 2, 4 * 10**6
        ),
    )(own, low, high, weight, bias)
    if not direct:
        out = out.reshape(levels, height, tiles, segments // tiles, SL)
        out = jnp.transpose(out, (2, 0, 1, 3, 4))
    return out


def line_sides(line):
    count = line.shape[0]
    row = lax.broadcasted_iota(jnp.int32, (count, HALF), 0)
    a0, a1 = line[:, :HALF], line[:, HALF:]
    before = pltpu.roll(a1.astype(F32), 1, 0)
    before = jnp.where(row == 0, 0.0, before).astype(BF16)
    after = pltpu.roll(a0.astype(F32), count - 1, 0)
    after = jnp.where(row == count - 1, 0.0, after).astype(BF16)
    first, second = [before, a0, a1], [a0, a1, after]
    return jnp.concatenate(first, axis=1), jnp.concatenate(second, axis=1)


def halo_sums(lines, weight_ref, beyond, height):
    wide = 3 * HALF
    first = beyond * (height + 3)
    full = beyond * (height // 2 - 1)
    at = pl.multiple_of((first - 2 * full + PAD) * wide, wide)
    stacked = jnp.concatenate([jnp.concatenate(line, axis=1) for line in lines], axis=0)
    total = jnp.dot(stacked, weight_ref[pl.ds(at, 3 * wide)], preferred_element_type=F32)
    nearest = [jnp.where(beyond == 1, line[0], line[2]) for line in lines]
    thin = height // 2 - 1 - full
    at = pl.multiple_of((first + 2 * (1 - beyond) - 2 * thin + PAD) * wide, wide)
    less = jnp.dot(
        jnp.concatenate(nearest, axis=0), weight_ref[pl.ds(at, wide)], preferred_element_type=F32
    )
    return total, less


def early_kernel(ids_ref, own_ref, pair_ref, weight_ref, out_ref):
    height, levels, segments, _ = own_ref.shape
    wide = 3 * HALF
    own, pair = [], []
    for z in range(levels):
        sides = [line_sides(own_ref[y, z]) for y in range(height)]
        for h in range(2):
            own.append(jnp.concatenate([side[h] for side in sides], axis=1))
        sides = [line_sides(pair_ref[y, z]) for y in range(3)]
        pair += [[side[h] for side in sides] for h in range(2)]
    own = jnp.concatenate(own, axis=0)
    beyond = 1 - ids_ref[1] % 2
    sums = halo_sums(pair, weight_ref, beyond, height)
    for n, total in enumerate(sums):
        yp = beyond if n == 0 else 1 - beyond
        at = pl.multiple_of((3 - 2 * yp + PAD) * wide, wide)
        weight = weight_ref[pl.ds(at, height * wide)]
        total = total + jnp.dot(own, weight, preferred_element_type=F32)
        out_ref[yp] = total.reshape(levels, 2, segments, SL)


def early_horizontal(ids, own, pair, weight):
    height, levels, segments, _ = own.shape
    full = pl.BlockSpec(memory_space=pltpu.VMEM)
    return pl.pallas_call(
        early_kernel,
        in_specs=[pl.BlockSpec(memory_space=pltpu.SMEM)] + [full] * 3,
        out_specs=full,
        out_shape=jax.ShapeDtypeStruct((height // 2, levels, 2, segments, SL), F32),
        compiler_params=params(),
        cost_estimate=cost(1000, 1000),
    )(ids, own, pair, weight)


def swap_halves(first, second):
    low = lax.broadcasted_iota(jnp.int32, first.shape, 1) < HALF // 2
    lower = jnp.where(low, first, pltpu.roll(second, HALF // 2, 1))
    upper = jnp.where(low, pltpu.roll(first, HALF // 2, 1), second)
    return lower, upper


def level_lanes(values):
    sides = [swap_halves(values[n], values[n + 1]) for n in (0, 2)]
    return [jnp.concatenate([side[n] for side in sides], axis=1) for n in range(2)]


def finish_kernel(ids_ref, own_ref, cross_ref, early_ref, weight_ref, bias_ref, *rest):
    extra_refs, out_refs, done = rest[:2], rest[2:-1], rest[-1]
    height, levels, segments, _ = own_ref.shape
    tiles = len(out_refs)
    per = segments // tiles
    bias = bias_row(bias_ref[...])
    cross = []
    for z in range(levels):
        sides = [line_sides(cross_ref[y, z]) for y in range(3)]
        cross += [[side[h] for side in sides] for h in range(2)]
    beyond = ids_ref[1] % 2
    sums = halo_sums(cross, weight_ref, beyond, height)
    for yn, total in enumerate(sums):
        yp = beyond if yn == 0 else 1 - beyond
        for h in range(2):
            for yo in range(2):
                y = 2 * yp + yo
                lane = slice(yo * HALF, (yo + 1) * HALF)
                values = []
                for z in range(levels):
                    row = (z * 2 + h) * segments
                    part = total[row : row + segments, lane] + early_ref[yp, z, h, :, lane]
                    center = own_ref[y, z, :, h * HALF : (h + 1) * HALF]
                    values.append(center.astype(F32) + gelu(part + bias))
                for n, lanes in enumerate(level_lanes(values)):
                    at = pl.multiple_of(((2 * h + n) * height + y) * per, per)
                    done[:, pl.ds(at, per)] = lanes.astype(BF16).reshape(tiles, per, SL)
    rows = levels * height * per
    for slot, out_ref in enumerate(out_refs):
        tile = ids_ref[0] ^ slot
        out_ref[:rows] = done[tile]
        if slot < tiles // 2:
            for n, extra_ref in enumerate(extra_refs):
                out_ref[rows:, n * HALF : (n + 1) * HALF] = extra_ref[tile % (tiles // 2)]


def finish_horizontal(ids, own, cross, early, weight, bias, extra, tiles):
    height, levels, segments, _ = own.shape
    rows = levels * height * segments // tiles
    full = pl.BlockSpec(memory_space=pltpu.VMEM)
    shape = lambda more: jax.ShapeDtypeStruct((rows + more, SL), BF16)
    return pl.pallas_call(
        finish_kernel,
        in_specs=[pl.BlockSpec(memory_space=pltpu.SMEM)] + [full] * 7,
        out_specs=[full] * tiles,
        out_shape=[shape(PACK)] * (tiles // 2) + [shape(0)] * (tiles // 2),
        scratch_shapes=[pltpu.VMEM((tiles, rows, SL), BF16)],
        compiler_params=params(),
        cost_estimate=cost(1000, 1000),
    )(ids, own, cross, early, weight, bias, *extra)


def bucket_kernel(ids_ref, rows_ref, owner_ref, cells_ref, *rest):
    out_refs, held = rest[:-1], rest[-1]
    count = rows_ref.shape[1]
    tiles, _, cap = held.shape
    owner, cells = owner_ref[...], cells_ref[...]
    row = lax.broadcasted_iota(jnp.int32, (count, count), 0)
    column = lax.broadcasted_iota(jnp.int32, (count, count), 1)
    before = (row < column).astype(BF16)
    named = (lax.broadcasted_iota(jnp.int32, (tiles, count), 0) == owner).astype(F32)
    rank = jnp.dot(named.astype(BF16), before, preferred_element_type=F32)
    rank = jnp.sum(rank * named, axis=0, keepdims=True).astype(jnp.int32)
    slot = owner * cap + rank
    chosen = lax.broadcasted_iota(jnp.int32, (tiles * cap, count), 0) == slot
    coarse = (cells // HALF).astype(F32)
    fine = (cells % HALF).astype(F32)
    index = lax.broadcasted_iota(jnp.int32, (PACK - C, count), 0)
    places = jnp.where(index == 0, coarse, jnp.where(index == 1, fine, 0.0)).astype(BF16)
    payload = jnp.concatenate([rows_ref[...], places], axis=0)
    out = lax.dot_general(
        payload, chosen.astype(BF16), NT, preferred_element_type=F32
    ).astype(BF16)
    if cap % HALF == 0:
        for t in range(tiles):
            held[t] = out[:, t * cap : (t + 1) * cap]
    else:
        held[...] = jnp.swapaxes(out.reshape(PACK, tiles, cap), 0, 1)
    size = tiles // len(out_refs)
    for n, out_ref in enumerate(out_refs):
        out_ref[...] = held[pl.ds((ids_ref[0] // size ^ n) * size, size)]


def bucket(ids, exhaust, owner, cells, tiles):
    count = exhaust.shape[0]
    cap = 2 * count // tiles
    full = pl.BlockSpec(memory_space=pltpu.VMEM)
    return pl.pallas_call(
        bucket_kernel,
        in_specs=[pl.BlockSpec(memory_space=pltpu.SMEM)] + [full] * 3,
        out_specs=[full],
        out_shape=[jax.ShapeDtypeStruct((tiles, PACK, cap), BF16)],
        scratch_shapes=[pltpu.VMEM((tiles, PACK, cap), BF16)],
        compiler_params=params(),
        cost_estimate=cost(1000, 1000),
    )(ids, exhaust.T, owner.reshape(1, count), cells.reshape(1, count))


def source_kernel(tiles, rows, ids_ref, *refs):
    got_refs, out_ref = refs[:-1], refs[-1]
    places = out_ref.shape[0]
    groups = places // (QUAD * rows)
    got = jnp.concatenate([ref[ref.shape[0] - PACK :] for ref in got_refs], axis=1)
    slots = got.shape[1]
    cells = (got[C : C + 1].astype(F32) * HALF + got[C + 1 : C + 2].astype(F32)).astype(jnp.int32)
    x, row, level = cells % SEG, cells // SEG % rows, cells // (SEG * rows)
    group = turned_index(ids_ref, tiles, level // QUAD, groups)
    place = (group * QUAD + x // 2) * rows + row
    within = level % QUAD * 2 + x % 2
    lane = lax.broadcasted_iota(jnp.int32, (SL, slots), 0) // C
    spread = jnp.where(lane == within, jnp.concatenate([got[:C]] * SEG, axis=0).astype(F32), 0.0)
    index = lax.broadcasted_iota(jnp.int32, (places, slots), 0)
    chosen = (index == place).astype(BF16)
    out_ref[...] = lax.dot_general(chosen, spread.astype(BF16), NT, preferred_element_type=F32)


def make_source(ids, got, places, rows, tiles):
    full = pl.BlockSpec(memory_space=pltpu.VMEM)
    return pl.pallas_call(
        functools.partial(source_kernel, tiles, rows),
        in_specs=[pl.BlockSpec(memory_space=pltpu.SMEM)] + [full] * len(got),
        out_specs=full,
        out_shape=jax.ShapeDtypeStruct((places, SL), F32),
        compiler_params=params(),
        cost_estimate=cost(1000, 1000),
    )(ids, *got)


def prepare_kernel(ids_ref, depth_ref, point_ref, rows_ref, owner_ref, cells_ref, *rest):
    across_ref, close_ref, far_ref, held = rest
    bucket_kernel(ids_ref, rows_ref, owner_ref, cells_ref, close_ref, far_ref, held)
    across_kernel(depth_ref, point_ref, across_ref)


def prepare(ids, depth_kernel, point_weight, exhaust, owner, cells, tiles):
    count = exhaust.shape[0]
    cap = 2 * count // tiles
    full = pl.BlockSpec(memory_space=pltpu.VMEM)
    block = jax.ShapeDtypeStruct((tiles // 2, PACK, cap), BF16)
    return pl.pallas_call(
        prepare_kernel,
        in_specs=[pl.BlockSpec(memory_space=pltpu.SMEM)] + [full] * 5,
        out_specs=[full] * 3,
        out_shape=[jax.ShapeDtypeStruct(((KH + 1 + 2 * PAD) * 3 * HALF, SL), BF16), block, block],
        scratch_shapes=[pltpu.VMEM((tiles, PACK, cap), BF16)],
        compiler_params=params(),
        cost_estimate=cost(1000, 1000),
    )(
        ids,
        depth_kernel,
        point_weight,
        exhaust.T,
        owner.reshape(1, count),
        cells.reshape(1, count),
    )


def chunks(first, last, size):
    return [(n, min(n + size, last)) for n in range(first, last, size)]


def layer_step(held, base, first, last, block, weight, bias):
    taps = [held[(first - base + k) * block : (last - base + k) * block] for k in range(TAPS)]
    total = jnp.dot(jnp.concatenate(taps, axis=1), weight, preferred_element_type=F32)
    rows = block // QUAD
    start = (first - base + 1) * block
    for n in range(0, (last - first) * block, rows):
        center = held[start + n : start + n + rows].astype(F32)
        yield n, center + gelu(total[n : n + rows] + bias)


def layer_store(out, at, values):
    for n, value in values:
        out[at + n : at + n + value.shape[0]] = value.astype(BF16)


def tile_matrix(height, across):
    size = 2 * height * across
    row = lax.broadcasted_iota(jnp.int32, (size, size), 0)
    column = lax.broadcasted_iota(jnp.int32, (size, size), 1)
    tile = row // height % 4
    segment = row // (4 * height) * 2 + tile // 2
    wanted = (tile % 2 * height + row % height) * across + segment
    return (column == wanted).astype(BF16)


def put_groups(out_ref, values, source_ref, first, height, block, place_of):
    rows = block // QUAD
    turn = tile_matrix(height, rows // height)
    parts, halves = [], [[], []]
    for n, value in values:
        value = value + source_ref[first * block + n : first * block + n + rows]
        parts.append([value[:, :HALF], value[:, HALF:]])
        if len(parts) == QUAD:
            for h in range(2):
                for t in range(2):
                    pair = swap_halves(parts[2 * h][t], parts[2 * h + 1][t])
                    halves[h] += [one.astype(BF16) for one in pair]
            parts = []
    stacked = jnp.concatenate([jnp.concatenate(half, axis=1) for half in halves], axis=0)
    turned = jnp.dot(turn, stacked, preferred_element_type=F32).astype(BF16)
    for n in range(len(halves[0]) // QUAD):
        at = place_of(n) * QUAD
        for z in range(QUAD):
            lane = (n * QUAD + z) * HALF
            out_ref[at + z] = turned[:, lane : lane + HALF].reshape(out_ref.shape[1:])


def lane_biases(bias_ref):
    rows = [bias_row(bias_ref[n : n + 1]) for n in range(2)]
    return [jnp.concatenate([row, row], axis=1) for row in rows]


def place_pieces(tiles, ids_ref, piece_refs, held, first, block):
    for d, piece_ref in enumerate(piece_refs):
        at = turned_index(ids_ref, tiles, ids_ref[0] % tiles ^ d, tiles) + first
        held[pl.ds(pl.multiple_of(at * block, block), block)] = piece_ref[:block]


def near_kernel(tiles, height, ids_ref, *refs):
    piece_refs = refs[:tiles]
    source_ref, weight_ref, bias_ref, out_ref, kept_ref, later_ref, held, step = refs[tiles:]
    groups = out_ref.shape[0] // QUAD + 2
    block = kept_ref.shape[0] // 2
    bias = lane_biases(bias_ref)
    held[:block] = jnp.zeros((block, SL), BF16)
    step[:block] = jnp.zeros((block, SL), BF16)
    place_pieces(tiles, ids_ref, piece_refs, held, 1, block)
    kept_ref[...] = held[(groups - 1) * block : (groups + 1) * block]
    for first, last in chunks(0, groups - 1, 2):
        values = layer_step(held, 0, first, last, block, weight_ref[0], bias[0])
        layer_store(step, (first + 1) * block, values)
    later_ref[...] = step[(groups - 2) * block : groups * block]
    for first, last in chunks(0, groups - 2, 2):
        values = layer_step(step, 0, first, last, block, weight_ref[1], bias[1])
        place_of = lambda n: turned_index(ids_ref, tiles, first + n, groups - 2)
        put_groups(out_ref, values, source_ref, first, height, block, place_of)


def far_kernel(tiles, height, ids_ref, *refs):
    piece_refs = refs[:tiles]
    early_ref, kept_ref, later_ref, source_ref, weight_ref, bias_ref = refs[tiles : tiles + 6]
    out_ref, held, step, result, sems = refs[tiles + 6 :]
    groups = out_ref.shape[0] // QUAD
    half = groups // 2
    block = kept_ref.shape[0] // 2
    early = early_ref.shape[0]
    at = turned_index(ids_ref, tiles, 0, groups * QUAD // early) * early
    copies = [pltpu.make_async_copy(early_ref, out_ref.at[pl.ds(at, early)], sems.at[groups])]
    copies[0].start()
    bias = lane_biases(bias_ref)
    held[: 2 * block] = kept_ref[...]
    held[(half + 2) * block :] = jnp.zeros((block, SL), BF16)
    step[: 2 * block] = later_ref[...]
    step[(half + 3) * block :] = jnp.zeros((block, SL), BF16)
    place_pieces(tiles, ids_ref, piece_refs, held, 2, block)
    for first, last in chunks(half - 1, groups, 3):
        values = layer_step(held, half - 1, first, last, block, weight_ref[0], bias[0])
        layer_store(step, (first - half + 3) * block, values)
    for first, last in chunks(half - 2, groups, 2):
        values = layer_step(step, half - 2, first, last, block, weight_ref[1], bias[1])
        place_of = lambda n: turned_index(ids_ref, tiles, first + n, groups)
        put_groups(result, values, source_ref, first, height, block, place_of)
        for n in range(last - first):
            span = pl.ds(place_of(n) * QUAD, QUAD)
            copies.append(
                pltpu.make_async_copy(result.at[span], out_ref.at[span], sems.at[first + n])
            )
            copies[-1].start()
    for copy in copies:
        copy.wait()


def whole_kernel(height, ids_ref, piece_ref, source_ref, weight_ref, bias_ref, out_ref, held, step):
    levels = out_ref.shape[0]
    groups = levels // QUAD
    rows = piece_ref.shape[0] // levels
    block = QUAD * rows
    bias = lane_biases(bias_ref)
    for buffer in (held, step):
        buffer[:block] = jnp.zeros((block, SL), BF16)
        buffer[(groups + 1) * block :] = jnp.zeros((block, SL), BF16)
    for group in range(groups):
        for h in range(2):
            values = []
            for z in range(group * QUAD, (group + 1) * QUAD):
                tile = piece_ref[z * rows : (z + 1) * rows, h * HALF : (h + 1) * HALF]
                values.append(tile.astype(F32))
            for n, lanes in enumerate(level_lanes(values)):
                at = (group + 1) * block + (2 * h + n) * rows
                held[at : at + rows] = lanes.astype(BF16)
    layer_store(step, block, layer_step(held, 0, 0, groups, block, weight_ref[0], bias[0]))
    values = layer_step(step, 0, 0, groups, block, weight_ref[1], bias[1])
    put_groups(out_ref, values, source_ref, 0, height, block, lambda n: n)


def in_order(out, height):
    levels, blocks, rows, lanes = out.shape
    out = out.reshape(levels, blocks, rows // height, height, lanes)
    return jnp.transpose(out, (0, 3, 1, 2, 4)).reshape(levels, height, -1)


def vertical(ids, close, far, source, weight, bias, levels, height, tiles):
    full = pl.BlockSpec(memory_space=pltpu.VMEM)
    smem = pl.BlockSpec(memory_space=pltpu.SMEM)
    rows = source.shape[0] // levels
    block = QUAD * rows
    groups = levels // QUAD
    lanes = rows // height * SL
    buffer = lambda count: pltpu.VMEM((count * block, SL), BF16)
    array = lambda count: jax.ShapeDtypeStruct((count * block, SL), BF16)
    kind = (lanes // (4 * HALF), 4 * height, HALF)
    result = lambda count: jax.ShapeDtypeStruct((count, *kind), BF16)
    if not far:
        out = pl.pallas_call(
            functools.partial(whole_kernel, height),
            in_specs=[smem] + [full] * 4,
            out_specs=full,
            out_shape=result(levels),
            scratch_shapes=[buffer(groups + 2)] * 2,
            compiler_params=params(),
            cost_estimate=cost(1000, 1000),
        )(ids, *close, source, weight, bias)
        return in_order(out, height)
    half = groups // 2
    early, kept, later = pl.pallas_call(
        functools.partial(near_kernel, tiles, height),
        in_specs=[smem] + [full] * (len(close) + 3),
        out_specs=[full] * 3,
        out_shape=[result(QUAD * (half - 2)), array(2), array(2)],
        scratch_shapes=[buffer(half + 1), buffer(half)],
        compiler_params=params(),
        cost_estimate=cost(1000, 1000),
    )(ids, *close, source, weight, bias)
    out = pl.pallas_call(
        functools.partial(far_kernel, tiles, height),
        in_specs=[smem] + [full] * (len(far) + 6),
        out_specs=pl.BlockSpec(memory_space=pl.ANY),
        out_shape=result(levels),
        scratch_shapes=[
            buffer(half + 3),
            buffer(half + 4),
            pltpu.VMEM((levels, *kind), BF16),
            pltpu.SemaphoreType.DMA((groups + 1,)),
        ],
        compiler_params=params(),
        cost_estimate=cost(1000, 1000),
    )(ids, *far, early, kept, later, source, weight, bias)
    return in_order(out, height)


def exchange(block, distance):
    count = lax.axis_size("cols")
    return lax.ppermute(block, "cols", [(i, i ^ distance) for i in range(count)])


def body(
    field, depth_kernel, point_weight, point_bias, vert_weight, vert_bias, exhaust, owner, cells
):
    columns, bands = lax.axis_size("cols"), lax.axis_size("rows")
    forward = [(i, i + 1) for i in range(bands - 1)]
    backward = [(target, source) for source, target in forward]
    levels, height, lanes = field.shape
    segments = lanes // SL
    per = segments // columns
    ids = jnp.stack([lax.axis_index("cols"), lax.axis_index("rows")]).astype(jnp.int32)
    bias = point_bias.reshape(1, C)
    if per % 16 == 0 and columns % 2 == 0 and bands % 2 == 0 and levels == QUAD and 256 % (levels * height) == 0:
        tiles = columns // 2
        (cross,) = to_segments(ids, field, True)
        ids_after, _ = lax.optimization_barrier((ids, cross))
        own, pair = to_segments(ids_after, field, False)
        inside = [(i, i ^ 1) for i in range(bands)]
        beyond = [(i, i + 1 if i % 2 else i - 1) for i in range(1, bands - 1)]
        cross = lax.ppermute(cross, "rows", beyond)
        pair = lax.ppermute(pair, "rows", inside)
        across, close_rows, far_rows = prepare(
            ids, depth_kernel, point_weight, exhaust, owner, cells, columns
        )
        relayed = exchange(far_rows, tiles)
        early = early_horizontal(ids, own, pair, across)
        pieces = finish_horizontal(
            ids, own, cross, early, across, bias, (close_rows, relayed), columns
        )
        pieces = [exchange(block, slot) if slot else block for slot, block in enumerate(pieces)]
        close, far = pieces[:tiles], pieces[tiles:]
        got = close
    else:
        tiles, far = 0, []
        (sent,) = bucket(ids, exhaust, owner, cells, columns)
        got = lax.all_to_all(sent, "cols", split_axis=0, concat_axis=0, tiled=True)
        got = [jnp.transpose(got, (1, 0, 2)).reshape(PACK, -1)]
        own = jnp.transpose(field.reshape(levels, height, segments, SL), (1, 0, 2, 3))
        low = lax.ppermute(own[height - 3 :], "rows", forward)
        high = lax.ppermute(own[:3], "rows", backward)
        across = across_weights(depth_kernel, point_weight)
        mixed = horizontal(own, low, high, across, bias, columns)
        mixed = mixed.reshape(columns, levels, -1, SL)
        taken = lax.all_to_all(mixed, "cols", split_axis=0, concat_axis=0, tiled=True)
        close = [taken.reshape(-1, SL)]
    depth = columns * levels
    source = make_source(ids, got, depth * height * per, height * per, tiles)
    up = up_weights(ids, vert_weight, tiles)
    return vertical(ids, close, far, source, up, vert_bias, depth, height, tiles)


def solution(mesh):
    placed = (
        P("cols", "rows", None),
        P(),
        P(),
        P(),
        P(),
        P(),
        P(("rows", "cols"), None),
        P(("rows", "cols"), None),
        P(("rows", "cols")),
    )
    return jax.shard_map(
        body, mesh=mesh, in_specs=placed, out_specs=P(None, "rows", "cols"), check_vma=False
    )
```

```python
import functools

import jax
import jax.numpy as jnp
from jax import lax
from jax.experimental import pallas as pl
from jax.experimental.pallas import tpu as pltpu
from jax.sharding import PartitionSpec as P

C = 32
KH = 7
KV = 9
SEG = 8
SL = SEG * C
PAD = 2
QUAD = 4
TAPS = 3
HALF = SL // 2
PACK = 48
VMEM = 20 * 1024 * 1024
NT = (((1,), (1,)), ((), ()))
F32 = jnp.float32
BF16 = jnp.bfloat16


def params():
    return pltpu.CompilerParams(vmem_limit_bytes=VMEM)


def cost(flops, moved):
    return pl.CostEstimate(flops=flops, bytes_accessed=moved, transcendentals=0)


def whole(shape):
    return pl.BlockSpec(shape, lambda *_: (0,) * len(shape))


def gelu(x):
    half = 0.5 * x
    return half + half * jnp.tanh(x * (0.7978845608028654 + 0.035677408136300125 * (x * x)))


def swap_matrix(outer, inner):
    size = outer * inner
    row = lax.broadcasted_iota(jnp.int32, (size, size), 0)
    column = lax.broadcasted_iota(jnp.int32, (size, size), 1)
    return (column == (row % outer) * inner + row // outer).astype(BF16)


def segment_kernel(only_cross, ids_ref, field_ref, *out_refs):
    levels, height, lanes = field_ref.shape
    rows = levels * height
    group = 256 // rows
    odd = ids_ref[1] % 2
    count = 3 if only_cross else height
    first = odd * (height - 3) if only_cross else 0
    row = lax.broadcasted_iota(jnp.int32, (count * levels * group, 256), 0)
    column = lax.broadcasted_iota(jnp.int32, (count * levels * group, 256), 1)
    line = row // group
    wanted = row % group * rows + line % levels * height + line // levels + first
    turn = (column == wanted).astype(BF16)
    for g in range(lanes // (group * SL)):
        at = [(g * group + s) * SL for s in range(group)]
        pieces = [field_ref[:, :, n : n + SL].reshape(rows, SL) for n in at]
        got = jnp.dot(
            turn, jnp.concatenate(pieces, axis=0), preferred_element_type=F32
        ).astype(BF16)
        out_refs[0][:, :, g * group : (g + 1) * group] = got.reshape(count, levels, group, SL)
    if not only_cross:
        for y in range(3):
            out_refs[1][y] = out_refs[0][(1 - odd) * (height - 3) + y]


def to_segments(ids, field, only_cross):
    levels, height, lanes = field.shape
    full = pl.BlockSpec(memory_space=pltpu.VMEM)
    shape = lambda n: (n, levels, lanes // SL, SL)
    out = lambda n: jax.ShapeDtypeStruct(shape(n), BF16)
    return pl.pallas_call(
        functools.partial(segment_kernel, only_cross),
        in_specs=[pl.BlockSpec(memory_space=pltpu.SMEM), full],
        out_specs=[full] if only_cross else [full] * 2,
        out_shape=[out(3)] if only_cross else [out(height), out(3)],
        compiler_params=params(),
        cost_estimate=cost(1000, 1000),
    )(ids, field)


def across_kernel(depth_ref, point_ref, out_ref):
    point = jnp.concatenate([point_ref[...].astype(F32)] * (HALF // C), axis=1)
    lane = lax.broadcasted_iota(jnp.int32, (C, HALF), 1) // C
    wide = 3 * HALF
    out_ref[...] = jnp.zeros_like(out_ref)
    for i in range(KH):
        columns = jnp.transpose(depth_ref[i])
        scaled = [point * columns[:, j : j + 1] for j in range(KH)]
        for xt in range(wide // C):
            block = jnp.zeros((C, HALF), F32)
            for xo in range(HALF // C):
                j = xt - 1 - xo
                if 0 <= j < KH:
                    block = jnp.where(lane == xo, scaled[j], block)
            block = block.astype(BF16)
            for yo in range(2):
                row = (i + yo + PAD) * wide + xt * C
                out_ref[row : row + C, yo * HALF : (yo + 1) * HALF] = block


def across_weights(depth_kernel, point_weight):
    return pl.pallas_call(
        across_kernel,
        out_shape=jax.ShapeDtypeStruct(((KH + 1 + 2 * PAD) * 3 * HALF, SL), BF16),
        compiler_params=params(),
        cost_estimate=cost(1000, 1000),
    )(depth_kernel, point_weight)


def up_kernel(tiles, ids_ref, vert_ref, out_ref):
    two = 2 * C
    row = lax.broadcasted_iota(jnp.int32, (KV * two, KV * C), 0)
    column = lax.broadcasted_iota(jnp.int32, (KV * two, KV * C), 1)
    spread = ((row // two == column // C) & (row % C == column % C)).astype(BF16)
    row = lax.broadcasted_iota(jnp.int32, (C, HALF), 0)
    column = lax.broadcasted_iota(jnp.int32, (C, HALF), 1)
    repeat = (row == column % C).astype(BF16)
    row = lax.broadcasted_iota(jnp.int32, (KV * two, HALF), 0)
    column = lax.broadcasted_iota(jnp.int32, (KV * two, HALF), 1)
    same = (row % two) // C == (column % two) // C
    low = lax.broadcasted_iota(jnp.int32, (two, HALF), 1) < two
    for layer in range(vert_ref.shape[0]):
        tall = lax.dot_general(spread, vert_ref[layer], NT, preferred_element_type=F32).astype(BF16)
        wide = jnp.dot(tall, repeat, preferred_element_type=F32)
        wide = jnp.where(same, wide, 0.0)
        tap = lambda k: wide[k * two : (k + 1) * two] if 0 <= k < KV else jnp.zeros((two, HALF), F32)
        for block in range(TAPS):
            at = pl.multiple_of(turned_index(ids_ref, tiles, block, TAPS) * SL, SL)
            rows = []
            for n in range(QUAD):
                zi = QUAD * block + n
                parts = [jnp.where(low, tap(zi - zo), tap(zi - zo - 1)) for zo in (0, 2)]
                rows.append(jnp.concatenate(parts, axis=1))
            out_ref[layer, pl.ds(at, SL)] = jnp.concatenate(rows, axis=0).astype(BF16)


def turned_index(ids_ref, tiles, index, count):
    if not tiles:
        return index
    return jnp.where(ids_ref[0] // tiles == 0, index, count - 1 - index)


def up_weights(ids, vert_weight, tiles):
    vert = jnp.transpose(vert_weight, (0, 2, 1))
    full = pl.BlockSpec(memory_space=pltpu.VMEM)
    return pl.pallas_call(
        functools.partial(up_kernel, tiles),
        in_specs=[pl.BlockSpec(memory_space=pltpu.SMEM), full],
        out_specs=full,
        out_shape=jax.ShapeDtypeStruct((vert.shape[0], TAPS * SL, SL), BF16),
        compiler_params=params(),
        cost_estimate=cost(1000, 1000),
    )(ids, vert)


def bias_row(row):
    return jnp.concatenate([row] * (HALF // C), axis=1)


def horizontal_kernel(own_ref, low_ref, high_ref, weight_ref, bias_ref, out_ref):
    height = own_ref.shape[0]
    segments = own_ref.shape[2]
    row = lax.broadcasted_iota(jnp.int32, (segments, HALF), 0)
    lines = [low_ref[y, 0] for y in range(3)]
    lines += [own_ref[y, 0] for y in range(height)]
    lines += [high_ref[y, 0] for y in range(3)]
    left, right = [], []
    for line in lines:
        a0, a1 = line[:, :HALF], line[:, HALF:]
        before = jnp.where(row == 0, 0.0, pltpu.roll(a1.astype(F32), 1, 0)).astype(BF16)
        after = jnp.where(
            row == segments - 1, 0.0, pltpu.roll(a0.astype(F32), segments - 1, 0)
        ).astype(BF16)
        left.append([before, a0, a1])
        right.append([a0, a1, after])
    stacked = []
    for yp in range(height // 2):
        for side in (left, right):
            stacked.append(
                jnp.concatenate(
                    [tile for y in range(2 * yp, 2 * yp + KH + 1) for tile in side[y]], axis=1
                )
            )
    wide = 3 * HALF
    total = jnp.dot(
        jnp.concatenate(stacked, axis=0),
        weight_ref[PAD * wide : (PAD + KH + 1) * wide],
        preferred_element_type=F32,
    )
    bias = bias_row(bias_ref[...])
    tiles, _, _, per, _ = out_ref.shape
    for yp in range(height // 2):
        for h in range(2):
            start = (yp * 2 + h) * segments
            for yo in range(2):
                y = 2 * yp + yo
                part = total[start : start + segments, yo * HALF : (yo + 1) * HALF]
                center = lines[y + 3][:, h * HALF : (h + 1) * HALF].astype(F32)
                value = (center + gelu(part + bias)).astype(BF16)
                out_ref[:, 0, y, :, h * HALF : (h + 1) * HALF] = value.reshape(tiles, per, HALF)


def horizontal(own, low, high, weight, bias, tiles):
    height, levels, segments, _ = own.shape
    direct = (segments // tiles) % 16 == 0
    parts = tiles if direct else 1
    per = segments // parts
    line = lambda n: pl.BlockSpec((n, 1, segments, SL), lambda z: (0, z, 0, 0))
    out = pl.pallas_call(
        horizontal_kernel,
        grid=(levels,),
        in_specs=[line(height), line(3), line(3), whole(weight.shape), whole(bias.shape)],
        out_specs=pl.BlockSpec((parts, 1, height, per, SL), lambda z: (0, z, 0, 0, 0)),
        out_shape=jax.ShapeDtypeStruct((parts, levels, height, per, SL), BF16),
        compiler_params=params(),
        cost_estimate=cost(
            2 * levels * height * segments * weight.shape[0] * SL // 2, 4 * 10**6
        ),
    )(own, low, high, weight, bias)
    if not direct:
        out = out.reshape(levels, height, tiles, segments // tiles, SL)
        out = jnp.transpose(out, (2, 0, 1, 3, 4))
    return out


def line_sides(line):
    count = line.shape[0]
    row = lax.broadcasted_iota(jnp.int32, (count, HALF), 0)
    a0, a1 = line[:, :HALF], line[:, HALF:]
    before = pltpu.roll(a1.astype(F32), 1, 0)
    before = jnp.where(row == 0, 0.0, before).astype(BF16)
    after = pltpu.roll(a0.astype(F32), count - 1, 0)
    after = jnp.where(row == count - 1, 0.0, after).astype(BF16)
    first, second = [before, a0, a1], [a0, a1, after]
    return jnp.concatenate(first, axis=1), jnp.concatenate(second, axis=1)


def halo_sums(lines, weight_ref, beyond, height):
    wide = 3 * HALF
    first = beyond * (height + 3)
    full = beyond * (height // 2 - 1)
    at = pl.multiple_of((first - 2 * full + PAD) * wide, wide)
    stacked = jnp.concatenate([jnp.concatenate(line, axis=1) for line in lines], axis=0)
    total = jnp.dot(stacked, weight_ref[pl.ds(at, 3 * wide)], preferred_element_type=F32)
    nearest = [jnp.where(beyond == 1, line[0], line[2]) for line in lines]
    thin = height // 2 - 1 - full
    at = pl.multiple_of((first + 2 * (1 - beyond) - 2 * thin + PAD) * wide, wide)
    less = jnp.dot(
        jnp.concatenate(nearest, axis=0), weight_ref[pl.ds(at, wide)], preferred_element_type=F32
    )
    return total, less


def early_kernel(ids_ref, own_ref, pair_ref, weight_ref, out_ref):
    height, levels, segments, _ = own_ref.shape
    wide = 3 * HALF
    own, pair = [], []
    for z in range(levels):
        sides = [line_sides(own_ref[y, z]) for y in range(height)]
        for h in range(2):
            own.append(jnp.concatenate([side[h] for side in sides], axis=1))
        sides = [line_sides(pair_ref[y, z]) for y in range(3)]
        pair += [[side[h] for side in sides] for h in range(2)]
    own = jnp.concatenate(own, axis=0)
    beyond = 1 - ids_ref[1] % 2
    sums = halo_sums(pair, weight_ref, beyond, height)
    for n, total in enumerate(sums):
        yp = beyond if n == 0 else 1 - beyond
        at = pl.multiple_of((3 - 2 * yp + PAD) * wide, wide)
        weight = weight_ref[pl.ds(at, height * wide)]
        total = total + jnp.dot(own, weight, preferred_element_type=F32)
        out_ref[yp] = total.reshape(levels, 2, segments, SL)


def early_horizontal(ids, own, pair, weight):
    height, levels, segments, _ = own.shape
    full = pl.BlockSpec(memory_space=pltpu.VMEM)
    return pl.pallas_call(
        early_kernel,
        in_specs=[pl.BlockSpec(memory_space=pltpu.SMEM)] + [full] * 3,
        out_specs=full,
        out_shape=jax.ShapeDtypeStruct((height // 2, levels, 2, segments, SL), F32),
        compiler_params=params(),
        cost_estimate=cost(1000, 1000),
    )(ids, own, pair, weight)


def swap_halves(first, second):
    low = lax.broadcasted_iota(jnp.int32, first.shape, 1) < HALF // 2
    lower = jnp.where(low, first, pltpu.roll(second, HALF // 2, 1))
    upper = jnp.where(low, pltpu.roll(first, HALF // 2, 1), second)
    return lower, upper


def level_lanes(values):
    sides = [swap_halves(values[n], values[n + 1]) for n in (0, 2)]
    return [jnp.concatenate([side[n] for side in sides], axis=1) for n in range(2)]


def finish_kernel(ids_ref, own_ref, cross_ref, early_ref, weight_ref, bias_ref, *rest):
    extra_refs, out_refs, done = rest[:2], rest[2:-1], rest[-1]
    height, levels, segments, _ = own_ref.shape
    tiles = len(out_refs)
    per = segments // tiles
    bias = bias_row(bias_ref[...])
    cross = []
    for z in range(levels):
        sides = [line_sides(cross_ref[y, z]) for y in range(3)]
        cross += [[side[h] for side in sides] for h in range(2)]
    beyond = ids_ref[1] % 2
    sums = halo_sums(cross, weight_ref, beyond, height)
    for yn, total in enumerate(sums):
        yp = beyond if yn == 0 else 1 - beyond
        for h in range(2):
            for yo in range(2):
                y = 2 * yp + yo
                lane = slice(yo * HALF, (yo + 1) * HALF)
                values = []
                for z in range(levels):
                    row = (z * 2 + h) * segments
                    part = total[row : row + segments, lane] + early_ref[yp, z, h, :, lane]
                    center = own_ref[y, z, :, h * HALF : (h + 1) * HALF]
                    values.append(center.astype(F32) + gelu(part + bias))
                for n, lanes in enumerate(level_lanes(values)):
                    at = pl.multiple_of(((2 * h + n) * height + y) * per, per)
                    done[:, pl.ds(at, per)] = lanes.astype(BF16).reshape(tiles, per, SL)
    rows = levels * height * per
    for slot, out_ref in enumerate(out_refs):
        tile = ids_ref[0] ^ slot
        out_ref[:rows] = done[tile]
        if slot < tiles // 2:
            for n, extra_ref in enumerate(extra_refs):
                out_ref[rows:, n * HALF : (n + 1) * HALF] = extra_ref[tile % (tiles // 2)]


def finish_horizontal(ids, own, cross, early, weight, bias, extra, tiles):
    height, levels, segments, _ = own.shape
    rows = levels * height * segments // tiles
    full = pl.BlockSpec(memory_space=pltpu.VMEM)
    shape = lambda more: jax.ShapeDtypeStruct((rows + more, SL), BF16)
    return pl.pallas_call(
        finish_kernel,
        in_specs=[pl.BlockSpec(memory_space=pltpu.SMEM)] + [full] * 7,
        out_specs=[full] * tiles,
        out_shape=[shape(PACK)] * (tiles // 2) + [shape(0)] * (tiles // 2),
        scratch_shapes=[pltpu.VMEM((tiles, rows, SL), BF16)],
        compiler_params=params(),
        cost_estimate=cost(1000, 1000),
    )(ids, own, cross, early, weight, bias, *extra)


def bucket_kernel(ids_ref, rows_ref, owner_ref, cells_ref, *rest):
    out_refs, held = rest[:-1], rest[-1]
    count = rows_ref.shape[1]
    tiles, _, cap = held.shape
    owner, cells = owner_ref[...], cells_ref[...]
    row = lax.broadcasted_iota(jnp.int32, (count, count), 0)
    column = lax.broadcasted_iota(jnp.int32, (count, count), 1)
    before = (row < column).astype(BF16)
    named = (lax.broadcasted_iota(jnp.int32, (tiles, count), 0) == owner).astype(F32)
    rank = jnp.dot(named.astype(BF16), before, preferred_element_type=F32)
    rank = jnp.sum(rank * named, axis=0, keepdims=True).astype(jnp.int32)
    slot = owner * cap + rank
    chosen = lax.broadcasted_iota(jnp.int32, (tiles * cap, count), 0) == slot
    coarse = (cells // HALF).astype(F32)
    fine = (cells % HALF).astype(F32)
    index = lax.broadcasted_iota(jnp.int32, (PACK - C, count), 0)
    places = jnp.where(index == 0, coarse, jnp.where(index == 1, fine, 0.0)).astype(BF16)
    payload = jnp.concatenate([rows_ref[...], places], axis=0)
    out = lax.dot_general(
        payload, chosen.astype(BF16), NT, preferred_element_type=F32
    ).astype(BF16)
    if cap % HALF == 0:
        for t in range(tiles):
            held[t] = out[:, t * cap : (t + 1) * cap]
    else:
        held[...] = jnp.swapaxes(out.reshape(PACK, tiles, cap), 0, 1)
    size = tiles // len(out_refs)
    for n, out_ref in enumerate(out_refs):
        out_ref[...] = held[pl.ds((ids_ref[0] // size ^ n) * size, size)]


def bucket(ids, exhaust, owner, cells, tiles):
    count = exhaust.shape[0]
    cap = 2 * count // tiles
    full = pl.BlockSpec(memory_space=pltpu.VMEM)
    return pl.pallas_call(
        bucket_kernel,
        in_specs=[pl.BlockSpec(memory_space=pltpu.SMEM)] + [full] * 3,
        out_specs=[full],
        out_shape=[jax.ShapeDtypeStruct((tiles, PACK, cap), BF16)],
        scratch_shapes=[pltpu.VMEM((tiles, PACK, cap), BF16)],
        compiler_params=params(),
        cost_estimate=cost(1000, 1000),
    )(ids, exhaust.T, owner.reshape(1, count), cells.reshape(1, count))


def source_kernel(tiles, rows, ids_ref, *refs):
    got_refs, out_ref = refs[:-1], refs[-1]
    places = out_ref.shape[0]
    groups = places // (QUAD * rows)
    got = jnp.concatenate([ref[ref.shape[0] - PACK :] for ref in got_refs], axis=1)
    slots = got.shape[1]
    cells = (got[C : C + 1].astype(F32) * HALF + got[C + 1 : C + 2].astype(F32)).astype(jnp.int32)
    x, row, level = cells % SEG, cells // SEG % rows, cells // (SEG * rows)
    group = turned_index(ids_ref, tiles, level // QUAD, groups)
    place = (group * QUAD + x // 2) * rows + row
    within = level % QUAD * 2 + x % 2
    lane = lax.broadcasted_iota(jnp.int32, (SL, slots), 0) // C
    spread = jnp.where(lane == within, jnp.concatenate([got[:C]] * SEG, axis=0).astype(F32), 0.0)
    index = lax.broadcasted_iota(jnp.int32, (places, slots), 0)
    chosen = (index == place).astype(BF16)
    out_ref[...] = lax.dot_general(chosen, spread.astype(BF16), NT, preferred_element_type=F32)


def make_source(ids, got, places, rows, tiles):
    full = pl.BlockSpec(memory_space=pltpu.VMEM)
    return pl.pallas_call(
        functools.partial(source_kernel, tiles, rows),
        in_specs=[pl.BlockSpec(memory_space=pltpu.SMEM)] + [full] * len(got),
        out_specs=full,
        out_shape=jax.ShapeDtypeStruct((places, SL), F32),
        compiler_params=params(),
        cost_estimate=cost(1000, 1000),
    )(ids, *got)


def prepare_kernel(ids_ref, depth_ref, point_ref, rows_ref, owner_ref, cells_ref, *rest):
    across_ref, close_ref, far_ref, held = rest
    bucket_kernel(ids_ref, rows_ref, owner_ref, cells_ref, close_ref, far_ref, held)
    across_kernel(depth_ref, point_ref, across_ref)


def prepare(ids, depth_kernel, point_weight, exhaust, owner, cells, tiles):
    count = exhaust.shape[0]
    cap = 2 * count // tiles
    full = pl.BlockSpec(memory_space=pltpu.VMEM)
    block = jax.ShapeDtypeStruct((tiles // 2, PACK, cap), BF16)
    return pl.pallas_call(
        prepare_kernel,
        in_specs=[pl.BlockSpec(memory_space=pltpu.SMEM)] + [full] * 5,
        out_specs=[full] * 3,
        out_shape=[jax.ShapeDtypeStruct(((KH + 1 + 2 * PAD) * 3 * HALF, SL), BF16), block, block],
        scratch_shapes=[pltpu.VMEM((tiles, PACK, cap), BF16)],
        compiler_params=params(),
        cost_estimate=cost(1000, 1000),
    )(
        ids,
        depth_kernel,
        point_weight,
        exhaust.T,
        owner.reshape(1, count),
        cells.reshape(1, count),
    )


def chunks(first, last, size):
    return [(n, min(n + size, last)) for n in range(first, last, size)]


def layer_step(held, base, first, last, block, weight, bias):
    taps = [held[(first - base + k) * block : (last - base + k) * block] for k in range(TAPS)]
    total = jnp.dot(jnp.concatenate(taps, axis=1), weight, preferred_element_type=F32)
    rows = block // QUAD
    start = (first - base + 1) * block
    for n in range(0, (last - first) * block, rows):
        center = held[start + n : start + n + rows].astype(F32)
        yield n, center + gelu(total[n : n + rows] + bias)


def layer_store(out, at, values):
    for n, value in values:
        out[at + n : at + n + value.shape[0]] = value.astype(BF16)


def tile_matrix(height, across):
    size = 2 * height * across
    row = lax.broadcasted_iota(jnp.int32, (size, size), 0)
    column = lax.broadcasted_iota(jnp.int32, (size, size), 1)
    tile = row // height % 4
    segment = row // (4 * height) * 2 + tile // 2
    wanted = (tile % 2 * height + row % height) * across + segment
    return (column == wanted).astype(BF16)


def put_groups(out_ref, values, source_ref, first, height, block, place_of):
    rows = block // QUAD
    turn = tile_matrix(height, rows // height)
    parts, halves = [], [[], []]
    for n, value in values:
        value = value + source_ref[first * block + n : first * block + n + rows]
        parts.append([value[:, :HALF], value[:, HALF:]])
        if len(parts) == QUAD:
            for h in range(2):
                for t in range(2):
                    pair = swap_halves(parts[2 * h][t], parts[2 * h + 1][t])
                    halves[h] += [one.astype(BF16) for one in pair]
            parts = []
    stacked = jnp.concatenate([jnp.concatenate(half, axis=1) for half in halves], axis=0)
    turned = jnp.dot(turn, stacked, preferred_element_type=F32).astype(BF16)
    for n in range(len(halves[0]) // QUAD):
        at = place_of(n) * QUAD
        for z in range(QUAD):
            lane = (n * QUAD + z) * HALF
            out_ref[at + z] = turned[:, lane : lane + HALF].reshape(out_ref.shape[1:])


def lane_biases(bias_ref):
    rows = [bias_row(bias_ref[n : n + 1]) for n in range(2)]
    return [jnp.concatenate([row, row], axis=1) for row in rows]


def place_pieces(tiles, ids_ref, piece_refs, held, first, block):
    for d, piece_ref in enumerate(piece_refs):
        at = turned_index(ids_ref, tiles, ids_ref[0] % tiles ^ d, tiles) + first
        held[pl.ds(pl.multiple_of(at * block, block), block)] = piece_ref[:block]


def near_kernel(tiles, height, ids_ref, *refs):
    piece_refs = refs[:tiles]
    source_ref, weight_ref, bias_ref, out_ref, kept_ref, later_ref, held, step = refs[tiles:]
    groups = out_ref.shape[0] // QUAD + 2
    block = kept_ref.shape[0] // 2
    bias = lane_biases(bias_ref)
    held[:block] = jnp.zeros((block, SL), BF16)
    step[:block] = jnp.zeros((block, SL), BF16)
    place_pieces(tiles, ids_ref, piece_refs, held, 1, block)
    kept_ref[...] = held[(groups - 1) * block : (groups + 1) * block]
    for first, last in chunks(0, groups - 1, 2):
        values = layer_step(held, 0, first, last, block, weight_ref[0], bias[0])
        layer_store(step, (first + 1) * block, values)
    later_ref[...] = step[(groups - 2) * block : groups * block]
    for first, last in chunks(0, groups - 2, 2):
        values = layer_step(step, 0, first, last, block, weight_ref[1], bias[1])
        place_of = lambda n: turned_index(ids_ref, tiles, first + n, groups - 2)
        put_groups(out_ref, values, source_ref, first, height, block, place_of)


def far_kernel(tiles, height, ids_ref, *refs):
    piece_refs = refs[:tiles]
    early_ref, kept_ref, later_ref, source_ref, weight_ref, bias_ref = refs[tiles : tiles + 6]
    out_ref, held, step, result, sems = refs[tiles + 6 :]
    groups = out_ref.shape[0] // QUAD
    half = groups // 2
    block = kept_ref.shape[0] // 2
    early = early_ref.shape[0]
    at = turned_index(ids_ref, tiles, 0, groups * QUAD // early) * early
    copies = [pltpu.make_async_copy(early_ref, out_ref.at[pl.ds(at, early)], sems.at[groups])]
    copies[0].start()
    bias = lane_biases(bias_ref)
    held[: 2 * block] = kept_ref[...]
    held[(half + 2) * block :] = jnp.zeros((block, SL), BF16)
    step[: 2 * block] = later_ref[...]
    step[(half + 3) * block :] = jnp.zeros((block, SL), BF16)
    place_pieces(tiles, ids_ref, piece_refs, held, 2, block)
    for first, last in chunks(half - 1, groups, 3):
        values = layer_step(held, half - 1, first, last, block, weight_ref[0], bias[0])
        layer_store(step, (first - half + 3) * block, values)
    for first, last in chunks(half - 2, groups, 2):
        values = layer_step(step, half - 2, first, last, block, weight_ref[1], bias[1])
        place_of = lambda n: turned_index(ids_ref, tiles, first + n, groups)
        put_groups(result, values, source_ref, first, height, block, place_of)
        for n in range(last - first):
            span = pl.ds(place_of(n) * QUAD, QUAD)
            copies.append(
                pltpu.make_async_copy(result.at[span], out_ref.at[span], sems.at[first + n])
            )
            copies[-1].start()
    for copy in copies:
        copy.wait()


def whole_kernel(height, ids_ref, piece_ref, source_ref, weight_ref, bias_ref, out_ref, held, step):
    levels = out_ref.shape[0]
    groups = levels // QUAD
    rows = piece_ref.shape[0] // levels
    block = QUAD * rows
    bias = lane_biases(bias_ref)
    for buffer in (held, step):
        buffer[:block] = jnp.zeros((block, SL), BF16)
        buffer[(groups + 1) * block :] = jnp.zeros((block, SL), BF16)
    for group in range(groups):
        for h in range(2):
            values = []
            for z in range(group * QUAD, (group + 1) * QUAD):
                tile = piece_ref[z * rows : (z + 1) * rows, h * HALF : (h + 1) * HALF]
                values.append(tile.astype(F32))
            for n, lanes in enumerate(level_lanes(values)):
                at = (group + 1) * block + (2 * h + n) * rows
                held[at : at + rows] = lanes.astype(BF16)
    layer_store(step, block, layer_step(held, 0, 0, groups, block, weight_ref[0], bias[0]))
    values = layer_step(step, 0, 0, groups, block, weight_ref[1], bias[1])
    put_groups(out_ref, values, source_ref, 0, height, block, lambda n: n)


def in_order(out, height):
    levels, blocks, rows, lanes = out.shape
    out = out.reshape(levels, blocks, rows // height, height, lanes)
    return jnp.transpose(out, (0, 3, 1, 2, 4)).reshape(levels, height, -1)


def vertical(ids, close, far, source, weight, bias, levels, height, tiles):
    full = pl.BlockSpec(memory_space=pltpu.VMEM)
    smem = pl.BlockSpec(memory_space=pltpu.SMEM)
    rows = source.shape[0] // levels
    block = QUAD * rows
    groups = levels // QUAD
    lanes = rows // height * SL
    buffer = lambda count: pltpu.VMEM((count * block, SL), BF16)
    array = lambda count: jax.ShapeDtypeStruct((count * block, SL), BF16)
    kind = (lanes // (4 * HALF), 4 * height, HALF)
    result = lambda count: jax.ShapeDtypeStruct((count, *kind), BF16)
    if not far:
        out = pl.pallas_call(
            functools.partial(whole_kernel, height),
            in_specs=[smem] + [full] * 4,
            out_specs=full,
            out_shape=result(levels),
            scratch_shapes=[buffer(groups + 2)] * 2,
            compiler_params=params(),
            cost_estimate=cost(1000, 1000),
        )(ids, *close, source, weight, bias)
        return in_order(out, height)
    half = groups // 2
    early, kept, later = pl.pallas_call(
        functools.partial(near_kernel, tiles, height),
        in_specs=[smem] + [full] * (len(close) + 3),
        out_specs=[full] * 3,
        out_shape=[result(QUAD * (half - 2)), array(2), array(2)],
        scratch_shapes=[buffer(half + 1), buffer(half)],
        compiler_params=params(),
        cost_estimate=cost(1000, 1000),
    )(ids, *close, source, weight, bias)
    out = pl.pallas_call(
        functools.partial(far_kernel, tiles, height),
        in_specs=[smem] + [full] * (len(far) + 6),
        out_specs=pl.BlockSpec(memory_space=pl.ANY),
        out_shape=result(levels),
        scratch_shapes=[
            buffer(half + 3),
            buffer(half + 4),
            pltpu.VMEM((levels, *kind), BF16),
            pltpu.SemaphoreType.DMA((groups + 1,)),
        ],
        compiler_params=params(),
        cost_estimate=cost(1000, 1000),
    )(ids, *far, early, kept, later, source, weight, bias)
    return in_order(out, height)


def exchange(block, distance):
    count = lax.axis_size("cols")
    return lax.ppermute(block, "cols", [(i, i ^ distance) for i in range(count)])


def body(
    field, depth_kernel, point_weight, point_bias, vert_weight, vert_bias, exhaust, owner, cells
):
    columns, bands = lax.axis_size("cols"), lax.axis_size("rows")
    forward = [(i, i + 1) for i in range(bands - 1)]
    backward = [(target, source) for source, target in forward]
    levels, height, lanes = field.shape
    segments = lanes // SL
    per = segments // columns
    ids = jnp.stack([lax.axis_index("cols"), lax.axis_index("rows")]).astype(jnp.int32)
    bias = point_bias.reshape(1, C)
    if per % 16 == 0 and columns % 2 == 0 and bands % 2 == 0 and levels == QUAD and 256 % (levels * height) == 0:
        tiles = columns // 2
        (cross,) = to_segments(ids, field, True)
        ids_after, _ = lax.optimization_barrier((ids, cross))
        own, pair = to_segments(ids_after, field, False)
        inside = [(i, i ^ 1) for i in range(bands)]
        beyond = [(i, i + 1 if i % 2 else i - 1) for i in range(1, bands - 1)]
        cross = lax.ppermute(cross, "rows", beyond)
        pair = lax.ppermute(pair, "rows", inside)
        across, close_rows, far_rows = prepare(
            ids, depth_kernel, point_weight, exhaust, owner, cells, columns
        )
        relayed = exchange(far_rows, tiles)
        early = early_horizontal(ids, own, pair, across)
        pieces = finish_horizontal(
            ids, own, cross, early, across, bias, (close_rows, relayed), columns
        )
        pieces = [exchange(block, slot) if slot else block for slot, block in enumerate(pieces)]
        close, far = pieces[:tiles], pieces[tiles:]
        got = close
    else:
        tiles, far = 0, []
        (sent,) = bucket(ids, exhaust, owner, cells, columns)
        got = lax.all_to_all(sent, "cols", split_axis=0, concat_axis=0, tiled=True)
        got = [jnp.transpose(got, (1, 0, 2)).reshape(PACK, -1)]
        own = jnp.transpose(field.reshape(levels, height, segments, SL), (1, 0, 2, 3))
        low = lax.ppermute(own[height - 3 :], "rows", forward)
        high = lax.ppermute(own[:3], "rows", backward)
        across = across_weights(depth_kernel, point_weight)
        mixed = horizontal(own, low, high, across, bias, columns)
        mixed = mixed.reshape(columns, levels, -1, SL)
        taken = lax.all_to_all(mixed, "cols", split_axis=0, concat_axis=0, tiled=True)
        close = [taken.reshape(-1, SL)]
    depth = columns * levels
    source = make_source(ids, got, depth * height * per, height * per, tiles)
    up = up_weights(ids, vert_weight, tiles)
    return vertical(ids, close, far, source, up, vert_bias, depth, height, tiles)


def solution(mesh):
    placed = (
        P("cols", "rows", None),
        P(),
        P(),
        P(),
        P(),
        P(),
        P(("rows", "cols"), None),
        P(("rows", "cols"), None),
        P(("rows", "cols")),
    )
    return jax.shard_map(
        body, mesh=mesh, in_specs=placed, out_specs=P(None, "rows", "cols"), check_vma=False
    )
```
